32 devices in a mesh: dp: 4 (over z), ctx: 4 (over x, core), tp: 2 (over y).
Axes of the slice: x: 2, y: 2, z: 4, core: 2. Of those that a mesh axis runs over, the one named last changes fastest.
Arguments:
- inputs: bfloat16 [16, 1024, 2048], P('dp', 'ctx'), may hold values from -6 to 6
- span_order: int32 [16, 8], P('dp'), may hold values from 0 to 7, each once within a row
- first_gain: bfloat16 [2048], P(('dp', 'ctx')), may hold values from 0.099609375 to 1.8984375
- query_proj: bfloat16 [2048, 2048], P(('dp', 'ctx'), 'tp'), may hold values from -0.125 to 0.125
- key_matrix: bfloat16 [2048, 1024], P(('dp', 'ctx'), 'tp'), may hold values from -0.125 to 0.125
- value_matrix: bfloat16 [2048, 1024], P(('dp', 'ctx'), 'tp'), may hold values from -0.125 to 0.125
- query_norm: bfloat16 [128], P(('dp', 'ctx')), may hold values from 0.5 to 2
- key_norm: bfloat16 [128], P(('dp', 'ctx')), may hold values from 0.5 to 2
- output_proj: bfloat16 [2048, 2048], P('tp', ('dp', 'ctx')), may hold values from -1 to 1
- second_gain: bfloat16 [2048], P(('dp', 'ctx')), may hold values from 0.099609375 to 1.8984375
- gate_proj: bfloat16 [2048, 6144], P(('dp', 'ctx'), 'tp'), may hold values from -0.125 to 0.125
- up_proj: bfloat16 [2048, 6144], P(('dp', 'ctx'), 'tp'), may hold values from -0.125 to 0.125
- down_proj: bfloat16 [6144, 2048], P('tp', ('dp', 'ctx')), may hold values from -0.078125 to 0.078125
- cotangent: bfloat16 [16, 1024, 2048], P('dp', 'ctx'), may hold values from -6 to 6
Outputs:
- outputs: bfloat16 [16, 1024, 2048], P('dp', 'ctx')
- input_grad: bfloat16 [16, 1024, 2048], P('dp', 'ctx')
- grad_first: float32 [2048], P(('dp', 'ctx'))
- grad_query: float32 [2048, 2048], P(('dp', 'ctx'), 'tp')
- grad_key: float32 [2048, 1024], P(('dp', 'ctx'), 'tp')
- grad_value: float32 [2048, 1024], P(('dp', 'ctx'), 'tp')
- grad_querynorm: float32 [128], P(('dp', 'ctx'))
- grad_keynorm: float32 [128], P(('dp', 'ctx'))
- grad_output: float32 [2048, 2048], P('tp', ('dp', 'ctx'))
- grad_second: float32 [2048], P(('dp', 'ctx'))
- grad_gate: float32 [2048, 6144], P(('dp', 'ctx'), 'tp')
- grad_upproj: float32 [2048, 6144], P(('dp', 'ctx'), 'tp')
- grad_down: float32 [6144, 2048], P('tp', ('dp', 'ctx'))
The draws below stay inside these ranges and needn't reach their ends.
Inputs may be any that keep to these rules, and one draw needn't show every extreme that they name: Each row of span_order is a permutation of the 8 spans of a sequence, each of 128 tokens.
All inputs are finite; a program needn't handle non-finite values.
Results may differ from the reference program's by a relative error of at most 0.04.
Values may be sent and summed in bfloat16 or wider, within the bound.
No kernel may reach another device: no remote copies, remote signals or barrier semaphores. Data moves between devices by JAX's collectives and lax.ppermute only.
A program may use at most 320 MiB of HBM per device.

```python
import math
import jax
import jax.numpy as jnp
from jax import lax

MODEL_DIM = 2048
QUERY_HEADS = 16
KEY_HEADS = 8
HEAD_DIM = 128
FF = 6144
SEQUENCE_TOKENS = 1024
SEQS = 16
SPAN = 128
N_CTX = 4


def levels(rng, extent, pieces, smallest, largest):
    def one(axis_at, parts):
        heights = jax.random.uniform(jax.random.fold_in(jax.random.fold_in(rng, 6), axis_at), (parts,), jnp.float32, smallest / len(pieces), largest / len(pieces))
        return jnp.repeat(jnp.exp(heights), extent[axis_at] // parts).reshape((-1,) + (1,) * (len(extent) - axis_at - 1))

    level = one(*pieces[0])
    for cut in pieces[1:]:
        level = level * one(*cut)
    return level


def bell_draw(own_key, extent, scale, limit, shards=(), held_as=jnp.bfloat16):
    array = jax.random.normal(own_key, extent, jnp.float32) * scale
    if len(shards) > 0:
        array = levels(own_key, extent, shards, -0.22, 0.18) * array
    return jnp.clip(array, min=-limit, max=limit).astype(held_as)


def setup_inputs(seed: int = 0) -> dict:
    splits = jax.random.split(jax.random.key(seed), 15)
    inputs = bell_draw(splits[0], (SEQS, SEQUENCE_TOKENS, MODEL_DIM), 1.0, 6.0, ((0, 4), (1, 4)))
    span_order = jax.vmap(lambda own: jax.random.permutation(own, 2 * N_CTX))(jax.random.split(splits[1], SEQS)).reshape((SEQS, 2 * N_CTX)).astype(jnp.int32)
    first_gain = jnp.clip(1.0 + 0.18 * jax.random.normal(splits[2], (MODEL_DIM,), jnp.float32), 0.099609375, 1.8984375).astype(jnp.bfloat16)
    query_proj = bell_draw(splits[3], (MODEL_DIM, QUERY_HEADS * HEAD_DIM), MODEL_DIM ** -0.5, 0.125, ((0, 16), (1, 2)))
    key_matrix = bell_draw(splits[4], (MODEL_DIM, KEY_HEADS * HEAD_DIM), MODEL_DIM ** -0.5, 0.125, ((0, 16), (1, 2)))
    value_matrix = bell_draw(splits[5], (MODEL_DIM, KEY_HEADS * HEAD_DIM), MODEL_DIM ** -0.5, 0.125, ((0, 16), (1, 2)))
    query_norm = jnp.clip(jnp.exp(math.log(2.0) - 1.3862944 * jax.random.uniform(splits[6], (HEAD_DIM,), jnp.float32) ** levels(splits[6], (HEAD_DIM,), ((0, 16),), -0.2, 0.2)), 0.5, 2.0).astype(jnp.bfloat16)
    key_norm = jnp.clip(jnp.exp(math.log(2.0) - 1.3862944 * jax.random.uniform(splits[7], (HEAD_DIM,), jnp.float32) ** levels(splits[7], (HEAD_DIM,), ((0, 16),), -0.2, 0.2)), 0.5, 2.0).astype(jnp.bfloat16)
    output_proj = bell_draw(splits[8], (QUERY_HEADS * HEAD_DIM, MODEL_DIM), (QUERY_HEADS * HEAD_DIM // 64) ** -0.5, 1.0, ((0, 2), (1, 16)))
    second_gain = jnp.clip(1.0 + 0.18 * jax.random.normal(splits[9], (MODEL_DIM,), jnp.float32), 0.099609375, 1.8984375).astype(jnp.bfloat16)
    gate_proj = bell_draw(splits[10], (MODEL_DIM, FF), MODEL_DIM ** -0.5, 0.125, ((0, 16), (1, 2)))
    up_proj = bell_draw(splits[11], (MODEL_DIM, FF), MODEL_DIM ** -0.5, 0.125, ((0, 16), (1, 2)))
    down_proj = bell_draw(splits[12], (FF, MODEL_DIM), FF ** -0.5, 0.078125, ((0, 2), (1, 16)))
    cotangent = bell_draw(splits[13], (SEQS, SEQUENCE_TOKENS, MODEL_DIM), 1.0, 6.0, ((0, 4), (1, 4)))
    return dict(inputs=inputs, span_order=span_order, first_gain=first_gain, query_proj=query_proj, key_matrix=key_matrix, value_matrix=value_matrix, query_norm=query_norm, key_norm=key_norm, output_proj=output_proj, second_gain=second_gain, gate_proj=gate_proj, up_proj=up_proj, down_proj=down_proj, cotangent=cotangent)


EPSILON = 1e-06
ROPE_BASE = 1000000.0

@jax.custom_vjp
def reduced_precision(v):
    return lax.optimization_barrier(v.astype(jnp.bfloat16)).astype(jnp.float32)

@jax.custom_vjp
def reduced_precision_back(v):
    return v

def low_keep(v):
    return (reduced_precision(v), None)

def low_pass(kept, grad):
    return (grad,)

def back_keep(v):
    return (v, None)

def back_low(kept, grad):
    return (reduced_precision(grad),)
reduced_precision.defvjp(low_keep, low_pass)
reduced_precision_back.defvjp(back_keep, back_low)

def matrix_product(left, right):
    return jnp.dot(left, right, precision=lax.Precision.HIGHEST, preferred_element_type=jnp.float32)

def rms_norm(values, gain):
    return values * lax.rsqrt(lax.optimization_barrier(jnp.mean(values * values, axis=-1, keepdims=True)) + EPSILON) * gain

def rotary(values, positions):
    half_dim = HEAD_DIM // 2
    frequency = ROPE_BASE ** (-(jnp.arange(half_dim, dtype=jnp.float32) * (2.0 / HEAD_DIM)))
    angles = positions.astype(jnp.float32)[:, None] * frequency[None, :]
    cosine_table = jnp.cos(angles)[:, None, :]
    sine_table = jnp.sin(angles)[:, None, :]
    lower_half = values[..., :half_dim]
    upper_half = values[..., half_dim:]
    return jnp.concatenate([lower_half * cosine_table - upper_half * sine_table, upper_half * cosine_table + lower_half * sine_table], axis=-1)

def attend_one(operands):
    query_rows, key_token_rows, value_token_rows, positions = operands
    scores = jnp.einsum('qkgd,pkd->kgqp', query_rows, key_token_rows, precision=lax.Precision.HIGHEST) * HEAD_DIM ** (-0.5)
    scores = reduced_precision_back(scores)
    allowed = positions[:, None] >= positions[None, :]
    scores = jnp.where(allowed[None, None], scores, -1e+30)
    peak_score = lax.optimization_barrier(jnp.max(scores, axis=-1, keepdims=True))
    exponent = jnp.exp(scores - peak_score)
    probability = reduced_precision(exponent / lax.optimization_barrier(jnp.sum(exponent, axis=-1, keepdims=True)))
    return jnp.einsum('kgqp,pkd->qkgd', probability, value_token_rows, precision=lax.Precision.HIGHEST)

def decoder_layer(params, inputs, positions):
    first_gain, query_proj, key_matrix, value_matrix, query_norm, key_norm, output_proj, second_gain, gate_proj, up_proj, down_proj = params
    head_groups = inputs.shape[0]
    token_rows = inputs.reshape(-1, MODEL_DIM)
    normalized = reduced_precision(rms_norm(token_rows, first_gain))
    query_rows = reduced_precision_back(matrix_product(normalized, query_proj)).reshape(head_groups, SEQUENCE_TOKENS, QUERY_HEADS, HEAD_DIM)
    key_token_rows = reduced_precision_back(matrix_product(normalized, key_matrix)).reshape(head_groups, SEQUENCE_TOKENS, KEY_HEADS, HEAD_DIM)
    value_token_rows = reduced_precision(reduced_precision_back(matrix_product(normalized, value_matrix))).reshape(head_groups, SEQUENCE_TOKENS, KEY_HEADS, HEAD_DIM)
    query_rows = reduced_precision(jax.vmap(rotary)(rms_norm(query_rows, query_norm), positions))
    key_token_rows = reduced_precision(jax.vmap(rotary)(rms_norm(key_token_rows, key_norm), positions))
    query_rows = query_rows.reshape(head_groups, SEQUENCE_TOKENS, KEY_HEADS, QUERY_HEADS // KEY_HEADS, HEAD_DIM)
    attended = lax.map(jax.checkpoint(attend_one), (query_rows, key_token_rows, value_token_rows, positions))
    attended = reduced_precision(reduced_precision_back(attended.reshape(-1, QUERY_HEADS * HEAD_DIM)))
    middle = token_rows + reduced_precision_back(matrix_product(attended, output_proj))
    normed_two = reduced_precision(rms_norm(middle, second_gain))
    gate_act = reduced_precision_back(matrix_product(normed_two, gate_proj))
    upward = reduced_precision_back(matrix_product(normed_two, up_proj))
    hidden = reduced_precision(gate_act * jax.nn.sigmoid(gate_act) * upward)
    return (middle + matrix_product(hidden, down_proj)).reshape(inputs.shape)

def reference(inputs, span_order, first_gain, query_proj, key_matrix, value_matrix, query_norm, key_norm, output_proj, second_gain, gate_proj, up_proj, down_proj, cotangent):
    positions = (span_order[:, :, None] * SPAN + jnp.arange(SPAN, dtype=jnp.int32)[None, None, :]).reshape(SEQS, SEQUENCE_TOKENS).astype(jnp.int32)
    params = tuple((weight.astype(jnp.float32) for weight in (first_gain, query_proj, key_matrix, value_matrix, query_norm, key_norm, output_proj, second_gain, gate_proj, up_proj, down_proj)))
    per_group = math.gcd(SEQS, max(1, 4096 // SEQUENCE_TOKENS))
    group_count = SEQS // per_group
    stacked_in = inputs.astype(jnp.float32).reshape(group_count, per_group, SEQUENCE_TOKENS, MODEL_DIM)
    stacked_pos = positions.reshape(group_count, per_group, SEQUENCE_TOKENS)
    stacked_cot = cotangent.astype(jnp.float32).reshape(group_count, per_group, SEQUENCE_TOKENS, MODEL_DIM)

    def one_group(totals, operands):
        group_in, group_pos, group_cot = operands
        produced, pullback = jax.vjp(lambda weights, sample: decoder_layer(weights, sample, group_pos), params, group_in)
        weight_grads, sample_grad = pullback(group_cot)
        totals = jax.tree.map(lambda summed, addend: summed + addend, totals, weight_grads)
        return (totals, (produced.astype(jnp.bfloat16), sample_grad.astype(jnp.bfloat16)))
    initial = tuple((jnp.zeros(weight.shape, jnp.float32) for weight in params))
    totals, (produced, sample_grad) = lax.scan(one_group, initial, (stacked_in, stacked_pos, stacked_cot))
    outputs = produced.reshape(SEQS, SEQUENCE_TOKENS, MODEL_DIM)
    input_grad = sample_grad.reshape(SEQS, SEQUENCE_TOKENS, MODEL_DIM)
    return (outputs, input_grad, totals[0], totals[1], totals[2], totals[3], totals[4], totals[5], totals[6], totals[7], totals[8], totals[9], totals[10])
```

```python
import functools

import jax
import jax.numpy as jnp
from jax import lax
from jax.experimental import pallas as pl
from jax.experimental.pallas import tpu as pltpu
from jax.sharding import PartitionSpec as P

HEAD_DIM = 128
GROUP = 2 * HEAD_DIM
BLOCK = 128
EPSILON = 1e-06
ROPE_BASE = 1000000.0
MASKED = -1e30
VMEM_LIMIT = 56 * 1024 * 1024
F32 = jnp.float32
BF16 = jnp.bfloat16

CORE_SWAP = [(0, 1), (1, 0), (2, 3), (3, 2)]
X_SWAP = [(0, 2), (2, 0), (1, 3), (3, 1)]
TP_SWAP = [(0, 1), (1, 0)]


def nn(left, right):
    return lax.dot_general(left, right, (((1,), (0,)), ((), ())), preferred_element_type=F32)


def nt(left, right):
    return lax.dot_general(left, right, (((1,), (1,)), ((), ())), preferred_element_type=F32)


def tn(left, right):
    return lax.dot_general(left, right, (((0,), (0,)), ((), ())), preferred_element_type=F32)


def unit_norm(values):
    inverse = lax.rsqrt(jnp.mean(values * values, axis=-1, keepdims=True) + EPSILON)
    return values * inverse, inverse


def swap_halves(values):
    return pltpu.roll(values, HEAD_DIM // 2, 1)


def call(kernel, grid, ins, outs, scratch=(), scalars=(), alias=None, after=(), name=None, cost=None):
    any_space = pl.BlockSpec(memory_space=pl.ANY)
    specs = [any_space if b is None else pl.BlockSpec(b, m) for _, b, m in ins]
    n_in, n_after, n_scalar = len(ins), len(after), len(scalars)

    def body(*refs):
        keep = refs[: n_scalar + n_in] + refs[n_scalar + n_in + n_after :]
        kernel(*keep)

    return pl.pallas_call(
        body,
        grid_spec=pltpu.PrefetchScalarGridSpec(
            num_scalar_prefetch=n_scalar,
            grid=grid,
            in_specs=specs + [any_space] * n_after,
            out_specs=[pl.BlockSpec(b, m) for _, _, b, m in outs],
            scratch_shapes=list(scratch),
        ),
        out_shape=[jax.ShapeDtypeStruct(s, d) for s, d, _, _ in outs],
        input_output_aliases={n_scalar + i: o for o, i in (alias or {}).items()},
        compiler_params=pltpu.CompilerParams(
            dimension_semantics=("arbitrary",) * len(grid), vmem_limit_bytes=VMEM_LIMIT
        ),
        cost_estimate=None
        if cost is None
        else pl.CostEstimate(flops=cost[0], bytes_accessed=cost[1], transcendentals=0),
        name=name,
    )(*scalars, *[a for a, _, _ in ins], *after)


def project_kernel(x_ref, w_ref, cos_ref, sin_ref, gain_ref, out_ref, raw_ref, *, groups, rows):
    is_query = pl.program_id(0) < groups
    gain = jnp.where(is_query, gain_ref[0:1, :], gain_ref[1:2, :])
    for at in range(0, x_ref.shape[0], rows):
        part = pl.ds(at, rows)
        raw = nn(x_ref[part, :], w_ref[...])
        raw_ref[part, :] = raw
        cosine, sine = cos_ref[part, :], sin_ref[part, :]
        for head in range(2):
            values = raw[:, head * HEAD_DIM : (head + 1) * HEAD_DIM]
            scaled = unit_norm(values)[0] * gain
            turned = scaled * cosine + swap_halves(scaled) * sine
            if head == 1:
                turned = jnp.where(is_query, turned, values)
            out_ref[part, head * HEAD_DIM : (head + 1) * HEAD_DIM] = turned.astype(BF16)


def project(x, weights, cosine, sine, gains, groups):
    tokens, width = x.shape
    whole = lambda j: (0, 0)
    column = lambda j: (0, j)
    columns = 2 * groups * GROUP
    return call(
        functools.partial(project_kernel, groups=groups, rows=min(256, tokens)),
        (2 * groups,),
        [
            (x, (tokens, width), whole),
            (weights, (width, GROUP), column),
            (cosine, (tokens, HEAD_DIM), whole),
            (sine, (tokens, HEAD_DIM), whole),
            (gains, (2, HEAD_DIM), whole),
        ],
        [
            ((tokens, columns), BF16, (tokens, GROUP), column),
            ((tokens, columns), F32, (tokens, GROUP), column),
        ],
        name="project",
        cost=(2 * tokens * width * columns, 2 * width * columns + 6 * tokens * columns),
    )


def span_places(orders_ref, seq, piece, span, shape, dim):
    index = lax.broadcasted_iota(jnp.int32, shape, dim)
    first, second = orders_ref[seq, 2 * piece], orders_ref[seq, 2 * piece + 1]
    return jnp.where(index < span, first * span + index, second * span + index - span)


def stacked_heads(block):
    return jnp.concatenate([block[:, 0:HEAD_DIM], block[:, HEAD_DIM:GROUP]], axis=0)


def masked_exponents(orders_ref, seq, query, pieces, span):
    rows, keys = query.shape[0], pieces[0].shape[0]
    scale = HEAD_DIM**-0.5
    places = span_places(orders_ref, seq, 0, span, (rows // 2, 1), 0)
    places = jnp.concatenate([places, places], axis=0)
    scores = []
    for at, piece in enumerate(pieces):
        key_places = span_places(orders_ref, seq, at, span, (1, keys), 1)
        product = nt(query, piece[:, 0:HEAD_DIM]) * scale
        scores.append(jnp.where(key_places <= places, product, MASKED))
    peak = functools.reduce(jnp.maximum, [jnp.max(s, axis=1, keepdims=True) for s in scores])
    exponents = [jnp.exp(s - peak) for s in scores]
    total = functools.reduce(jnp.add, [jnp.sum(e, axis=1, keepdims=True) for e in exponents])
    return exponents, 1.0 / total


def attend_kernel(orders_ref, q_ref, own_ref, core_ref, x_ref, diag_ref, *rest, first, span):
    out_ref = rest[-1]
    seq = pl.program_id(0) + first
    query = stacked_heads(q_ref[...])
    pieces = [own_ref[...], core_ref[...], x_ref[...], diag_ref[...]]
    exponents, inverse = masked_exponents(orders_ref, seq, query, pieces, span)
    total = functools.reduce(
        jnp.add, [nn(e.astype(BF16), p[:, HEAD_DIM:GROUP]) for e, p in zip(exponents, pieces)]
    )
    result = (total * inverse).astype(BF16)
    local = q_ref.shape[0]
    out_ref[:, 0:HEAD_DIM] = result[0:local]
    out_ref[:, HEAD_DIM:GROUP] = result[local:]


def attend(orders, qkv, others, first, count, local, into, after=()):
    columns = qkv.shape[1] // 2
    groups = columns // GROUP
    block = (local, GROUP)
    at_query = lambda s, g, o: (s + first, g)
    at_own = lambda s, g, o: (s + first, g + groups)
    at_half = lambda s, g, o: (s, g)
    ins = [(qkv, block, at_query), (qkv, block, at_own)] + [(k, block, at_half) for k in others]
    if into is not None:
        ins.append((into, None, None))
    return call(
        functools.partial(attend_kernel, first=first, span=local // 2),
        (count, groups),
        ins,
        [((qkv.shape[0], columns), BF16, block, at_query)],
        scalars=(orders,),
        alias=None if into is None else {0: len(ins) - 1},
        after=after,
        name="attend",
        cost=(32 * count * local * local * columns, 12 * count * local * columns),
    )[0]


def turn_back(grad, raw, cosine, sine, gain):
    turned = grad * cosine - swap_halves(grad) * sine
    unit, inverse = unit_norm(raw)
    grad_normed = turned * gain
    mean = jnp.mean(grad_normed * unit, axis=-1, keepdims=True)
    terms = jnp.sum((turned * unit).reshape(-1, 8, HEAD_DIM), axis=0)
    return (inverse * (grad_normed - unit * mean)).astype(BF16), terms


def clear_at_start(ref, dims):
    start = functools.reduce(jnp.logical_and, [pl.program_id(d) == 0 for d in range(dims)])

    @pl.when(start)
    def _():
        ref[...] = jnp.zeros_like(ref)


def attend_back_kernel(
    orders_ref, q_ref, own_ref, core_ref, x_ref, diag_ref, grad_ref, raw_ref, cos_ref, sin_ref, gain_ref,
    *rest, first, span
):
    q_back_ref, own_out, core_out, x_out, diag_out, gain_out = rest[-6:]
    seq = pl.program_id(0) + first
    scale = HEAD_DIM**-0.5
    query = stacked_heads(q_ref[...])
    grad = stacked_heads(grad_ref[...])
    pieces = [own_ref[...], core_ref[...], x_ref[...], diag_ref[...]]
    exponents, inverse = masked_exponents(orders_ref, seq, query, pieces, span)
    probability = [e * inverse for e in exponents]
    grad_prob = [nt(grad, p[:, HEAD_DIM:GROUP]) for p in pieces]
    delta = functools.reduce(
        jnp.add, [jnp.sum(p * g, axis=1, keepdims=True) for p, g in zip(probability, grad_prob)]
    )
    grad_scores = [(p * (g - delta)).astype(BF16) for p, g in zip(probability, grad_prob)]
    grad_query = functools.reduce(
        jnp.add, [nn(s, p[:, 0:HEAD_DIM]) for s, p in zip(grad_scores, pieces)]
    )
    for out, scores, prob in zip((own_out, core_out, x_out, diag_out), grad_scores, probability):
        out[:, 0:HEAD_DIM] = (tn(scores, query) * scale).astype(BF16)
        out[:, HEAD_DIM:GROUP] = tn(prob.astype(BF16), grad).astype(BF16)

    clear_at_start(gain_out, 2)
    local = q_ref.shape[0]
    for head in range(2):
        columns = pl.ds(head * HEAD_DIM, HEAD_DIM)
        result, terms = turn_back(
            grad_query[head * local : (head + 1) * local] * scale,
            raw_ref[:, columns],
            cos_ref[...],
            sin_ref[...],
            gain_ref[0:1, :],
        )
        q_back_ref[:, columns] = result
        gain_out[...] += terms


def attend_back(orders, qkv, others, grad, raw, cosine, sine, gains, first, count, local, into, after=()):
    columns = qkv.shape[1] // 2
    groups = columns // GROUP
    block = (local, GROUP)
    at_query = lambda s, g, o: (s + first, g)
    at_own = lambda s, g, o: (s + first, g + groups)
    at_half = lambda s, g, o: (s, g)
    at_table = lambda s, g, o: (s + first, 0)
    fixed = lambda s, g, o: (0, 0)
    ins = [(qkv, block, at_query), (qkv, block, at_own)] + [(k, block, at_half) for k in others]
    ins += [(grad, block, at_half), (raw, block, at_query)]
    ins += [(cosine, (local, HEAD_DIM), at_table), (sine, (local, HEAD_DIM), at_table)]
    ins += [(gains, (2, HEAD_DIM), fixed)]
    if into is not None:
        ins.append((into, None, None))
    piece = ((count * local, columns), BF16, block, at_half)
    return call(
        functools.partial(attend_back_kernel, first=first, span=local // 2),
        (count, groups),
        ins,
        [((qkv.shape[0], columns), BF16, block, at_query)]
        + [piece] * 4
        + [((8, HEAD_DIM), F32, (8, HEAD_DIM), fixed)],
        scalars=(orders,),
        alias=None if into is None else {0: len(ins) - 1},
        after=after,
        name="attend_back",
        cost=(80 * count * local * local * columns, 26 * count * local * columns),
    )


def key_back_kernel(mine_ref, core_ref, x_ref, raw_ref, cos_ref, sin_ref, gain_ref, *rest):
    out_ref, gain_out = rest[-2:]
    clear_at_start(gain_out, 2)
    grad = mine_ref[...].astype(F32) + core_ref[...].astype(F32) + x_ref[...].astype(F32)
    result, terms = turn_back(
        grad[:, 0:HEAD_DIM], raw_ref[:, 0:HEAD_DIM], cos_ref[...], sin_ref[...], gain_ref[1:2, :]
    )
    out_ref[:, 0:HEAD_DIM] = result
    out_ref[:, HEAD_DIM:GROUP] = grad[:, HEAD_DIM:GROUP].astype(BF16)
    gain_out[...] += terms


def key_back(mine, core, x, raw, cosine, sine, gains, first, count, local, into, after=()):
    columns = mine.shape[1]
    groups = columns // GROUP
    block = (local, GROUP)
    at_half = lambda s, g: (s, g)
    at_table = lambda s, g: (s + first, 0)
    fixed = lambda s, g: (0, 0)
    ins = [(mine, block, at_half), (core, block, at_half), (x, block, at_half)]
    ins += [(raw, block, lambda s, g: (s + first, g + groups))]
    ins += [(cosine, (local, HEAD_DIM), at_table), (sine, (local, HEAD_DIM), at_table)]
    ins += [(gains, (2, HEAD_DIM), fixed)]
    if into is not None:
        ins.append((into, None, None))
    return call(
        key_back_kernel,
        (count, groups),
        ins,
        [
            ((raw.shape[0], columns), BF16, block, lambda s, g: (s + first, g)),
            ((8, HEAD_DIM), F32, (8, HEAD_DIM), fixed),
        ],
        alias=None if into is None else {0: len(ins) - 1},
        after=after,
        name="key_back",
        cost=(20 * count * local * columns, 12 * count * local * columns),
    )


def feed_kernel(x_ref, c_ref, g_ref, u_ref, d_ref, *rest, rows):
    hidden_ref, gate_ref, up_ref = rest[-3:]
    for at in range(0, x_ref.shape[0], rows):
        part = pl.ds(at, rows)
        gate = nn(x_ref[part, :], g_ref[...])
        upward = nn(x_ref[part, :], u_ref[...])
        grad = nn(c_ref[part, :], d_ref[...])
        sigmoid = jax.nn.sigmoid(gate)
        silu = gate * sigmoid
        hidden_ref[part, :] = (silu * upward).astype(BF16)
        slope = sigmoid + silu * (1.0 - sigmoid)
        gate_ref[part, :] = (grad * upward * slope).astype(BF16)
        up_ref[part, :] = (grad * silu).astype(BF16)


def feed(x, c, weights, units, tile, first, count, into, after=()):
    tokens, width = x.shape
    tiles = units // tile
    whole = lambda j: (0, 0)
    ins = [(x, (tokens, width), whole), (c, (tokens, width), whole)]
    for at in range(3):
        ins.append((weights, (width, tile), lambda j, at=at: (0, at * tiles + first + j)))
    alias = None
    if into is not None:
        alias = {o: len(ins) + o for o in range(3)}
        ins += [(array, None, None) for array in into]
    return call(
        functools.partial(feed_kernel, rows=min(256, tokens)),
        (count,),
        ins,
        [((tokens, units), BF16, (tokens, tile), lambda j: (0, first + j))] * 3,
        alias=alias,
        after=after,
        name="feed",
        cost=(6 * tokens * width * count * tile, 6 * (width + tokens) * count * tile + 4 * tokens * width),
    )


def nt_kernel(*refs, count):
    w_ref, out_ref = refs[count], refs[-1]
    total, at = None, 0
    for ref in refs[:count]:
        depth = ref.shape[1]
        product = nt(ref[...], w_ref[:, at : at + depth])
        total, at = product if total is None else total + product, at + depth
    out_ref[...] = total.astype(out_ref.dtype)


def nt_product(lefts, weights, first_column, row, rows, after=()):
    width = weights.shape[0]
    depth = sum(left.shape[1] for left in lefts)
    tile = min(256, width)
    fixed = lambda j: (row // rows, 0)
    ins = [(left, (rows, left.shape[1]), fixed) for left in lefts]
    ins.append((weights, (tile, depth), lambda j: (j, first_column // depth)))
    return call(
        functools.partial(nt_kernel, count=len(lefts)),
        (width // tile,),
        ins,
        [((rows, width), BF16, (rows, tile), lambda j: (0, j))],
        after=after,
        name="nt_product",
        cost=(2 * rows * width * depth, 2 * (rows + width) * depth + 2 * rows * width),
    )[0]


def nn_kernel(x_ref, w_ref, out_ref):
    out_ref[...] = nn(x_ref[...], w_ref[...]).astype(out_ref.dtype)


def nn_product(left, weights, first_column, columns, row, rows, after=()):
    width = weights.shape[0]
    tile = min(256, columns)
    return call(
        nn_kernel,
        (columns // tile,),
        [
            (left, (rows, width), lambda j: (row // rows, 0)),
            (weights, (width, tile), lambda j: (0, first_column // tile + j)),
        ],
        [((rows, columns), BF16, (rows, tile), lambda j: (0, j))],
        after=after,
        name="nn_product",
        cost=(2 * rows * width * columns, 2 * (rows + columns) * width + 2 * rows * columns),
    )[0]


def turn_kernel(order_ref, in_ref, out_ref):
    out_ref[...] = in_ref[...].T


def turned_blocks(order, left, after=()):
    tokens, width = left.shape
    return call(
        turn_kernel,
        (width // BLOCK,),
        [(left, (tokens, BLOCK), lambda j, o: (0, o[j]))],
        [((width, tokens), BF16, (BLOCK, tokens), lambda j, o: (j, 0))],
        scalars=(order,),
        after=after,
        name="turned_blocks",
        cost=(0, 4 * tokens * width),
    )[0]


def grad_kernel(left_ref, right_ref, *outs):
    right, at = right_ref[...], 0
    for out in outs:
        rows = out.shape[0]
        out[...] = nn(left_ref[at : at + rows, :], right).astype(BF16)
        at += rows


def grad_product(left, right, cuts, first, columns, after=()):
    width, tokens = left.shape
    tile = min(512, columns)
    return call(
        grad_kernel,
        (columns // tile,),
        [
            (left, (width, tokens), lambda j: (0, 0)),
            (right, (tokens, tile), lambda j: (0, first // tile + j)),
        ],
        [((cut, columns), BF16, (cut, tile), lambda j: (0, j)) for cut in cuts],
        after=after,
        name="grad_product",
        cost=(2 * tokens * width * columns, 2 * (width + columns) * tokens + 2 * width * columns),
    )


def join_kernel(x_ref, own_ref, other_ref, gain_ref, *rest):
    middle_ref, normed_ref = rest[-2:]
    middle = x_ref[...].astype(F32) + (own_ref[...].astype(F32) + other_ref[...].astype(F32))
    middle_ref[...] = middle
    normed_ref[...] = (unit_norm(middle)[0] * gain_ref[...]).astype(BF16)


def join(x, own, other, gain, row, into, after=()):
    tokens, width = x.shape
    rows = own.shape[0]
    tile = min(128, rows)
    block = (tile, width)
    at_whole = lambda j: (row // tile + j, 0)
    at_half = lambda j: (j, 0)
    ins = [(x, block, at_whole), (own, block, at_half), (other, block, at_half)]
    ins += [(gain, (1, width), lambda j: (0, 0))]
    alias = None
    if into is not None:
        alias = {o: len(ins) + o for o in range(2)}
        ins += [(array, None, None) for array in into]
    return call(
        join_kernel,
        (rows // tile,),
        ins,
        [((tokens, width), F32, block, at_whole), ((tokens, width), BF16, block, at_whole)],
        alias=alias,
        after=after,
        name="join",
        cost=(10 * rows * width, 12 * rows * width),
    )


def norm_back_kernel(v_ref, base_ref, own_ref, other_ref, gain_ref, *rest, outs):
    out_refs, terms_ref = rest[-outs - 1 : -1], rest[-1]
    clear_at_start(terms_ref, 1)
    own = own_ref[...].astype(F32)
    unit, inverse = unit_norm(v_ref[...].astype(F32))
    grad_normed = (own + other_ref[...].astype(F32)) * gain_ref[...]
    mean = jnp.mean(grad_normed * unit, axis=-1, keepdims=True)
    result = base_ref[...].astype(F32) + inverse * (grad_normed - unit * mean)
    for ref in out_refs:
        ref[...] = result.astype(ref.dtype)
    terms_ref[...] += jnp.sum((own * unit).reshape(-1, 8, own.shape[1]), axis=0)


def norm_back(values, base, own, other, gain, row, types, into, after=()):
    tokens, width = values.shape
    rows = own.shape[0]
    tile = min(128, rows)
    block = (tile, width)
    at_whole = lambda j: (row // tile + j, 0)
    at_half = lambda j: (j, 0)
    fixed = lambda j: (0, 0)
    ins = [(values, block, at_whole), (base, block, at_whole)]
    ins += [(own, block, at_half), (other, block, at_half), (gain, (1, width), fixed)]
    alias = None
    if into is not None:
        alias = {o: len(ins) + o for o in range(len(types))}
        ins += [(array, None, None) for array in into]
    return call(
        functools.partial(norm_back_kernel, outs=len(types)),
        (rows // tile,),
        ins,
        [((tokens, width), kind, block, at_whole) for kind in types]
        + [((8, width), F32, (8, width), fixed)],
        alias=alias,
        after=after,
        name="norm_back",
        cost=(20 * rows * width, 16 * rows * width),
    )


def pair_heads(left, right):
    heads = left.shape[1] // HEAD_DIM
    cut = lambda array, at: array[:, at * HEAD_DIM : (at + 1) * HEAD_DIM]
    return jnp.concatenate([cut(a, at) for at in range(heads) for a in (left, right)], axis=1)


def split_heads(both, which):
    cuts = range(which, both.shape[1] // HEAD_DIM, 2)
    return jnp.concatenate([both[:, at * HEAD_DIM : (at + 1) * HEAD_DIM] for at in cuts], axis=1)


def behind(value, *others):
    return lax.optimization_barrier((value,) + others)[0]


def shards(
    inputs,
    span_order,
    first_gain,
    query_proj,
    key_matrix,
    value_matrix,
    query_norm,
    key_norm,
    output_proj,
    second_gain,
    gate_proj,
    up_proj,
    down_proj,
    cotangent,
):
    seqs, local, width = inputs.shape
    tokens = seqs * local
    span = local // 2
    shard = query_proj.shape[0]
    head_shard = query_norm.shape[0]
    q_cols, kv_cols = query_proj.shape[1], 2 * key_matrix.shape[1]
    groups = q_cols // GROUP
    units = gate_proj.shape[1]
    tile = 256
    tiles = units // tile
    dp_size, tp_size = lax.axis_size("dp"), lax.axis_size("tp")
    ctx = lax.axis_index("ctx")
    x_at, core_at = ctx // 2, ctx % 2
    share = lax.axis_index("dp") * 4 + ctx
    half_rows = tokens // 2
    half_seqs = seqs // 2

    def tp_start(part):
        if tp_size == 2:
            return part, lax.ppermute(part, "tp", TP_SWAP)
        return lax.psum(part, "tp"), jnp.zeros_like(part)

    core_swap = lambda value: lax.ppermute(value, "ctx", CORE_SWAP)
    x_swap = lambda value: lax.ppermute(value, "ctx", X_SWAP)

    heads = jnp.zeros((shard - head_shard,), BF16)
    small = [first_gain, second_gain]
    small += [jnp.concatenate([gain, heads]) for gain in (query_norm, key_norm)]
    small = jnp.pad(jnp.stack(small, axis=1), ((0, 0), (0, BLOCK - len(small))))
    attention_shard = jnp.concatenate(
        [query_proj, pair_heads(key_matrix, value_matrix), output_proj.T, small], axis=1
    )
    feed_shard = jnp.concatenate([gate_proj, up_proj, down_proj.T], axis=1)
    weights = lax.all_gather(attention_shard, ("dp", "ctx"), axis=0, tiled=True)
    feed_shard = behind(feed_shard, weights)
    feed_weights = lax.all_gather(feed_shard, ("dp", "ctx"), axis=0, tiled=True)
    small = weights[:, q_cols * 2 + kv_cols :].astype(F32)
    gain_first = small[:, 0].reshape(1, width)
    gain_second = small[:, 1].reshape(1, width)
    head_gains = small.reshape(-1, shard, BLOCK)[:, 0:head_shard, 2:4]
    head_gains = head_gains.reshape(HEAD_DIM, 2).T

    pairs = span_order.reshape(seqs, 4, 2)
    relative = jnp.stack([ctx, ctx ^ 1, ctx ^ 2, ctx ^ 3])
    orders = jnp.take(pairs, relative, axis=1).reshape(seqs, 8)
    places = (
        orders[:, 0:2, None] * span + jnp.arange(span, dtype=jnp.int32)[None, None, :]
    ).reshape(tokens)
    half_dim = HEAD_DIM // 2
    frequency = ROPE_BASE ** (-(jnp.arange(half_dim, dtype=F32) * (2.0 / HEAD_DIM)))
    angles = places.astype(F32)[:, None] * frequency[None, :]
    cosine, sine = jnp.cos(angles), jnp.sin(angles)
    cosine = jnp.concatenate([cosine, cosine], axis=1)
    sine = jnp.concatenate([-sine, sine], axis=1)

    dps = jnp.arange(dp_size, dtype=jnp.int32)
    other_first = jnp.stack([1 - x_at, x_at])
    cores = jnp.stack([1 - core_at, core_at])
    by_x = cores[:, None, None] + 2 * other_first[None, :, None] + 4 * dps[None, None, :]
    by_x = by_x.reshape(-1).astype(jnp.int32)
    by_dp = cores[:, None, None] + 4 * dps[None, :, None] + 2 * other_first[None, None, :]
    by_dp = by_dp.reshape(-1).astype(jnp.int32)
    cut = width // 4

    def scatter(value):
        return lax.psum_scatter(value, "dp", scatter_dimension=0, tiled=True)

    def add(*values):
        return functools.reduce(jnp.add, [v.astype(F32) for v in values]).astype(BF16)

    input_rows = inputs.reshape(tokens, width)
    cot_rows = cotangent.reshape(tokens, width)
    unit_one = unit_norm(input_rows.astype(F32))[0]
    cot_turned = turned_blocks(by_x, cot_rows)
    feed_one = (unit_one * gain_first).astype(BF16)
    qkv, raw = project(feed_one, weights, cosine, sine, head_gains, groups)

    kv = [qkv[h * half_rows : (h + 1) * half_rows, q_cols:] for h in range(2)]
    across_a = x_swap(kv[0])
    beside_a = core_swap(kv[0])
    one_turned = turned_blocks(by_dp, feed_one, after=(qkv,))
    across_b = x_swap(behind(kv[1], across_a))
    others = [(beside_a, across_a, core_swap(across_a))]
    others += [(core_swap(kv[1]), across_b, core_swap(across_b))]
    attended, joined, started = None, None, []
    for h in range(2):
        attended = attend(orders, qkv, others[h], h * half_seqs, half_seqs, local, attended)
        part = nt_product([attended], weights, q_cols + kv_cols, h * half_rows, half_rows)
        started.append(tp_start(part))
    for h in range(2):
        joined = join(input_rows, *started[h], gain_second, h * half_rows, joined)
    middle, feed_two = joined

    count_a = (tiles + 1) // 2
    run_feed = lambda first, count, into, after: feed(
        feed_two, cot_rows, feed_weights, units, tile, first, count, into, after
    )
    acts = run_feed(0, count_a, None, ())
    columns_a = count_a * tile

    x_cuts = (2 * cut, cut, cut)
    down_a = grad_product(cot_turned, acts[0], x_cuts, 0, columns_a)
    down_a_core = core_swap(down_a[0])
    two_turned = turned_blocks(by_x, feed_two, after=(down_a[0],))
    down_a_x = add(down_a[1], behind(down_a_core, two_turned)[0:cut])
    down_a_from = x_swap(down_a_x)
    acts = run_feed(count_a, tiles - count_a, acts, (down_a_x,))
    hidden, gate_back, up_back = acts

    back = []
    part = nt_product([gate_back, up_back], feed_weights, 0, 0, half_rows)
    back.append(tp_start(part))
    down_b = grad_product(
        cot_turned, hidden, x_cuts, columns_a, units - columns_a, after=(part,)
    )
    down_b_core = core_swap(down_b[0])
    part = nt_product(
        [gate_back, up_back], feed_weights, 0, half_rows, half_rows, after=(down_b[0],)
    )
    back.append(tp_start(behind(part, back[0][1])))
    down_b_x = add(down_b[1], behind(down_b_core, part)[0:cut])
    down_b_from = x_swap(behind(down_b_x, down_a_from))

    gate = grad_product(two_turned, gate_back, x_cuts, 0, units, after=(down_b_x,))
    gate_core = core_swap(gate[0])
    up = grad_product(two_turned, up_back, x_cuts, 0, units, after=(gate[0],))
    up_core = core_swap(up[0])
    gate_x = add(gate[1], behind(gate_core, up[0])[0:cut])
    gate_from = x_swap(behind(gate_x, down_b_from))
    down_a_out = scatter(add(down_a[2], down_a_core[cut:], behind(down_a_from, gate_x)))

    grads, q_back, k_back, pieces = None, None, None, []
    terms = {"second": 0.0, "query": 0.0, "key": 0.0, "first": 0.0}
    latest = gate_x
    for h in range(2):
        row = h * half_rows
        *grads, second = norm_back(
            middle, cot_rows, *back[h], gain_second, row, (F32, BF16), grads, after=(latest,)
        )
        terms["second"] = terms["second"] + jnp.sum(second, axis=0)
        grad_attended = nn_product(grads[1], weights, q_cols + kv_cols, q_cols, row, half_rows)
        q_back, to_own, to_core, to_x, to_diag, query = attend_back(
            orders, qkv, others[h], grad_attended, raw, cosine, sine, head_gains,
            h * half_seqs, half_seqs, local, q_back,
        )
        terms["query"] = terms["query"] + jnp.sum(query, axis=0)
        from_diag = core_swap(to_diag)
        from_core = core_swap(to_core)
        if h == 0:
            up_x = add(up[1], behind(up_core, to_own)[0:cut])
            latest = up_x
        pieces.append((to_own, from_core, add(to_x, from_diag)))
    grad_middle, middle_low = grads

    from_x_a = x_swap(behind(pieces[0][2], gate_from))
    from_x_b = x_swap(behind(pieces[1][2], from_x_a))
    up_from = x_swap(behind(up_x, from_x_b))
    down_b_out = scatter(add(down_b[2], down_b_core[cut:], behind(down_b_from, q_back)))

    z_cuts = (2 * cut, 2 * cut)

    def scatter_first(left, right, after):
        to_core, kept = grad_product(left, right, z_cuts, 0, right.shape[1], after=after)
        from_core = core_swap(to_core)
        return kept, from_core

    query_parts = scatter_first(one_turned, q_back, ())
    low_turned = turned_blocks(by_dp, middle_low, after=(query_parts[0],))
    query_out = scatter(add(query_parts[0], behind(query_parts[1], low_turned)))
    output_parts = scatter_first(low_turned, attended, (query_out,) if False else ())
    out_part = nt_product([hidden], feed_weights, 2 * units, 0, tokens, after=(output_parts[0],))
    out_started = tp_start(behind(out_part, back[1][1]))
    output_out = scatter(add(output_parts[0], behind(output_parts[1], out_part)))

    one = []
    for h in range(2):
        from_x = (from_x_a, from_x_b)[h]
        k_back, key = key_back(
            pieces[h][0], pieces[h][1], from_x, raw, cosine, sine, head_gains,
            h * half_seqs, half_seqs, local, k_back, after=(out_part,),
        )
        terms["key"] = terms["key"] + jnp.sum(key, axis=0)
        part = nt_product([q_back, k_back], weights, 0, h * half_rows, half_rows)
        one.append(tp_start(behind(part, out_started[1])))
    key_parts = scatter_first(one_turned, k_back, ())
    key_out = scatter(add(*key_parts))
    gate_out = scatter(add(gate[2], gate_core[cut:], gate_from))
    up_out = scatter(add(up[2], up_core[cut:], up_from))

    finish = lambda value: add(value[shard:], x_swap(value[0:shard])).astype(F32)
    grad_query, grad_output, grad_kv = finish(query_out), finish(output_out), finish(key_out)

    result = None
    for h in range(2):
        *result, first = norm_back(
            input_rows, grad_middle, *one[h], gain_first, h * half_rows, (BF16,), result
        )
        terms["first"] = terms["first"] + jnp.sum(first, axis=0)

    if tp_size != 2:
        terms["first"], terms["second"] = terms["first"] / tp_size, terms["second"] / tp_size
    totals = jnp.concatenate([terms[name] for name in ("first", "second", "query", "key")])
    totals = lax.psum(totals, ("dp", "ctx", "tp"))
    cut_total = lambda start, size: lax.dynamic_slice(totals, (start + share * size,), (size,))

    outputs = middle + (out_started[0].astype(F32) + out_started[1].astype(F32))
    grad_down = jnp.concatenate([down_a_out, down_b_out], axis=1)
    return (
        outputs.astype(BF16).reshape(inputs.shape),
        result[0].reshape(inputs.shape),
        cut_total(0, shard),
        grad_query,
        split_heads(grad_kv, 0),
        split_heads(grad_kv, 1),
        cut_total(2 * width, head_shard),
        cut_total(2 * width + HEAD_DIM, head_shard),
        grad_output.T,
        cut_total(width, shard),
        gate_out.astype(F32),
        up_out.astype(F32),
        grad_down.astype(F32).T,
    )


def solution(mesh):
    rows = P(("dp", "ctx"))
    columns = P(("dp", "ctx"), "tp")
    turned = P("tp", ("dp", "ctx"))
    tokens = P("dp", "ctx", None)
    in_specs = (
        (tokens, P("dp", None), rows, columns, columns, columns, rows, rows, turned, rows)
        + (columns, columns, turned, tokens)
    )
    out_specs = (
        (tokens, tokens, rows, columns, columns, columns, rows, rows, turned, rows)
        + (columns, columns, turned)
    )
    return jax.shard_map(shards, mesh=mesh, in_specs=in_specs, out_specs=out_specs, check_vma=False)
```

```python
import functools

import jax
import jax.numpy as jnp
from jax import lax
from jax.experimental import pallas as pl
from jax.experimental.pallas import tpu as pltpu
from jax.sharding import PartitionSpec as P

HEAD_DIM = 128
GROUP = 2 * HEAD_DIM
BLOCK = 128
EPSILON = 1e-06
ROPE_BASE = 1000000.0
MASKED = -1e30
VMEM_LIMIT = 56 * 1024 * 1024
F32 = jnp.float32
BF16 = jnp.bfloat16
FLOPS_PER_US = 1e10

CORE_SWAP = [(0, 1), (1, 0), (2, 3), (3, 2)]
X_SWAP = [(0, 2), (2, 0), (1, 3), (3, 1)]
TP_SWAP = [(0, 1), (1, 0)]


def nn(left, right):
    return lax.dot_general(left, right, (((1,), (0,)), ((), ())), preferred_element_type=F32)


def nt(left, right):
    return lax.dot_general(left, right, (((1,), (1,)), ((), ())), preferred_element_type=F32)


def tn(left, right):
    return lax.dot_general(left, right, (((0,), (0,)), ((), ())), preferred_element_type=F32)


def unit_norm(values):
    inverse = lax.rsqrt(jnp.mean(values * values, axis=-1, keepdims=True) + EPSILON)
    return values * inverse, inverse


def swap_halves(values):
    return pltpu.roll(values, HEAD_DIM // 2, 1)


def call(kernel, grid, ins, outs, scratch=(), scalars=(), alias=None, after=(), name=None, cost=1.0):
    any_space = pl.BlockSpec(memory_space=pl.ANY)
    specs = [any_space if b is None else pl.BlockSpec(b, m) for _, b, m in ins]
    n_in, n_after, n_scalar = len(ins), len(after), len(scalars)

    def body(*refs):
        keep = refs[: n_scalar + n_in] + refs[n_scalar + n_in + n_after :]
        kernel(*keep)

    return pl.pallas_call(
        body,
        grid_spec=pltpu.PrefetchScalarGridSpec(
            num_scalar_prefetch=n_scalar,
            grid=grid,
            in_specs=specs + [any_space] * n_after,
            out_specs=[pl.BlockSpec(b, m) for _, _, b, m in outs],
            scratch_shapes=list(scratch),
        ),
        out_shape=[jax.ShapeDtypeStruct(s, d) for s, d, _, _ in outs],
        input_output_aliases={n_scalar + i: o for o, i in (alias or {}).items()},
        compiler_params=pltpu.CompilerParams(
            dimension_semantics=("arbitrary",) * len(grid), vmem_limit_bytes=VMEM_LIMIT
        ),
        cost_estimate=pl.CostEstimate(
            flops=int(cost * FLOPS_PER_US), bytes_accessed=0, transcendentals=0
        ),
        name=name,
    )(*scalars, *[a for a, _, _ in ins], *after)


def pack_first_kernel(q_ref, k_ref, v_ref, o_ref, g_ref, u_ref, d_ref, small_ref, out_ref):
    columns, third = q_ref.shape[1], g_ref.shape[1]
    out_ref[:, 0:columns] = q_ref[...]
    for at in range(columns // GROUP):
        cut = slice(at * HEAD_DIM, (at + 1) * HEAD_DIM)
        start = columns + at * GROUP
        out_ref[:, start : start + HEAD_DIM] = k_ref[:, cut]
        out_ref[:, start + HEAD_DIM : start + GROUP] = v_ref[:, cut]
    out_ref[:, 2 * columns : 3 * columns] = o_ref[...].T
    start = 3 * columns
    out_ref[:, start : start + third] = g_ref[...]
    out_ref[:, start + third : start + 2 * third] = u_ref[...]
    out_ref[:, start + 2 * third : start + 3 * third] = d_ref[...].T
    out_ref[:, start + 3 * third :] = small_ref[...]


def pack_first(q, k, v, o, g, u, d, small, third):
    shard, columns = q.shape
    whole = lambda array: (array, array.shape, lambda j: (0, 0))
    total = 3 * columns + 3 * third + BLOCK
    return call(
        pack_first_kernel,
        (1,),
        [whole(q), whole(k), whole(v), whole(o)]
        + [(g, (shard, third), lambda j: (0, 0)), (u, (shard, third), lambda j: (0, 0))]
        + [(d, (third, shard), lambda j: (0, 0)), whole(small)],
        [((shard, total), BF16, (shard, total), lambda j: (0, 0))],
        name="pack_first",
        cost=3,
    )[0]


def pack_second_kernel(g_ref, u_ref, d_ref, out_ref):
    step = pl.program_id(0)
    part = step // 2

    @pl.when(part == 0)
    def _():
        out_ref[...] = g_ref[...]

    @pl.when(part == 1)
    def _():
        out_ref[...] = u_ref[...]

    @pl.when(part == 2)
    def _():
        out_ref[...] = d_ref[...].T


def pack_second(g, u, d, third, after=()):
    shard = g.shape[0]
    return call(
        pack_second_kernel,
        (6,),
        [(g, (shard, third), lambda j: (0, 1 + j % 2)), (u, (shard, third), lambda j: (0, 1 + j % 2))]
        + [(d, (third, shard), lambda j: (1 + j % 2, 0))],
        [((shard, 6 * third), BF16, (shard, third), lambda j: (0, j))],
        after=after,
        name="pack_second",
        cost=5,
    )[0]


def norm_kernel(x_ref, gain_ref, out_ref):
    out_ref[...] = (unit_norm(x_ref[...].astype(F32))[0] * gain_ref[...]).astype(BF16)


def norm_rows(x, gain, after=()):
    tokens, width = x.shape
    tile = min(256, tokens)
    block = (tile, width)
    return call(
        norm_kernel,
        (tokens // tile,),
        [(x, block, lambda j: (j, 0)), (gain, (1, width), lambda j: (0, 0))],
        [((tokens, width), BF16, block, lambda j: (j, 0))],
        after=after,
        name="norm_rows",
        cost=5,
    )[0]


def project_kernel(x_ref, w_ref, cos_ref, sin_ref, gain_ref, out_ref, raw_ref, *, turned, rows):
    for at in range(0, x_ref.shape[0], rows):
        part = pl.ds(at, rows)
        raw = nn(x_ref[part, :], w_ref[...])
        raw_ref[part, :] = raw
        cosine, sine = cos_ref[part, :], sin_ref[part, :]
        for head in range(2):
            values = raw[:, head * HEAD_DIM : (head + 1) * HEAD_DIM]
            if head < turned:
                scaled = unit_norm(values)[0] * gain_ref[...]
                values = scaled * cosine + swap_halves(scaled) * sine
            out_ref[part, head * HEAD_DIM : (head + 1) * HEAD_DIM] = values.astype(BF16)


def project(x, weights, cosine, sine, gain, groups, first, turned, row, rows, after=()):
    width = x.shape[1]
    some = lambda j: (row // rows, 0)
    column = lambda j: (0, j)
    columns = groups * GROUP
    return call(
        functools.partial(project_kernel, turned=turned, rows=min(256, rows)),
        (groups,),
        [
            (x, (rows, width), some),
            (weights, (width, GROUP), lambda j: (0, first + j)),
            (cosine, (rows, HEAD_DIM), some),
            (sine, (rows, HEAD_DIM), some),
            (gain, (1, HEAD_DIM), lambda j: (0, 0)),
        ],
        [
            ((rows, columns), BF16, (rows, GROUP), column),
            ((rows, columns), F32, (rows, GROUP), column),
        ],
        after=after,
        name="project",
        cost=10,
    )


def span_places(orders_ref, seq, piece, span, shape, dim):
    index = lax.broadcasted_iota(jnp.int32, shape, dim)
    first, second = orders_ref[seq, 2 * piece], orders_ref[seq, 2 * piece + 1]
    return jnp.where(index < span, first * span + index, second * span + index - span)


def stacked_heads(block):
    return jnp.concatenate([block[:, 0:HEAD_DIM], block[:, HEAD_DIM:GROUP]], axis=0)


def masked_exponents(orders_ref, seq, query, pieces, span):
    rows, keys = query.shape[0], pieces[0].shape[0]
    scale = HEAD_DIM**-0.5
    places = span_places(orders_ref, seq, 0, span, (rows // 2, 1), 0)
    places = jnp.concatenate([places, places], axis=0)
    scores = []
    for at, piece in enumerate(pieces):
        key_places = span_places(orders_ref, seq, at, span, (1, keys), 1)
        product = nt(query, piece[:, 0:HEAD_DIM]) * scale
        scores.append(jnp.where(key_places <= places, product, MASKED))
    peak = functools.reduce(jnp.maximum, [jnp.max(s, axis=1, keepdims=True) for s in scores])
    exponents = [jnp.exp(s - peak) for s in scores]
    total = functools.reduce(jnp.add, [jnp.sum(e, axis=1, keepdims=True) for e in exponents])
    return exponents, 1.0 / total


def attend_kernel(orders_ref, q_ref, own_ref, core_ref, x_ref, diag_ref, out_ref, *, first, span):
    seq = pl.program_id(0) + first
    local = q_ref.shape[0]
    for group in range(q_ref.shape[1] // GROUP):
        columns = slice(group * GROUP, (group + 1) * GROUP)
        query = stacked_heads(q_ref[:, columns])
        pieces = [ref[:, columns] for ref in (own_ref, core_ref, x_ref, diag_ref)]
        exponents, inverse = masked_exponents(orders_ref, seq, query, pieces, span)
        total = functools.reduce(
            jnp.add, [nn(e.astype(BF16), p[:, HEAD_DIM:GROUP]) for e, p in zip(exponents, pieces)]
        )
        result = (total * inverse).astype(BF16)
        for head in range(2):
            start = group * GROUP + head * HEAD_DIM
            out_ref[:, start : start + HEAD_DIM] = result[head * local : (head + 1) * local]


def attend(orders, q, kv, others, first, count, local, after=()):
    columns = q.shape[1]
    block = (local, columns)
    at_whole = lambda s, o: (s + first, 0)
    at_half = lambda s, o: (s, 0)
    ins = [(q, block, at_whole), (kv, block, at_half)] + [(k, block, at_half) for k in others]
    return call(
        functools.partial(attend_kernel, first=first, span=local // 2),
        (count,),
        ins,
        [((count * local, columns), BF16, block, at_half)],
        scalars=(orders,),
        after=after,
        name="attend",
        cost=11,
    )[0]


def turn_back(grad, raw, cosine, sine, gain):
    turned = grad * cosine - swap_halves(grad) * sine
    unit, inverse = unit_norm(raw)
    grad_normed = turned * gain
    mean = jnp.mean(grad_normed * unit, axis=-1, keepdims=True)
    terms = jnp.sum((turned * unit).reshape(-1, 8, HEAD_DIM), axis=0)
    return (inverse * (grad_normed - unit * mean)).astype(BF16), terms


def clear_at_start(ref, dims):
    start = functools.reduce(jnp.logical_and, [pl.program_id(d) == 0 for d in range(dims)])

    @pl.when(start)
    def _():
        ref[...] = jnp.zeros_like(ref)


def attend_back_kernel(
    orders_ref, q_ref, own_ref, core_ref, x_ref, diag_ref, grad_ref, raw_ref, cos_ref, sin_ref, gain_ref,
    *rest, first, span
):
    q_back_ref, own_out, x_out, core_out, gain_out = rest[-5:]
    clear_at_start(gain_out, 1)
    seq = pl.program_id(0) + first
    scale = HEAD_DIM**-0.5
    local = q_ref.shape[0]
    for group in range(q_ref.shape[1] // GROUP):
        start = group * GROUP
        both = slice(start, start + GROUP)
        query = stacked_heads(q_ref[:, both])
        grad = stacked_heads(grad_ref[:, both])
        pieces = [ref[:, both] for ref in (own_ref, core_ref, x_ref, diag_ref)]
        exponents, inverse = masked_exponents(orders_ref, seq, query, pieces, span)
        probability = [e * inverse for e in exponents]
        grad_prob = [nt(grad, p[:, HEAD_DIM:GROUP]) for p in pieces]
        delta = functools.reduce(
            jnp.add, [jnp.sum(p * g, axis=1, keepdims=True) for p, g in zip(probability, grad_prob)]
        )
        grad_scores = [(p * (g - delta)).astype(BF16) for p, g in zip(probability, grad_prob)]
        grad_query = functools.reduce(
            jnp.add, [nn(s, p[:, 0:HEAD_DIM]) for s, p in zip(grad_scores, pieces)]
        )
        outs = (own_out, core_out.at[0], x_out, core_out.at[1])
        for out, scores, prob in zip(outs, grad_scores, probability):
            out[:, start : start + HEAD_DIM] = (tn(scores, query) * scale).astype(BF16)
            out[:, start + HEAD_DIM : start + GROUP] = tn(prob.astype(BF16), grad).astype(BF16)
        for head in range(2):
            columns = slice(start + head * HEAD_DIM, start + (head + 1) * HEAD_DIM)
            result, terms = turn_back(
                grad_query[head * local : (head + 1) * local] * scale,
                raw_ref[:, columns],
                cos_ref[...],
                sin_ref[...],
                gain_ref[...],
            )
            q_back_ref[:, columns] = result
            gain_out[...] += terms


def attend_back(orders, q, kv, others, grad, raw, cosine, sine, gain, first, count, local, into, after=()):
    columns = q.shape[1]
    block = (local, columns)
    at_whole = lambda s, o: (s + first, 0)
    at_half = lambda s, o: (s, 0)
    fixed = lambda s, o: (0, 0)
    ins = [(q, block, at_whole), (kv, block, at_half)] + [(k, block, at_half) for k in others]
    ins += [(grad, block, at_half), (raw, block, at_whole)]
    ins += [(cosine, (local, HEAD_DIM), at_whole), (sine, (local, HEAD_DIM), at_whole)]
    ins += [(gain, (1, HEAD_DIM), fixed)]
    if into is not None:
        ins.append((into, None, None))
    piece = ((count * local, columns), BF16, block, at_half)
    return call(
        functools.partial(attend_back_kernel, first=first, span=local // 2),
        (count,),
        ins,
        [(q.shape, BF16, block, at_whole)]
        + [piece] * 2
        + [((2, count * local, columns), BF16, (2, local, columns), lambda s, o: (0, s, 0))]
        + [((8, HEAD_DIM), F32, (8, HEAD_DIM), fixed)],
        scalars=(orders,),
        alias=None if into is None else {0: len(ins) - 1},
        after=after,
        name="attend_back",
        cost=25,
    )


def key_back_kernel(mine_ref, core_ref, x_ref, raw_ref, cos_ref, sin_ref, gain_ref, *rest):
    out_ref, gain_out = rest[-2:]
    clear_at_start(gain_out, 1)
    for group in range(mine_ref.shape[1] // GROUP):
        start = group * GROUP
        both = slice(start, start + GROUP)
        parts = [ref[:, both].astype(F32) for ref in (mine_ref, core_ref.at[0], x_ref)]
        grad = functools.reduce(jnp.add, parts)
        result, terms = turn_back(
            grad[:, 0:HEAD_DIM],
            raw_ref[:, start : start + HEAD_DIM],
            cos_ref[...],
            sin_ref[...],
            gain_ref[...],
        )
        out_ref[:, start : start + HEAD_DIM] = result
        out_ref[:, start + HEAD_DIM : start + GROUP] = grad[:, HEAD_DIM:GROUP].astype(BF16)
        gain_out[...] += terms


def key_back(mine, core, x, raw, cosine, sine, gain, first, count, local, tokens, into, after=()):
    columns = mine.shape[1]
    block = (local, columns)
    at_whole = lambda s: (s + first, 0)
    at_half = lambda s: (s, 0)
    fixed = lambda s: (0, 0)
    ins = [(mine, block, at_half), (core, (1,) + block, lambda s: (0, s, 0)), (x, block, at_half)]
    ins += [(raw, block, at_half)]
    ins += [(cosine, (local, HEAD_DIM), at_whole), (sine, (local, HEAD_DIM), at_whole)]
    ins += [(gain, (1, HEAD_DIM), fixed)]
    if into is not None:
        ins.append((into, None, None))
    return call(
        key_back_kernel,
        (count,),
        ins,
        [
            ((tokens, columns), BF16, block, at_whole),
            ((8, HEAD_DIM), F32, (8, HEAD_DIM), fixed),
        ],
        alias=None if into is None else {0: len(ins) - 1},
        after=after,
        name="key_back",
        cost=5,
    )


def feed_kernel(x_ref, c_ref, g_ref, u_ref, d_ref, *outs, rows, steps):
    step, pieces = pl.program_id(0), len(outs) // 3

    def fill(hidden_ref, gate_ref, up_ref):
        for at in range(0, x_ref.shape[0], rows):
            part = pl.ds(at, rows)
            gate = nn(x_ref[part, :], g_ref[...])
            upward = nn(x_ref[part, :], u_ref[...])
            grad = nn(c_ref[part, :], d_ref[...])
            sigmoid = jax.nn.sigmoid(gate)
            silu = gate * sigmoid
            hidden_ref[part, :] = (silu * upward).astype(BF16)
            slope = sigmoid + silu * (1.0 - sigmoid)
            gate_ref[part, :] = (grad * upward * slope).astype(BF16)
            up_ref[part, :] = (grad * silu).astype(BF16)

    for piece in range(pieces):
        run = functools.partial(fill, *outs[piece::pieces])
        if pieces == 1:
            run()
        else:
            pl.when(step // steps == piece)(run)


def feed(x, c, weights, starts, tile, piece, pieces, after=()):
    tokens, width = x.shape
    steps = piece // tile
    whole = lambda j: (0, 0)
    ins = [(x, (tokens, width), whole), (c, (tokens, width), whole)]
    for start in starts:
        ins.append((weights, (width, tile), lambda j, start=start: (0, start // tile + j)))
    outs = [
        ((tokens, piece), BF16, (tokens, tile), lambda j, at=at: (0, jnp.clip(j - at * steps, 0, steps - 1)))
        for _ in range(3)
        for at in range(pieces)
    ]
    found = call(
        functools.partial(feed_kernel, rows=min(256, tokens), steps=steps),
        (steps * pieces,),
        ins,
        outs,
        after=after,
        name="feed",
        cost=2 + piece * pieces * 0.0165,
    )
    return [found[kind * pieces : (kind + 1) * pieces] for kind in range(3)]


def nt_kernel(*refs, count):
    out_ref = refs[-1]
    total = None
    for left_ref, w_ref in zip(refs[:count], refs[count : 2 * count]):
        product = nt(left_ref[...], w_ref[...])
        total = product if total is None else total + product
    out_ref[...] = total.astype(out_ref.dtype)


def nt_product(terms, row, rows, after=()):
    width = terms[0][1].shape[0]
    tile = min(512, width)
    ins = [(left, (rows, left.shape[1]), lambda j: (row // rows, 0)) for left, _, _ in terms]
    ins += [
        (weights, (tile, left.shape[1]), lambda j, at=at // left.shape[1]: (j, at))
        for left, weights, at in terms
    ]
    return call(
        functools.partial(nt_kernel, count=len(terms)),
        (width // tile,),
        ins,
        [((rows, width), BF16, (rows, tile), lambda j: (0, j))],
        after=after,
        name="nt_product",
        cost=1.5 + rows * sum(left.shape[1] for left, _, _ in terms) * 6.0e-6,
    )[0]


def nn_kernel(x_ref, w_ref, out_ref):
    out_ref[...] = nn(x_ref[...], w_ref[...]).astype(out_ref.dtype)


def nn_product(left, weights, first_column, columns, row, rows, after=()):
    width = weights.shape[0]
    tile = min(512, columns)
    return call(
        nn_kernel,
        (columns // tile,),
        [
            (left, (rows, width), lambda j: (row // rows, 0)),
            (weights, (width, tile), lambda j: (0, first_column // tile + j)),
        ],
        [((rows, columns), BF16, (rows, tile), lambda j: (0, j))],
        after=after,
        name="nn_product",
        cost=6,
    )[0]


def output_join_kernel(
    at_ref, x_ref, mine_ref, other_ref, w_mine_ref, w_same_ref, w_swap_ref, gain_ref, *rest, steps
):
    middle_ref, normed_ref, rows_ref = rest[-3:]
    step = pl.program_id(0)
    tile = x_ref.shape[1]
    is_first, core = at_ref[0] == 0, at_ref[1]
    direct = (step * 2 // steps) == core
    mine, other, w_mine = mine_ref[...], other_ref[...], w_mine_ref[...]
    w_other = jnp.where(direct, w_same_ref[...], w_swap_ref[...])
    total = nt(jnp.where(is_first, mine, other), jnp.where(is_first, w_mine, w_other))
    total += nt(jnp.where(is_first, other, mine), jnp.where(is_first, w_other, w_mine))
    columns = pl.ds(pl.multiple_of(step * tile, tile), tile)
    rows_ref[:, columns] = x_ref[...].astype(F32) + total

    @pl.when(step == steps - 1)
    def _():
        middle = rows_ref[...]
        middle_ref[...] = middle
        normed_ref[...] = (unit_norm(middle)[0] * gain_ref[...]).astype(BF16)


def output_join(at, x, mine, other, weights, block, same, swapped, gain, row, into, after=()):
    tokens, width = x.shape
    rows, columns = mine.shape
    tile = min(512, width // 2)
    steps = width // tile
    fixed = lambda j, a: (0, 0)
    fetched = lambda j, a: (j % (steps // 2), 0)
    ins = [
        (x, (rows, tile), lambda j, a: (row // rows, j)),
        (mine, (rows, columns), fixed),
        (other, (rows, columns), fixed),
        (weights, (tile, columns), lambda j, a: (j, block)),
        (same, (tile, columns), fetched),
        (swapped, (tile, columns), fetched),
        (gain, (1, width), fixed),
    ]
    alias = None
    if into is not None:
        alias = {o: len(ins) + o for o in range(2)}
        ins += [(array, None, None) for array in into]
    out = lambda kind: ((tokens, width), kind, (rows, width), lambda j, a: (row // rows, 0))
    return call(
        functools.partial(output_join_kernel, steps=steps),
        (steps,),
        ins,
        [out(F32), out(BF16)],
        scratch=[pltpu.VMEM((rows, width), F32)],
        scalars=(at,),
        alias=alias,
        after=after,
        name="output_join",
        cost=15,
    )


def turn_kernel(order_ref, *refs):
    ins, outs = refs[:4], refs[4:]
    step = pl.program_id(0)

    def fill(out_ref):
        for at, ref in enumerate(ins):
            out_ref[at * BLOCK : (at + 1) * BLOCK, :] = ref[...].T

    pl.when(step < 2)(lambda: fill(outs[0]))
    pl.when(step >= 2)(lambda: fill(outs[1]))


def turned_blocks(order, left, after=()):
    tokens, width = left.shape
    ins = [(left, (tokens, BLOCK), lambda j, o, at=at: (0, o[4 * j + at])) for at in range(4)]
    out = lambda spot: ((width // 2, tokens), BF16, (4 * BLOCK, tokens), spot)
    return call(
        turn_kernel,
        (width // BLOCK // 4,),
        ins,
        [out(lambda j, o: (jnp.minimum(j, 1), 0)), out(lambda j, o: (jnp.maximum(j - 2, 0), 0))],
        scalars=(order,),
        after=after,
        name="turned_blocks",
        cost=6,
    )


def grad_kernel(*refs, plan, outs):
    step, begin, used = pl.program_id(0), 0, 0
    out_refs = refs[-outs:]

    def fill(left_refs, right_refs):
        for at, out in enumerate(out_refs):
            size, total = out.shape[0], None
            rows = pl.ds(at * size, size)
            for left_ref, pieces in zip(left_refs, right_refs):
                start = 0
                for piece in pieces:
                    tokens = piece.shape[0]
                    product = nn(left_ref[rows, start : start + tokens], piece[...])
                    total = product if total is None else total + product
                    start += tokens
            out[...] = total.astype(BF16)

    for pieces, count in plan:
        part = refs[used : used + 2 + 2 * pieces]
        run = functools.partial(fill, part[:2], (part[2 : 2 + pieces], part[2 + pieces :]))
        if len(plan) == 1:
            run()
        else:
            pl.when((step >= begin) & (step < begin + count))(run)
        begin, used = begin + count, used + 2 + 2 * pieces


def grad_product(parts, tile, cuts, after=()):
    width, tokens = parts[0][0][0].shape
    ins, begin, plan = [], 0, []
    for lefts, rights in parts:
        count = rights[0][0].shape[1] // tile
        ins += [(left, left.shape, lambda j: (0, 0)) for left in lefts]
        spot = lambda j, begin=begin, count=count: (0, jnp.clip(j - begin, 0, count - 1))
        ins += [(piece, (piece.shape[0], tile), spot) for pieces in rights for piece in pieces]
        plan.append((len(rights[0]), count))
        begin += count
    return call(
        functools.partial(grad_kernel, plan=plan, outs=len(cuts)),
        (begin,),
        ins,
        [((cut, begin * tile), BF16, (cut, tile), lambda j: (0, j)) for cut in cuts],
        after=after,
        name="grad_product",
        cost=3.5 + begin * tile * 0.0047,
    )


def join_kernel(x_ref, own_ref, other_ref, gain_ref, *rest):
    middle_ref, normed_ref = rest[-2:]
    middle = x_ref[...].astype(F32) + (own_ref[...].astype(F32) + other_ref[...].astype(F32))
    middle_ref[...] = middle
    normed_ref[...] = (unit_norm(middle)[0] * gain_ref[...]).astype(BF16)


def join(x, own, other, gain, row, into, after=()):
    tokens, width = x.shape
    rows = own.shape[0]
    tile = min(256, rows)
    block = (tile, width)
    at_whole = lambda j: (row // tile + j, 0)
    at_half = lambda j: (j, 0)
    ins = [(x, block, at_whole), (own, block, at_half), (other, block, at_half)]
    ins += [(gain, (1, width), lambda j: (0, 0))]
    alias = None
    if into is not None:
        alias = {o: len(ins) + o for o in range(2)}
        ins += [(array, None, None) for array in into]
    return call(
        join_kernel,
        (rows // tile,),
        ins,
        [((tokens, width), F32, block, at_whole), ((tokens, width), BF16, block, at_whole)],
        alias=alias,
        after=after,
        name="join",
        cost=7.5,
    )


def norm_back_kernel(v_ref, base_ref, own_ref, other_ref, gain_ref, *rest, outs):
    out_refs, terms_ref = rest[-outs - 1 : -1], rest[-1]
    clear_at_start(terms_ref, 1)
    own = own_ref[...].astype(F32)
    unit, inverse = unit_norm(v_ref[...].astype(F32))
    grad_normed = (own + other_ref[...].astype(F32)) * gain_ref[...]
    mean = jnp.mean(grad_normed * unit, axis=-1, keepdims=True)
    result = base_ref[...].astype(F32) + inverse * (grad_normed - unit * mean)
    for ref in out_refs:
        ref[...] = result.astype(ref.dtype)
    terms_ref[...] += jnp.sum((own * unit).reshape(-1, 8, own.shape[1]), axis=0)


def norm_back(values, base, own, other, gain, row, types, into, after=()):
    tokens, width = values.shape
    rows = own.shape[0]
    tile = min(256, rows)
    block = (tile, width)
    at_whole = lambda j: (row // tile + j, 0)
    at_half = lambda j: (j, 0)
    fixed = lambda j: (0, 0)
    ins = [(values, block, at_whole), (base, block, at_whole)]
    ins += [(own, block, at_half), (other, block, at_half), (gain, (1, width), fixed)]
    alias = None
    if into is not None:
        alias = {o: len(ins) + o for o in range(len(types))}
        ins += [(array, None, None) for array in into]
    return call(
        functools.partial(norm_back_kernel, outs=len(types)),
        (rows // tile,),
        ins,
        [((tokens, width), kind, block, at_whole) for kind in types]
        + [((8, width), F32, (8, width), fixed)],
        alias=alias,
        after=after,
        name="norm_back",
        cost=7.5,
    )


def sum_kernel(*refs):
    own, other = refs[1][...].astype(F32), refs[2][...].astype(F32)
    refs[-1][...] = (refs[0][...] + (own + other)).astype(BF16)


def sum_rows(values, parts, row, into, after=()):
    tokens, width = values.shape
    rows = parts[0].shape[0]
    tile = min(256, rows)
    block = (tile, width)
    at_whole = lambda j: (row // tile + j, 0)
    ins = [(values, block, at_whole)] + [(part, block, lambda j: (j, 0)) for part in parts]
    if into is not None:
        ins.append((into, None, None))
    return call(
        sum_kernel,
        (rows // tile,),
        ins,
        [((tokens, width), BF16, block, at_whole)],
        alias=None if into is None else {0: len(ins) - 1},
        after=after,
        name="sum_rows",
        cost=6,
    )[0]


def terms_kernel(v_ref, own_ref, terms_ref):
    clear_at_start(terms_ref, 1)
    unit = unit_norm(v_ref[...].astype(F32))[0]
    terms_ref[...] += jnp.sum((own_ref[...].astype(F32) * unit).reshape(-1, 8, unit.shape[1]), axis=0)


def gain_terms(values, own, row, after=()):
    width = values.shape[1]
    rows = own.shape[0]
    tile = min(256, rows)
    return call(
        terms_kernel,
        (rows // tile,),
        [
            (values, (tile, width), lambda j: (row // tile + j, 0)),
            (own, (tile, width), lambda j: (j, 0)),
        ],
        [((8, width), F32, (8, width), lambda j: (0, 0))],
        after=after,
        name="gain_terms",
        cost=4,
    )[0]


def add_kernel(*refs, widths):
    start = 0
    for at, width in enumerate(widths):
        left, right = refs[2 * at][...].astype(F32), refs[2 * at + 1][...].astype(F32)
        refs[-1][:, start : start + width] = (left + right.reshape(left.shape)).astype(BF16)
        start += width


def add_rows(parts, after=()):
    rows = parts[0][0].shape[0]
    widths = [left.shape[1] for left, _ in parts]
    tile, total = rows // 2, sum(widths)
    ins = []
    for left, right in parts:
        ins.append((left, (tile, left.shape[1]), lambda j: (j, 0)))
        if right.ndim == 3:
            ins.append((right, (1, tile, right.shape[2]), lambda j: (1, j, 0)))
        else:
            ins.append((right, (tile, right.shape[1]), lambda j: (j, 0)))
    return call(
        functools.partial(add_kernel, widths=widths),
        (2,),
        ins,
        [((rows, total), BF16, (tile, total), lambda j: (j, 0))],
        after=after,
        name="add_rows",
        cost=3,
    )[0]


def split_heads(both, which):
    cuts = range(which, both.shape[1] // HEAD_DIM, 2)
    return jnp.concatenate([both[:, at * HEAD_DIM : (at + 1) * HEAD_DIM] for at in cuts], axis=1)


def behind(value, *others):
    return lax.optimization_barrier((value,) + others)[0]


def shards(
    inputs,
    span_order,
    first_gain,
    query_proj,
    key_matrix,
    value_matrix,
    query_norm,
    key_norm,
    output_proj,
    second_gain,
    gate_proj,
    up_proj,
    down_proj,
    cotangent,
):
    seqs, local, width = inputs.shape
    tokens = seqs * local
    span = local // 2
    shard = query_proj.shape[0]
    head_shard = query_norm.shape[0]
    columns = query_proj.shape[1]
    groups = columns // GROUP
    units = gate_proj.shape[1]
    third = units // 3
    dp_size, tp_size = lax.axis_size("dp"), lax.axis_size("tp")
    ctx, tp_at = lax.axis_index("ctx"), lax.axis_index("tp")
    x_at, core_at = ctx // 2, ctx % 2
    share = lax.axis_index("dp") * 4 + ctx
    half_rows = tokens // 2
    half_seqs = seqs // 2
    pair = tp_size == 2

    def swap(axis, pairs, value, name):
        with jax.named_scope(name):
            return lax.ppermute(value, axis, pairs)

    tp_swap = lambda value, name: swap("tp", TP_SWAP, value, name + "_over_tp")
    core_swap = lambda value, name: swap("ctx", CORE_SWAP, value, name + "_over_core")
    x_swap = lambda value, name: swap("ctx", X_SWAP, value, name + "_over_x")

    def tp_start(part, name):
        if pair:
            return part, tp_swap(part, name)
        return lax.psum(part, "tp"), jnp.zeros_like(part)

    small = [first_gain, second_gain, jnp.pad(query_norm, (0, shard - head_shard))]
    small += [jnp.pad(key_norm, (0, shard - head_shard))]
    small = jnp.pad(jnp.stack(small), ((0, shard - len(small)), (0, BLOCK - shard)))
    shard_one = pack_first(
        query_proj, key_matrix, value_matrix, output_proj, gate_proj, up_proj, down_proj, small, third
    )
    weights = lax.all_gather(shard_one, ("dp", "ctx"), axis=0, tiled=True)

    pairs = span_order.reshape(seqs, 4, 2)
    relative = jnp.stack([ctx, ctx ^ 1, ctx ^ 2, ctx ^ 3])
    orders = jnp.take(pairs, relative, axis=1).reshape(seqs, 8)
    places = (
        orders[:, 0:2, None] * span + jnp.arange(span, dtype=jnp.int32)[None, None, :]
    ).reshape(tokens)
    half_dim = HEAD_DIM // 2
    frequency = ROPE_BASE ** (-(jnp.arange(half_dim, dtype=F32) * (2.0 / HEAD_DIM)))
    angles = places.astype(F32)[:, None] * frequency[None, :]
    cosine, sine = jnp.cos(angles), jnp.sin(angles)
    cosine = jnp.concatenate([cosine, cosine], axis=1)
    sine = jnp.concatenate([-sine, sine], axis=1)
    dps = jnp.arange(dp_size, dtype=jnp.int32)
    other_first = jnp.stack([1 - x_at, x_at])
    cores = jnp.stack([1 - core_at, core_at])
    order = cores[:, None, None] + 2 * other_first[None, :, None] + 4 * dps[None, None, :]
    order = order.reshape(-1).astype(jnp.int32)
    spot = jnp.stack([tp_at, core_at]).astype(jnp.int32)
    input_rows = inputs.reshape(tokens, width)
    cot_rows = cotangent.reshape(tokens, width)
    shard_two = pack_second(gate_proj, up_proj, down_proj, third, after=(shard_one,))

    def turned(left, name, after=()):
        to_core, own = turned_blocks(order, left, after=after)
        return own, core_swap(to_core, name)

    cot_turned = turned(cot_rows, "cotangent", after=(shard_two,))
    weights, cosine, sine, orders, order, spot, cot_turned, shard_two = lax.optimization_barrier(
        (weights, cosine, sine, orders, order, spot, cot_turned, shard_two)
    )

    small = weights[:, 3 * columns + 3 * third :].reshape(-1, shard, BLOCK)[:, 0:4, 0:shard]
    small = jnp.transpose(small, (1, 0, 2)).astype(F32)
    gain_first, gain_second = small[0].reshape(1, width), small[1].reshape(1, width)
    gain_query = small[2, :, 0:head_shard].reshape(1, HEAD_DIM)
    gain_key = small[3, :, 0:head_shard].reshape(1, HEAD_DIM)

    feed_one = norm_rows(input_rows, gain_first)
    kv, raw_kv, latest = [], [], ()
    for h in range(2):
        part = project(
            feed_one, weights, cosine, sine, gain_key, groups, groups, 1, h * half_rows, half_rows, after=latest
        )
        kv.append(part[0])
        raw_kv.append(part[1])
        latest = (part[0],)
        if pair and h == 0:
            half_width = width // 2
            sent = lax.dynamic_slice(
                behind(weights, part[0]), (core_at * half_width, 2 * columns), (half_width, columns)
            )
            output_same = tp_swap(sent, "output_proj")
            latest = (sent,)
    across = [x_swap(kv[0], "kv0")]
    q, raw_q = project(
        feed_one, weights, cosine, sine, gain_query, groups, 0, 2, 0, tokens, after=(kv[1],)
    )
    one_turned = turned(feed_one, "normed_one", after=(q,))
    across.append(x_swap(behind(kv[1], across[0], one_turned[0]), "kv1"))
    others = [
        (core_swap(kv[h], f"kv{h}"), across[h], core_swap(across[h], f"kv{h}_across"))
        for h in range(2)
    ]
    shard_two = behind(shard_two, across[1], *others[0])
    weights_two = lax.all_gather(shard_two, ("dp", "ctx"), axis=0, tiled=True)

    settled = ()
    if pair:
        output_swapped = core_swap(behind(output_same, across[1]), "output_proj")
        settled = (output_swapped,)
    attended, joined = [], None
    for h in range(2):
        attended.append(
            attend(
                orders, q, kv[h], others[h], h * half_seqs, half_seqs, local, after=tuple(attended) or settled
            )
        )
    attended_pair = attended, [core_swap(part, "attended") for part in attended]
    if pair:
        other_heads = [tp_swap(part, f"attended{h}") for h, part in enumerate(attended)]
        for h in range(2):
            joined = output_join(
                spot, input_rows, attended[h], other_heads[h], weights, 2,
                output_same, output_swapped, gain_second, h * half_rows, joined,
            )
    else:
        for h in range(2):
            part = nt_product([(attended[h], weights, 2 * columns)], 0, half_rows)
            started = tp_start(part, f"attended{h}")
            joined = join(input_rows, *started, gain_second, h * half_rows, joined)
    middle, feed_two = joined

    cut = width // 4
    tile = min(512, third)

    class Gradient:
        def __init__(self, name, parts, after=()):
            self.name = name
            to_x, self.keep = grad_product(parts, tile, (cut, cut), after=after)
            self.from_x = x_swap(to_x, name)

    def over_dp(name, grads, after=()):
        summed = add_rows([(grad.keep, grad.from_x) for grad in grads], after=after)
        with jax.named_scope(name + "_over_dp"):
            return summed, lax.psum_scatter(summed, "dp", scatter_dimension=0, tiled=True)

    def with_core(values, name):
        return [([value], [core_swap(value, name)]) for value in values]

    names = ("hidden", "gate_back", "up_back")
    starts = [3 * columns + at * third for at in range(3)]
    settled = (*attended_pair[1], one_turned[1])
    two_turned = turned(feed_two, "normed_two", after=settled)
    acts = feed(feed_two, cot_rows, weights, starts, tile, third, 1, after=(two_turned[0],))
    firsts = [([a[0]], [core_swap(a[0], n + "_one")]) for a, n in zip(acts, names)]
    parts = [(cot_turned, firsts[0]), (two_turned, firsts[1]), (two_turned, firsts[2])]
    first_third = Gradient("first_third", parts)
    starts = [at * 2 * third for at in range(3)]
    acts = feed(
        feed_two, cot_rows, weights_two, starts, tile, 2 * third, 1, after=(first_third.keep,)
    )
    seconds = [([a[0]], [core_swap(a[0], n + "_two")]) for a, n in zip(acts, names)]

    def feed_terms(at, kind):
        place = 3 * columns + kind * third
        return [(firsts[at][0][0], weights, place), (seconds[at][0][0], weights_two, 2 * kind * third)]

    back_terms = feed_terms(1, 0) + feed_terms(2, 1)
    back, out_started = [], []
    part = nt_product(back_terms, 0, half_rows)
    back.append(tp_start(part, "back0"))
    down_two = Gradient("down_two", [(cot_turned, seconds[0])], after=(part,))
    landed = (seconds[1][1][0], seconds[2][1][0])
    part = nt_product(back_terms, half_rows, half_rows, after=(down_two.keep, *landed))
    back.append(tp_start(part, "back1"))
    done, first_out = over_dp("first_third", [first_third], after=(part,))
    gate_two = Gradient("gate_two", [(two_turned, seconds[1])], after=(done,))

    def out_half(h, after):
        part = nt_product(feed_terms(0, 2), h * half_rows, half_rows, after=after)
        out_started.append(tp_start(part, f"out{h}"))
        return part

    grads, q_back, k_back, pieces, one = None, None, None, [], []
    sums = {"second": 0.0, "query": 0.0, "key": 0.0, "first": 0.0}

    def middle_half(h, after):
        *found, second = norm_back(
            middle, cot_rows, *back[h], gain_second, h * half_rows, (F32, BF16), grads, after=after
        )
        sums["second"] = sums["second"] + jnp.sum(second, axis=0)
        return found, nn_product(found[1], weights, 2 * columns, columns, h * half_rows, half_rows)

    def attention_half(h, grad_attended, after):
        found, to_own, to_x, to_core, query = attend_back(
            orders, q, kv[h], others[h], grad_attended, raw_q, cosine, sine, gain_query,
            h * half_seqs, half_seqs, local, q_back, after=after,
        )
        sums["query"] = sums["query"] + jnp.sum(query, axis=0)
        return found, to_own, to_x, core_swap(to_core, f"kv_grad{h}")

    def send_keys(h, held, after):
        to_own, to_x, from_core = held
        sent = add_rows([(to_x, from_core)], after=after)
        pieces.append((to_own, from_core, x_swap(sent, f"kv_grad{h}")))
        return sent

    def key_half(h, after):
        found, key = key_back(
            *pieces[h], raw_kv[h], cosine, sine, gain_key, h * half_seqs, half_seqs, local,
            tokens, k_back, after=after,
        )
        sums["key"] = sums["key"] + jnp.sum(key, axis=0)
        return found

    def one_half(h, after):
        terms = [(q_back, weights, 0), (k_back, weights, columns)]
        part = nt_product(terms, h * half_rows, half_rows, after=after)
        one.append(tp_start(part, f"one{h}"))
        return part

    grads, grad_attended = middle_half(0, (gate_two.keep,))
    part = out_half(0, (grad_attended,))
    q_back, *held = attention_half(0, grad_attended, (part,))
    grads, grad_attended = middle_half(1, (held[0],))
    grad_middle, middle_low = grads
    sent = send_keys(0, held, (grad_attended,))
    done, more_out = over_dp("down_gate_two", [down_two, gate_two], after=(sent, first_out))
    part = out_half(1, (done,))
    up_two = Gradient("up_two", [(two_turned, seconds[2])], after=(part,))
    landed = (pieces[0][2], out_started[0][1])
    q_back, *held = attention_half(1, grad_attended, (up_two.keep, *landed))
    q_pair = [q_back], [core_swap(q_back, "query_back")]
    k_back = key_half(0, (held[0],))
    sent = send_keys(1, held, (k_back,))
    outputs = sum_rows(middle, out_started[0], 0, None, after=(sent,))
    part = one_half(0, (outputs,))
    done, up_out = over_dp("up_two", [up_two], after=(part, more_out))
    query_grad = Gradient("query", [(one_turned, q_pair)], after=(done, out_started[1][1]))
    low_turned = turned(middle_low, "grad_middle", after=(query_grad.keep,))
    k_back = key_half(1, (low_turned[0],))
    outputs = sum_rows(middle, out_started[1], half_rows, outputs, after=(k_back,))
    part = one_half(1, (outputs,))
    k_pair = [k_back], [core_swap(k_back, "key_back")]
    key_grad = Gradient("key", [(one_turned, k_pair)], after=(part,))
    output_grad = Gradient("output", [(low_turned, attended_pair)], after=(key_grad.keep,))
    latest = (output_grad.keep,)
    for h in range(2):
        part = gain_terms(input_rows, one[h][0], h * half_rows, after=latest)
        latest = (part,)
        sums["first"] = sums["first"] + jnp.sum(part, axis=0)
    result = None
    for h in range(2):
        result = norm_back(
            input_rows, grad_middle, *one[h], gain_first, h * half_rows, (BF16,), result, after=latest
        )[0:1]
        latest = ()
    last = [query_grad, key_grad, output_grad]
    done, heads_out = over_dp("query_key_output", last, after=(result[0],))

    if not pair:
        sums["first"], sums["second"] = sums["first"] / tp_size, sums["second"] / tp_size
    totals = jnp.concatenate([sums[name] for name in ("first", "second", "query", "key")])
    totals = lax.psum(behind(totals, done), ("dp", "ctx", "tp"))
    cut_total = lambda start, size: lax.dynamic_slice(totals, (start + share * size,), (size,))

    grad_kv = heads_out[:, columns : 2 * columns].astype(F32)
    down_out, gate_out, up_first = [first_out[:, at * third : (at + 1) * third] for at in range(3)]
    beside = lambda left, right: jnp.concatenate([left, right], axis=1).astype(F32)
    return (
        outputs.reshape(inputs.shape),
        result[0].reshape(inputs.shape),
        cut_total(0, shard),
        heads_out[:, 0:columns].astype(F32),
        split_heads(grad_kv, 0),
        split_heads(grad_kv, 1),
        cut_total(2 * width, head_shard),
        cut_total(2 * width + HEAD_DIM, head_shard),
        heads_out[:, 2 * columns :].astype(F32).T,
        cut_total(width, shard),
        beside(gate_out, more_out[:, 2 * third :]),
        beside(up_first, up_out),
        beside(down_out, more_out[:, 0 : 2 * third]).T,
    )


def solution(mesh):
    rows = P(("dp", "ctx"))
    columns = P(("dp", "ctx"), "tp")
    turned = P("tp", ("dp", "ctx"))
    tokens = P("dp", "ctx", None)
    in_specs = (
        (tokens, P("dp", None), rows, columns, columns, columns, rows, rows, turned, rows)
        + (columns, columns, turned, tokens)
    )
    out_specs = (
        (tokens, tokens, rows, columns, columns, columns, rows, rows, turned, rows)
        + (columns, columns, turned)
    )
    return jax.shard_map(shards, mesh=mesh, in_specs=in_specs, out_specs=out_specs, check_vma=False)
```

```python
import functools

import jax
import jax.numpy as jnp
from jax import lax
from jax.experimental import pallas as pl
from jax.experimental.pallas import tpu as pltpu
from jax.sharding import PartitionSpec as P

HEAD_DIM = 128
GROUP = 2 * HEAD_DIM
BLOCK = 128
EPSILON = 1e-06
ROPE_BASE = 1000000.0
MASKED = -1e30
VMEM_LIMIT = 56 * 1024 * 1024
F32 = jnp.float32
BF16 = jnp.bfloat16
FLOPS_PER_US = 1e10

CORE_SWAP = [(0, 1), (1, 0), (2, 3), (3, 2)]
X_SWAP = [(0, 2), (2, 0), (1, 3), (3, 1)]
TP_SWAP = [(0, 1), (1, 0)]


def nn(left, right):
    return lax.dot_general(left, right, (((1,), (0,)), ((), ())), preferred_element_type=F32)


def nt(left, right):
    return lax.dot_general(left, right, (((1,), (1,)), ((), ())), preferred_element_type=F32)


def tn(left, right):
    return lax.dot_general(left, right, (((0,), (0,)), ((), ())), preferred_element_type=F32)


def unit_norm(values):
    inverse = lax.rsqrt(jnp.mean(values * values, axis=-1, keepdims=True) + EPSILON)
    return values * inverse, inverse


def swap_halves(values):
    return pltpu.roll(values, HEAD_DIM // 2, 1)


def call(kernel, grid, ins, outs, scratch=(), scalars=(), alias=None, after=(), name=None, cost=1.0):
    any_space = pl.BlockSpec(memory_space=pl.ANY)
    specs = [any_space if b is None else pl.BlockSpec(b, m) for _, b, m in ins]
    n_in, n_after, n_scalar = len(ins), len(after), len(scalars)

    def body(*refs):
        keep = refs[: n_scalar + n_in] + refs[n_scalar + n_in + n_after :]
        kernel(*keep)

    return pl.pallas_call(
        body,
        grid_spec=pltpu.PrefetchScalarGridSpec(
            num_scalar_prefetch=n_scalar,
            grid=grid,
            in_specs=specs + [any_space] * n_after,
            out_specs=[pl.BlockSpec(b, m) for _, _, b, m in outs],
            scratch_shapes=list(scratch),
        ),
        out_shape=[jax.ShapeDtypeStruct(s, d) for s, d, _, _ in outs],
        input_output_aliases={n_scalar + i: o for o, i in (alias or {}).items()},
        compiler_params=pltpu.CompilerParams(
            dimension_semantics=("arbitrary",) * len(grid), vmem_limit_bytes=VMEM_LIMIT
        ),
        cost_estimate=pl.CostEstimate(
            flops=int(cost * FLOPS_PER_US), bytes_accessed=0, transcendentals=0
        ),
        name=name,
    )(*scalars, *[a for a, _, _ in ins], *after)


def pack_first_kernel(q_ref, k_ref, v_ref, o_ref, g_ref, u_ref, d_ref, small_ref, out_ref):
    columns, third = q_ref.shape[1], g_ref.shape[1]
    out_ref[:, 0:columns] = q_ref[...]
    for at in range(columns // GROUP):
        cut = slice(at * HEAD_DIM, (at + 1) * HEAD_DIM)
        start = columns + at * GROUP
        out_ref[:, start : start + HEAD_DIM] = k_ref[:, cut]
        out_ref[:, start + HEAD_DIM : start + GROUP] = v_ref[:, cut]
    out_ref[:, 2 * columns : 3 * columns] = o_ref[...].T
    start = 3 * columns
    out_ref[:, start : start + third] = g_ref[...]
    out_ref[:, start + third : start + 2 * third] = u_ref[...]
    out_ref[:, start + 2 * third : start + 3 * third] = d_ref[...].T
    out_ref[:, start + 3 * third :] = small_ref[...]


def pack_first(q, k, v, o, g, u, d, small, third):
    shard, columns = q.shape
    whole = lambda array: (array, array.shape, lambda j: (0, 0))
    total = 3 * columns + 3 * third + BLOCK
    return call(
        pack_first_kernel,
        (1,),
        [whole(q), whole(k), whole(v), whole(o)]
        + [(g, (shard, third), lambda j: (0, 0)), (u, (shard, third), lambda j: (0, 0))]
        + [(d, (third, shard), lambda j: (0, 0)), whole(small)],
        [((shard, total), BF16, (shard, total), lambda j: (0, 0))],
        name="pack_first",
        cost=3,
    )[0]


def pack_second_kernel(g_ref, u_ref, d_ref, out_ref):
    step = pl.program_id(0)
    part = step // 2

    @pl.when(part == 0)
    def _():
        out_ref[...] = g_ref[...]

    @pl.when(part == 1)
    def _():
        out_ref[...] = u_ref[...]

    @pl.when(part == 2)
    def _():
        out_ref[...] = d_ref[...].T


def pack_second(g, u, d, third, after=()):
    shard = g.shape[0]
    return call(
        pack_second_kernel,
        (6,),
        [(g, (shard, third), lambda j: (0, 1 + j % 2)), (u, (shard, third), lambda j: (0, 1 + j % 2))]
        + [(d, (third, shard), lambda j: (1 + j % 2, 0))],
        [((shard, 6 * third), BF16, (shard, third), lambda j: (0, j))],
        after=after,
        name="pack_second",
        cost=5,
    )[0]


def norm_kernel(x_ref, gain_ref, out_ref):
    out_ref[...] = (unit_norm(x_ref[...].astype(F32))[0] * gain_ref[...]).astype(BF16)


def norm_rows(x, gain, after=()):
    tokens, width = x.shape
    tile = min(256, tokens)
    block = (tile, width)
    return call(
        norm_kernel,
        (tokens // tile,),
        [(x, block, lambda j: (j, 0)), (gain, (1, width), lambda j: (0, 0))],
        [((tokens, width), BF16, block, lambda j: (j, 0))],
        after=after,
        name="norm_rows",
        cost=5,
    )[0]


def project_kernel(x_ref, w_ref, cos_ref, sin_ref, gain_ref, out_ref, raw_ref, *, turned, rows):
    for at in range(0, x_ref.shape[0], rows):
        part = pl.ds(at, rows)
        raw = nn(x_ref[part, :], w_ref[...])
        raw_ref[part, :] = raw
        cosine, sine = cos_ref[part, :], sin_ref[part, :]
        for head in range(2):
            values = raw[:, head * HEAD_DIM : (head + 1) * HEAD_DIM]
            if head < turned:
                scaled = unit_norm(values)[0] * gain_ref[...]
                values = scaled * cosine + swap_halves(scaled) * sine
            out_ref[part, head * HEAD_DIM : (head + 1) * HEAD_DIM] = values.astype(BF16)


def project(x, weights, cosine, sine, gain, groups, first, turned, row, rows, after=()):
    width = x.shape[1]
    some = lambda j: (row // rows, 0)
    column = lambda j: (0, j)
    columns = groups * GROUP
    return call(
        functools.partial(project_kernel, turned=turned, rows=min(256, rows)),
        (groups,),
        [
            (x, (rows, width), some),
            (weights, (width, GROUP), lambda j: (0, first + j)),
            (cosine, (rows, HEAD_DIM), some),
            (sine, (rows, HEAD_DIM), some),
            (gain, (1, HEAD_DIM), lambda j: (0, 0)),
        ],
        [
            ((rows, columns), BF16, (rows, GROUP), column),
            ((rows, columns), F32, (rows, GROUP), column),
        ],
        after=after,
        name="project",
        cost=10,
    )


def span_places(orders_ref, seq, piece, span, shape, dim):
    index = lax.broadcasted_iota(jnp.int32, shape, dim)
    first, second = orders_ref[seq, 2 * piece], orders_ref[seq, 2 * piece + 1]
    return jnp.where(index < span, first * span + index, second * span + index - span)


def stacked_heads(block):
    return jnp.concatenate([block[:, 0:HEAD_DIM], block[:, HEAD_DIM:GROUP]], axis=0)


def masked_exponents(orders_ref, seq, query, pieces, span):
    rows, keys = query.shape[0], pieces[0].shape[0]
    scale = HEAD_DIM**-0.5
    places = span_places(orders_ref, seq, 0, span, (rows // 2, 1), 0)
    places = jnp.concatenate([places, places], axis=0)
    scores = []
    for at, piece in enumerate(pieces):
        key_places = span_places(orders_ref, seq, at, span, (1, keys), 1)
        product = nt(query, piece[:, 0:HEAD_DIM]) * scale
        scores.append(jnp.where(key_places <= places, product, MASKED))
    peak = functools.reduce(jnp.maximum, [jnp.max(s, axis=1, keepdims=True) for s in scores])
    exponents = [jnp.exp(s - peak) for s in scores]
    total = functools.reduce(jnp.add, [jnp.sum(e, axis=1, keepdims=True) for e in exponents])
    return exponents, 1.0 / total


def attend_kernel(orders_ref, q_ref, own_ref, core_ref, x_ref, diag_ref, out_ref, prob_ref, *, first, span):
    seq = pl.program_id(0) + first
    local = q_ref.shape[0]
    for group in range(q_ref.shape[1] // GROUP):
        columns = slice(group * GROUP, (group + 1) * GROUP)
        rows = slice(group * 2 * local, (group + 1) * 2 * local)
        query = stacked_heads(q_ref[:, columns])
        pieces = [ref[:, columns] for ref in (own_ref, core_ref, x_ref, diag_ref)]
        exponents, inverse = masked_exponents(orders_ref, seq, query, pieces, span)
        total = None
        for at, (exponent, piece) in enumerate(zip(exponents, pieces)):
            prob = (exponent * inverse).astype(BF16)
            prob_ref[0, rows, at * local : (at + 1) * local] = prob
            product = nn(prob, piece[:, HEAD_DIM:GROUP])
            total = product if total is None else total + product
        result = total.astype(BF16)
        for head in range(2):
            start = group * GROUP + head * HEAD_DIM
            out_ref[:, start : start + HEAD_DIM] = result[head * local : (head + 1) * local]


def attend(orders, q, kv, others, first, count, local, after=()):
    columns = q.shape[1]
    block = (local, columns)
    at_whole = lambda s, o: (s + first, 0)
    at_half = lambda s, o: (s, 0)
    ins = [(q, block, at_whole), (kv, block, at_half)] + [(k, block, at_half) for k in others]
    prob = (1, columns // GROUP * 2 * local, 4 * local)
    return call(
        functools.partial(attend_kernel, first=first, span=local // 2),
        (count,),
        ins,
        [
            ((count * local, columns), BF16, block, at_half),
            ((count,) + prob[1:], BF16, prob, lambda s, o: (s, 0, 0)),
        ],
        scalars=(orders,),
        after=after,
        name="attend",
        cost=11,
    )


def turn_back(grad, raw, cosine, sine, gain):
    turned = grad * cosine - swap_halves(grad) * sine
    unit, inverse = unit_norm(raw)
    grad_normed = turned * gain
    mean = jnp.mean(grad_normed * unit, axis=-1, keepdims=True)
    terms = jnp.sum((turned * unit).reshape(-1, 8, HEAD_DIM), axis=0)
    return (inverse * (grad_normed - unit * mean)).astype(BF16), terms


def clear_at_start(ref, dims):
    start = functools.reduce(jnp.logical_and, [pl.program_id(d) == 0 for d in range(dims)])

    @pl.when(start)
    def _():
        ref[...] = jnp.zeros_like(ref)


def attend_back_kernel(
    q_ref, own_ref, core_ref, x_ref, diag_ref, prob_ref, grad_ref, raw_ref, cos_ref, sin_ref, gain_ref, *rest
):
    q_back_ref, own_out, x_out, core_out, gain_out = rest[-5:]
    clear_at_start(gain_out, 1)
    scale = HEAD_DIM**-0.5
    local = q_ref.shape[0]
    outs = (own_out, core_out.at[0], x_out, core_out.at[1])
    for group in range(q_ref.shape[1] // GROUP):
        start = group * GROUP
        both = slice(start, start + GROUP)
        rows = slice(group * 2 * local, (group + 1) * 2 * local)
        query = stacked_heads(q_ref[:, both])
        grad = stacked_heads(grad_ref[:, both])
        pieces = [ref[:, both] for ref in (own_ref, core_ref, x_ref, diag_ref)]
        lows = [prob_ref[0, rows, at * local : (at + 1) * local] for at in range(4)]
        products = [low.astype(F32) * nt(grad, p[:, HEAD_DIM:GROUP]) for low, p in zip(lows, pieces)]
        delta = functools.reduce(jnp.add, [jnp.sum(p, axis=1, keepdims=True) for p in products])
        grad_scores = [(p - low.astype(F32) * delta).astype(BF16) for p, low in zip(products, lows)]
        grad_query = functools.reduce(
            jnp.add, [nn(s, p[:, 0:HEAD_DIM]) for s, p in zip(grad_scores, pieces)]
        )
        for out, scores, low in zip(outs, grad_scores, lows):
            out[:, start : start + HEAD_DIM] = (tn(scores, query) * scale).astype(BF16)
            out[:, start + HEAD_DIM : start + GROUP] = tn(low, grad).astype(BF16)
        for head in range(2):
            columns = slice(start + head * HEAD_DIM, start + (head + 1) * HEAD_DIM)
            result, terms = turn_back(
                grad_query[head * local : (head + 1) * local] * scale,
                raw_ref[:, columns],
                cos_ref[...],
                sin_ref[...],
                gain_ref[...],
            )
            q_back_ref[:, columns] = result
            gain_out[...] += terms


def attend_back(q, kv, others, prob, grad, raw, cosine, sine, gain, first, count, local, into, after=()):
    columns = q.shape[1]
    block = (local, columns)
    at_whole = lambda s: (s + first, 0)
    at_half = lambda s: (s, 0)
    fixed = lambda s: (0, 0)
    ins = [(q, block, at_whole), (kv, block, at_half)] + [(k, block, at_half) for k in others]
    ins += [(prob, (1,) + prob.shape[1:], lambda s: (s, 0, 0))]
    ins += [(grad, block, at_half), (raw, block, at_whole)]
    ins += [(cosine, (local, HEAD_DIM), at_whole), (sine, (local, HEAD_DIM), at_whole)]
    ins += [(gain, (1, HEAD_DIM), fixed)]
    if into is not None:
        ins.append((into, None, None))
    piece = ((count * local, columns), BF16, block, at_half)
    return call(
        attend_back_kernel,
        (count,),
        ins,
        [(q.shape, BF16, block, at_whole)]
        + [piece] * 2
        + [((2, count * local, columns), BF16, (2, local, columns), lambda s: (0, s, 0))]
        + [((8, HEAD_DIM), F32, (8, HEAD_DIM), fixed)],
        alias=None if into is None else {0: len(ins) - 1},
        after=after,
        name="attend_back",
        cost=25,
    )


def key_back_kernel(mine_ref, core_ref, x_ref, raw_ref, cos_ref, sin_ref, gain_ref, *rest):
    out_ref, gain_out = rest[-2:]
    clear_at_start(gain_out, 1)
    for group in range(mine_ref.shape[1] // GROUP):
        start = group * GROUP
        both = slice(start, start + GROUP)
        parts = [ref[:, both].astype(F32) for ref in (mine_ref, core_ref.at[0], x_ref)]
        grad = functools.reduce(jnp.add, parts)
        result, terms = turn_back(
            grad[:, 0:HEAD_DIM],
            raw_ref[:, start : start + HEAD_DIM],
            cos_ref[...],
            sin_ref[...],
            gain_ref[...],
        )
        out_ref[:, start : start + HEAD_DIM] = result
        out_ref[:, start + HEAD_DIM : start + GROUP] = grad[:, HEAD_DIM:GROUP].astype(BF16)
        gain_out[...] += terms


def key_back(mine, core, x, raw, cosine, sine, gain, first, count, local, tokens, into, after=()):
    columns = mine.shape[1]
    block = (local, columns)
    at_whole = lambda s: (s + first, 0)
    at_half = lambda s: (s, 0)
    fixed = lambda s: (0, 0)
    ins = [(mine, block, at_half), (core, (1,) + block, lambda s: (0, s, 0)), (x, block, at_half)]
    ins += [(raw, block, at_half)]
    ins += [(cosine, (local, HEAD_DIM), at_whole), (sine, (local, HEAD_DIM), at_whole)]
    ins += [(gain, (1, HEAD_DIM), fixed)]
    if into is not None:
        ins.append((into, None, None))
    return call(
        key_back_kernel,
        (count,),
        ins,
        [
            ((tokens, columns), BF16, block, at_whole),
            ((8, HEAD_DIM), F32, (8, HEAD_DIM), fixed),
        ],
        alias=None if into is None else {0: len(ins) - 1},
        after=after,
        name="key_back",
        cost=5,
    )


def feed_kernel(x_ref, c_ref, g_ref, u_ref, d_ref, *outs, rows, steps):
    step, pieces = pl.program_id(0), len(outs) // 3

    def fill(hidden_ref, gate_ref, up_ref):
        for at in range(0, x_ref.shape[0], rows):
            part = pl.ds(at, rows)
            gate = nn(x_ref[part, :], g_ref[...])
            upward = nn(x_ref[part, :], u_ref[...])
            grad = nn(c_ref[part, :], d_ref[...])
            sigmoid = jax.nn.sigmoid(gate)
            silu = gate * sigmoid
            hidden_ref[part, :] = (silu * upward).astype(BF16)
            slope = sigmoid + silu * (1.0 - sigmoid)
            gate_ref[part, :] = (grad * upward * slope).astype(BF16)
            up_ref[part, :] = (grad * silu).astype(BF16)

    for piece in range(pieces):
        run = functools.partial(fill, *outs[piece::pieces])
        if pieces == 1:
            run()
        else:
            pl.when(step // steps == piece)(run)


def feed(x, c, weights, starts, tile, piece, pieces, after=()):
    tokens, width = x.shape
    steps = piece // tile
    whole = lambda j: (0, 0)
    ins = [(x, (tokens, width), whole), (c, (tokens, width), whole)]
    for start in starts:
        ins.append((weights, (width, tile), lambda j, start=start: (0, start // tile + j)))
    outs = [
        ((tokens, piece), BF16, (tokens, tile), lambda j, at=at: (0, jnp.clip(j - at * steps, 0, steps - 1)))
        for _ in range(3)
        for at in range(pieces)
    ]
    found = call(
        functools.partial(feed_kernel, rows=min(256, tokens), steps=steps),
        (steps * pieces,),
        ins,
        outs,
        after=after,
        name="feed",
        cost=2 + piece * pieces * 0.0165,
    )
    return [found[kind * pieces : (kind + 1) * pieces] for kind in range(3)]


def nt_kernel(*refs, count):
    out_ref = refs[-1]
    total = None
    for left_ref, w_ref in zip(refs[:count], refs[count : 2 * count]):
        product = nt(left_ref[...], w_ref[...])
        total = product if total is None else total + product
    out_ref[...] = total.astype(out_ref.dtype)


def nt_product(terms, row, rows, after=()):
    width = terms[0][1].shape[0]
    tile = min(512, width)
    ins = [(left, (rows, left.shape[1]), lambda j: (row // rows, 0)) for left, _, _ in terms]
    ins += [
        (weights, (tile, left.shape[1]), lambda j, at=at // left.shape[1]: (j, at))
        for left, weights, at in terms
    ]
    return call(
        functools.partial(nt_kernel, count=len(terms)),
        (width // tile,),
        ins,
        [((rows, width), BF16, (rows, tile), lambda j: (0, j))],
        after=after,
        name="nt_product",
        cost=1.5 + rows * sum(left.shape[1] for left, _, _ in terms) * 6.0e-6,
    )[0]


def nn_kernel(x_ref, w_ref, out_ref):
    out_ref[...] = nn(x_ref[...], w_ref[...]).astype(out_ref.dtype)


def nn_product(left, weights, first_column, columns, row, rows, after=()):
    width = weights.shape[0]
    tile = min(512, columns)
    return call(
        nn_kernel,
        (columns // tile,),
        [
            (left, (rows, width), lambda j: (row // rows, 0)),
            (weights, (width, tile), lambda j: (0, first_column // tile + j)),
        ],
        [((rows, columns), BF16, (rows, tile), lambda j: (0, j))],
        after=after,
        name="nn_product",
        cost=6,
    )[0]


def output_join_kernel(
    at_ref, x_ref, mine_ref, other_ref, w_mine_ref, w_same_ref, w_swap_ref, gain_ref, *rest, steps
):
    middle_ref, normed_ref, rows_ref = rest[-3:]
    step = pl.program_id(0)
    tile = x_ref.shape[1]
    is_first, core = at_ref[0] == 0, at_ref[1]
    direct = (step * 2 // steps) == core
    mine, other, w_mine = mine_ref[...], other_ref[...], w_mine_ref[...]
    w_other = jnp.where(direct, w_same_ref[...], w_swap_ref[...])
    total = nt(jnp.where(is_first, mine, other), jnp.where(is_first, w_mine, w_other))
    total += nt(jnp.where(is_first, other, mine), jnp.where(is_first, w_other, w_mine))
    columns = pl.ds(pl.multiple_of(step * tile, tile), tile)
    rows_ref[:, columns] = x_ref[...].astype(F32) + total

    @pl.when(step == steps - 1)
    def _():
        middle = rows_ref[...]
        middle_ref[...] = middle
        normed_ref[...] = (unit_norm(middle)[0] * gain_ref[...]).astype(BF16)


def output_join(at, x, mine, other, weights, block, same, swapped, gain, row, into, after=()):
    tokens, width = x.shape
    rows, columns = mine.shape
    tile = min(512, width // 2)
    steps = width // tile
    fixed = lambda j, a: (0, 0)
    fetched = lambda j, a: (j % (steps // 2), 0)
    ins = [
        (x, (rows, tile), lambda j, a: (row // rows, j)),
        (mine, (rows, columns), fixed),
        (other, (rows, columns), fixed),
        (weights, (tile, columns), lambda j, a: (j, block)),
        (same, (tile, columns), fetched),
        (swapped, (tile, columns), fetched),
        (gain, (1, width), fixed),
    ]
    alias = None
    if into is not None:
        alias = {o: len(ins) + o for o in range(2)}
        ins += [(array, None, None) for array in into]
    out = lambda kind: ((tokens, width), kind, (rows, width), lambda j, a: (row // rows, 0))
    return call(
        functools.partial(output_join_kernel, steps=steps),
        (steps,),
        ins,
        [out(F32), out(BF16)],
        scratch=[pltpu.VMEM((rows, width), F32)],
        scalars=(at,),
        alias=alias,
        after=after,
        name="output_join",
        cost=15,
    )


def turn_kernel(order_ref, *refs):
    ins, outs = refs[:4], refs[4:]
    step = pl.program_id(0)

    def fill(out_ref):
        for at, ref in enumerate(ins):
            out_ref[at * BLOCK : (at + 1) * BLOCK, :] = ref[...].T

    pl.when(step < 2)(lambda: fill(outs[0]))
    pl.when(step >= 2)(lambda: fill(outs[1]))


def turned_blocks(order, left, after=()):
    tokens, width = left.shape
    ins = [(left, (tokens, BLOCK), lambda j, o, at=at: (0, o[4 * j + at])) for at in range(4)]
    out = lambda spot: ((width // 2, tokens), BF16, (4 * BLOCK, tokens), spot)
    return call(
        turn_kernel,
        (width // BLOCK // 4,),
        ins,
        [out(lambda j, o: (jnp.minimum(j, 1), 0)), out(lambda j, o: (jnp.maximum(j - 2, 0), 0))],
        scalars=(order,),
        after=after,
        name="turned_blocks",
        cost=6,
    )


def grad_kernel(*refs, plan, outs):
    step, begin, used = pl.program_id(0), 0, 0
    out_refs = refs[-outs:]

    def fill(left_refs, right_refs):
        for at, out in enumerate(out_refs):
            size, total = out.shape[0], None
            rows = pl.ds(at * size, size)
            for left_ref, pieces in zip(left_refs, right_refs):
                start = 0
                for piece in pieces:
                    tokens = piece.shape[0]
                    product = nn(left_ref[rows, start : start + tokens], piece[...])
                    total = product if total is None else total + product
                    start += tokens
            out[...] = total.astype(BF16)

    for pieces, count in plan:
        part = refs[used : used + 2 + 2 * pieces]
        run = functools.partial(fill, part[:2], (part[2 : 2 + pieces], part[2 + pieces :]))
        if len(plan) == 1:
            run()
        else:
            pl.when((step >= begin) & (step < begin + count))(run)
        begin, used = begin + count, used + 2 + 2 * pieces


def grad_product(parts, tile, cuts, after=()):
    width, tokens = parts[0][0][0].shape
    ins, begin, plan = [], 0, []
    for lefts, rights in parts:
        count = rights[0][0].shape[1] // tile
        ins += [(left, left.shape, lambda j: (0, 0)) for left in lefts]
        spot = lambda j, begin=begin, count=count: (0, jnp.clip(j - begin, 0, count - 1))
        ins += [(piece, (piece.shape[0], tile), spot) for pieces in rights for piece in pieces]
        plan.append((len(rights[0]), count))
        begin += count
    return call(
        functools.partial(grad_kernel, plan=plan, outs=len(cuts)),
        (begin,),
        ins,
        [((cut, begin * tile), BF16, (cut, tile), lambda j: (0, j)) for cut in cuts],
        after=after,
        name="grad_product",
        cost=3.5 + begin * tile * 0.0047,
    )


def join_kernel(x_ref, own_ref, other_ref, gain_ref, *rest):
    middle_ref, normed_ref = rest[-2:]
    middle = x_ref[...].astype(F32) + (own_ref[...].astype(F32) + other_ref[...].astype(F32))
    middle_ref[...] = middle
    normed_ref[...] = (unit_norm(middle)[0] * gain_ref[...]).astype(BF16)


def join(x, own, other, gain, row, into, after=()):
    tokens, width = x.shape
    rows = own.shape[0]
    tile = min(256, rows)
    block = (tile, width)
    at_whole = lambda j: (row // tile + j, 0)
    at_half = lambda j: (j, 0)
    ins = [(x, block, at_whole), (own, block, at_half), (other, block, at_half)]
    ins += [(gain, (1, width), lambda j: (0, 0))]
    alias = None
    if into is not None:
        alias = {o: len(ins) + o for o in range(2)}
        ins += [(array, None, None) for array in into]
    return call(
        join_kernel,
        (rows // tile,),
        ins,
        [((tokens, width), F32, block, at_whole), ((tokens, width), BF16, block, at_whole)],
        alias=alias,
        after=after,
        name="join",
        cost=7.5,
    )


def norm_back_kernel(v_ref, base_ref, own_ref, other_ref, gain_ref, *rest, outs):
    out_refs, terms_ref = rest[-outs - 1 : -1], rest[-1]
    clear_at_start(terms_ref, 1)
    own = own_ref[...].astype(F32)
    unit, inverse = unit_norm(v_ref[...].astype(F32))
    grad_normed = (own + other_ref[...].astype(F32)) * gain_ref[...]
    mean = jnp.mean(grad_normed * unit, axis=-1, keepdims=True)
    result = base_ref[...].astype(F32) + inverse * (grad_normed - unit * mean)
    for ref in out_refs:
        ref[...] = result.astype(ref.dtype)
    terms_ref[...] += jnp.sum((own * unit).reshape(-1, 8, own.shape[1]), axis=0)


def norm_back(values, base, own, other, gain, row, types, into, after=()):
    tokens, width = values.shape
    rows = own.shape[0]
    tile = min(256, rows)
    block = (tile, width)
    at_whole = lambda j: (row // tile + j, 0)
    at_half = lambda j: (j, 0)
    fixed = lambda j: (0, 0)
    ins = [(values, block, at_whole), (base, block, at_whole)]
    ins += [(own, block, at_half), (other, block, at_half), (gain, (1, width), fixed)]
    alias = None
    if into is not None:
        alias = {o: len(ins) + o for o in range(len(types))}
        ins += [(array, None, None) for array in into]
    return call(
        functools.partial(norm_back_kernel, outs=len(types)),
        (rows // tile,),
        ins,
        [((tokens, width), kind, block, at_whole) for kind in types]
        + [((8, width), F32, (8, width), fixed)],
        alias=alias,
        after=after,
        name="norm_back",
        cost=7.5,
    )


def sum_kernel(*refs):
    own, other = refs[1][...].astype(F32), refs[2][...].astype(F32)
    refs[-1][...] = (refs[0][...] + (own + other)).astype(BF16)


def sum_rows(values, parts, row, into, after=()):
    tokens, width = values.shape
    rows = parts[0].shape[0]
    tile = min(256, rows)
    block = (tile, width)
    at_whole = lambda j: (row // tile + j, 0)
    ins = [(values, block, at_whole)] + [(part, block, lambda j: (j, 0)) for part in parts]
    if into is not None:
        ins.append((into, None, None))
    return call(
        sum_kernel,
        (rows // tile,),
        ins,
        [((tokens, width), BF16, block, at_whole)],
        alias=None if into is None else {0: len(ins) - 1},
        after=after,
        name="sum_rows",
        cost=6,
    )[0]


def terms_kernel(v_ref, own_ref, terms_ref):
    clear_at_start(terms_ref, 1)
    unit = unit_norm(v_ref[...].astype(F32))[0]
    terms_ref[...] += jnp.sum((own_ref[...].astype(F32) * unit).reshape(-1, 8, unit.shape[1]), axis=0)


def gain_terms(values, own, row, after=()):
    width = values.shape[1]
    rows = own.shape[0]
    tile = min(256, rows)
    return call(
        terms_kernel,
        (rows // tile,),
        [
            (values, (tile, width), lambda j: (row // tile + j, 0)),
            (own, (tile, width), lambda j: (j, 0)),
        ],
        [((8, width), F32, (8, width), lambda j: (0, 0))],
        after=after,
        name="gain_terms",
        cost=4,
    )[0]


def add_kernel(*refs, widths):
    start = 0
    for at, width in enumerate(widths):
        left, right = refs[2 * at][...].astype(F32), refs[2 * at + 1][...].astype(F32)
        refs[-1][:, start : start + width] = (left + right.reshape(left.shape)).astype(BF16)
        start += width


def add_rows(parts, after=()):
    rows = parts[0][0].shape[0]
    widths = [left.shape[1] for left, _ in parts]
    tile, total = rows // 2, sum(widths)
    ins = []
    for left, right in parts:
        ins.append((left, (tile, left.shape[1]), lambda j: (j, 0)))
        if right.ndim == 3:
            ins.append((right, (1, tile, right.shape[2]), lambda j: (1, j, 0)))
        else:
            ins.append((right, (tile, right.shape[1]), lambda j: (j, 0)))
    return call(
        functools.partial(add_kernel, widths=widths),
        (2,),
        ins,
        [((rows, total), BF16, (tile, total), lambda j: (j, 0))],
        after=after,
        name="add_rows",
        cost=3,
    )[0]


def split_heads(both, which):
    cuts = range(which, both.shape[1] // HEAD_DIM, 2)
    return jnp.concatenate([both[:, at * HEAD_DIM : (at + 1) * HEAD_DIM] for at in cuts], axis=1)


def behind(value, *others):
    return lax.optimization_barrier((value,) + others)[0]


def shards(
    inputs,
    span_order,
    first_gain,
    query_proj,
    key_matrix,
    value_matrix,
    query_norm,
    key_norm,
    output_proj,
    second_gain,
    gate_proj,
    up_proj,
    down_proj,
    cotangent,
):
    seqs, local, width = inputs.shape
    tokens = seqs * local
    span = local // 2
    shard = query_proj.shape[0]
    head_shard = query_norm.shape[0]
    columns = query_proj.shape[1]
    groups = columns // GROUP
    units = gate_proj.shape[1]
    third = units // 3
    dp_size, tp_size = lax.axis_size("dp"), lax.axis_size("tp")
    ctx, tp_at = lax.axis_index("ctx"), lax.axis_index("tp")
    x_at, core_at = ctx // 2, ctx % 2
    share = lax.axis_index("dp") * 4 + ctx
    half_rows = tokens // 2
    half_seqs = seqs // 2
    pair = tp_size == 2

    def swap(axis, pairs, value, name):
        with jax.named_scope(name):
            return lax.ppermute(value, axis, pairs)

    tp_swap = lambda value, name: swap("tp", TP_SWAP, value, name + "_over_tp")
    core_swap = lambda value, name: swap("ctx", CORE_SWAP, value, name + "_over_core")
    x_swap = lambda value, name: swap("ctx", X_SWAP, value, name + "_over_x")

    def tp_start(part, name):
        if pair:
            return part, tp_swap(part, name)
        return lax.psum(part, "tp"), jnp.zeros_like(part)

    small = [first_gain, second_gain, jnp.pad(query_norm, (0, shard - head_shard))]
    small += [jnp.pad(key_norm, (0, shard - head_shard))]
    small = jnp.pad(jnp.stack(small), ((0, shard - len(small)), (0, BLOCK - shard)))
    shard_one = pack_first(
        query_proj, key_matrix, value_matrix, output_proj, gate_proj, up_proj, down_proj, small, third
    )
    weights = lax.all_gather(shard_one, ("dp", "ctx"), axis=0, tiled=True)

    pairs = span_order.reshape(seqs, 4, 2)
    relative = jnp.stack([ctx, ctx ^ 1, ctx ^ 2, ctx ^ 3])
    orders = jnp.take(pairs, relative, axis=1).reshape(seqs, 8)
    places = (
        orders[:, 0:2, None] * span + jnp.arange(span, dtype=jnp.int32)[None, None, :]
    ).reshape(tokens)
    half_dim = HEAD_DIM // 2
    frequency = ROPE_BASE ** (-(jnp.arange(half_dim, dtype=F32) * (2.0 / HEAD_DIM)))
    angles = places.astype(F32)[:, None] * frequency[None, :]
    cosine, sine = jnp.cos(angles), jnp.sin(angles)
    cosine = jnp.concatenate([cosine, cosine], axis=1)
    sine = jnp.concatenate([-sine, sine], axis=1)
    dps = jnp.arange(dp_size, dtype=jnp.int32)
    other_first = jnp.stack([1 - x_at, x_at])
    cores = jnp.stack([1 - core_at, core_at])
    order = cores[:, None, None] + 2 * other_first[None, :, None] + 4 * dps[None, None, :]
    order = order.reshape(-1).astype(jnp.int32)
    spot = jnp.stack([tp_at, core_at]).astype(jnp.int32)
    input_rows = inputs.reshape(tokens, width)
    cot_rows = cotangent.reshape(tokens, width)
    shard_two = pack_second(gate_proj, up_proj, down_proj, third, after=(shard_one,))

    def turned(left, name, after=()):
        to_core, own = turned_blocks(order, left, after=after)
        return own, core_swap(to_core, name)

    cot_turned = turned(cot_rows, "cotangent", after=(shard_two,))
    weights, cosine, sine, orders, order, spot, cot_turned, shard_two = lax.optimization_barrier(
        (weights, cosine, sine, orders, order, spot, cot_turned, shard_two)
    )

    small = weights[:, 3 * columns + 3 * third :].reshape(-1, shard, BLOCK)[:, 0:4, 0:shard]
    small = jnp.transpose(small, (1, 0, 2)).astype(F32)
    gain_first, gain_second = small[0].reshape(1, width), small[1].reshape(1, width)
    gain_query = small[2, :, 0:head_shard].reshape(1, HEAD_DIM)
    gain_key = small[3, :, 0:head_shard].reshape(1, HEAD_DIM)

    feed_one = norm_rows(input_rows, gain_first)
    kv, raw_kv, latest = [], [], ()
    for h in range(2):
        part = project(
            feed_one, weights, cosine, sine, gain_key, groups, groups, 1, h * half_rows, half_rows, after=latest
        )
        kv.append(part[0])
        raw_kv.append(part[1])
        latest = (part[0],)
        if pair and h == 0:
            half_width = width // 2
            sent = lax.dynamic_slice(
                behind(weights, part[0]), (core_at * half_width, 2 * columns), (half_width, columns)
            )
            output_same = tp_swap(sent, "output_proj")
            latest = (sent,)
    across = [x_swap(kv[0], "kv0")]
    beside = [core_swap(kv[0], "kv0")]
    one_turned = turned(feed_one, "normed_one", after=(kv[1],))
    across.append(x_swap(behind(kv[1], across[0], one_turned[0]), "kv1"))
    beside.append(core_swap(kv[1], "kv1"))
    others = [(beside[0], across[0], core_swap(across[0], "kv0_across"))]
    q, raw_q = project(
        feed_one, weights, cosine, sine, gain_query, groups, 0, 2, 0, tokens,
        after=(one_turned[0], beside[0], across[0], beside[1]),
    )
    found = [attend(orders, q, kv[0], others[0], 0, half_seqs, local)]
    attended = [found[0][0]]
    arrived = behind(across[1], attended[0])
    shard_two = behind(shard_two, arrived)
    others.append((beside[1], arrived, core_swap(arrived, "kv1_across")))
    weights_two = lax.all_gather(shard_two, ("dp", "ctx"), axis=0, tiled=True)

    settled = (attended[0],)
    if pair:
        output_swapped = core_swap(behind(output_same, arrived), "output_proj")
        settled += (output_swapped,)
    found.append(attend(orders, q, kv[1], others[1], half_seqs, half_seqs, local, after=settled))
    attended, probs = [list(parts) for parts in zip(*found)]
    joined = None
    attended_pair = attended, [core_swap(part, "attended") for part in attended]
    if pair:
        other_heads = [tp_swap(part, f"attended{h}") for h, part in enumerate(attended)]
        for h in range(2):
            joined = output_join(
                spot, input_rows, attended[h], other_heads[h], weights, 2,
                output_same, output_swapped, gain_second, h * half_rows, joined,
            )
    else:
        for h in range(2):
            part = nt_product([(attended[h], weights, 2 * columns)], 0, half_rows)
            started = tp_start(part, f"attended{h}")
            joined = join(input_rows, *started, gain_second, h * half_rows, joined)
    middle, feed_two = joined

    cut = width // 4
    tile = min(512, third)

    class Gradient:
        def __init__(self, name, parts, after=()):
            self.name = name
            to_x, self.keep = grad_product(parts, tile, (cut, cut), after=after)
            self.from_x = x_swap(to_x, name)

    def over_dp(name, grads, after=()):
        summed = add_rows([(grad.keep, grad.from_x) for grad in grads], after=after)
        with jax.named_scope(name + "_over_dp"):
            return summed, lax.psum_scatter(summed, "dp", scatter_dimension=0, tiled=True)

    def with_core(values, name):
        return [([value], [core_swap(value, name)]) for value in values]

    names = ("hidden", "gate_back", "up_back")
    starts = [3 * columns + at * third for at in range(3)]
    settled = (*attended_pair[1], one_turned[1])
    two_turned = turned(feed_two, "normed_two", after=settled)
    acts = feed(feed_two, cot_rows, weights, starts, tile, third, 1, after=(two_turned[0],))
    firsts = [([a[0]], [core_swap(a[0], n + "_one")]) for a, n in zip(acts, names)]
    parts = [(cot_turned, firsts[0]), (two_turned, firsts[1]), (two_turned, firsts[2])]
    first_third = Gradient("first_third", parts)
    starts = [at * 2 * third for at in range(3)]
    acts = feed(
        feed_two, cot_rows, weights_two, starts, tile, 2 * third, 1, after=(first_third.keep,)
    )
    seconds = [([a[0]], [core_swap(a[0], n + "_two")]) for a, n in zip(acts, names)]

    def feed_terms(at, kind):
        place = 3 * columns + kind * third
        return [(firsts[at][0][0], weights, place), (seconds[at][0][0], weights_two, 2 * kind * third)]

    back_terms = feed_terms(1, 0) + feed_terms(2, 1)
    back, out_started = [], []
    part = nt_product(back_terms, 0, half_rows)
    back.append(tp_start(part, "back0"))
    down_two = Gradient("down_two", [(cot_turned, seconds[0])], after=(part,))
    landed = (seconds[1][1][0], seconds[2][1][0])
    part = nt_product(back_terms, half_rows, half_rows, after=(down_two.keep, *landed))
    back.append(tp_start(part, "back1"))
    done, first_out = over_dp("first_third", [first_third], after=(part,))
    gate_two = Gradient("gate_two", [(two_turned, seconds[1])], after=(done,))

    def out_half(h, after):
        part = nt_product(feed_terms(0, 2), h * half_rows, half_rows, after=after)
        out_started.append(tp_start(part, f"out{h}"))
        return part

    grads, q_back, k_back, pieces, one = None, None, None, [], []
    sums = {"second": 0.0, "query": 0.0, "key": 0.0, "first": 0.0}

    def middle_half(h, after):
        *found, second = norm_back(
            middle, cot_rows, *back[h], gain_second, h * half_rows, (F32, BF16), grads, after=after
        )
        sums["second"] = sums["second"] + jnp.sum(second, axis=0)
        return found, nn_product(found[1], weights, 2 * columns, columns, h * half_rows, half_rows)

    def attention_half(h, grad_attended, after):
        found, to_own, to_x, to_core, query = attend_back(
            q, kv[h], others[h], probs[h], grad_attended, raw_q, cosine, sine, gain_query,
            h * half_seqs, half_seqs, local, q_back, after=after,
        )
        sums["query"] = sums["query"] + jnp.sum(query, axis=0)
        return found, to_own, to_x, core_swap(to_core, f"kv_grad{h}")

    def send_keys(h, held, after):
        to_own, to_x, from_core = held
        sent = add_rows([(to_x, from_core)], after=after)
        pieces.append((to_own, from_core, x_swap(sent, f"kv_grad{h}")))
        return sent

    def key_half(h, after):
        found, key = key_back(
            *pieces[h], raw_kv[h], cosine, sine, gain_key, h * half_seqs, half_seqs, local,
            tokens, k_back, after=after,
        )
        sums["key"] = sums["key"] + jnp.sum(key, axis=0)
        return found

    def one_half(h, after):
        terms = [(q_back, weights, 0), (k_back, weights, columns)]
        part = nt_product(terms, h * half_rows, half_rows, after=after)
        one.append(tp_start(part, f"one{h}"))
        return part

    grads, grad_attended = middle_half(0, (gate_two.keep,))
    part = out_half(0, (grad_attended,))
    q_back, *held = attention_half(0, grad_attended, (part,))
    grads, grad_attended = middle_half(1, (held[0],))
    grad_middle, middle_low = grads
    low_turned = turned(middle_low, "grad_middle", after=(grad_attended, gate_two.from_x))
    sent = send_keys(0, held, (low_turned[0],))
    done, more_out = over_dp("down_gate_two", [down_two, gate_two], after=(sent, first_out))
    output_grad = Gradient("output", [(low_turned, attended_pair)], after=(done,))
    part = out_half(1, (output_grad.keep,))
    landed = (part, out_started[0][1])
    up_two = Gradient("up_two", [(two_turned, seconds[2])], after=landed)
    k_back = key_half(0, (up_two.keep,))
    part = one_half(0, (output_grad.from_x,))
    q_back, *held = attention_half(1, grad_attended, (part,))
    q_pair = [q_back], [core_swap(q_back, "query_back")]
    outputs = sum_rows(middle, out_started[0], 0, None, after=(held[0],))
    sent = send_keys(1, held, (outputs,))
    outputs = sum_rows(middle, out_started[1], half_rows, outputs, after=(sent,))
    done, up_out = over_dp("up_two_output", [up_two, output_grad], after=(outputs, more_out))
    query_grad = Gradient("query", [(one_turned, q_pair)], after=(done,))
    k_back = key_half(1, (query_grad.keep,))
    part = one_half(1, ())
    k_pair = [k_back], [core_swap(k_back, "key_back")]
    key_grad = Gradient("key", [(one_turned, k_pair)], after=(part,))
    latest = (key_grad.keep,)
    for h in range(2):
        part = gain_terms(input_rows, one[h][0], h * half_rows, after=latest)
        latest = (part,)
        sums["first"] = sums["first"] + jnp.sum(part, axis=0)
    result = None
    for h in range(2):
        result = norm_back(
            input_rows, grad_middle, *one[h], gain_first, h * half_rows, (BF16,), result, after=latest
        )[0:1]
        latest = ()
    done, heads_out = over_dp("query_key", [query_grad, key_grad], after=(result[0],))

    if not pair:
        sums["first"], sums["second"] = sums["first"] / tp_size, sums["second"] / tp_size
    totals = jnp.concatenate([sums[name] for name in ("first", "second", "query", "key")])
    totals = lax.psum(behind(totals, done), ("dp", "ctx", "tp"))
    cut_total = lambda start, size: lax.dynamic_slice(totals, (start + share * size,), (size,))

    grad_kv = heads_out[:, columns:].astype(F32)
    down_out, gate_out, up_first = [first_out[:, at * third : (at + 1) * third] for at in range(3)]
    beside = lambda left, right: jnp.concatenate([left, right], axis=1).astype(F32)
    return (
        outputs.reshape(inputs.shape),
        result[0].reshape(inputs.shape),
        cut_total(0, shard),
        heads_out[:, 0:columns].astype(F32),
        split_heads(grad_kv, 0),
        split_heads(grad_kv, 1),
        cut_total(2 * width, head_shard),
        cut_total(2 * width + HEAD_DIM, head_shard),
        up_out[:, 2 * third :].astype(F32).T,
        cut_total(width, shard),
        beside(gate_out, more_out[:, 2 * third :]),
        beside(up_first, up_out[:, 0 : 2 * third]),
        beside(down_out, more_out[:, 0 : 2 * third]).T,
    )


def solution(mesh):
    rows = P(("dp", "ctx"))
    columns = P(("dp", "ctx"), "tp")
    turned = P("tp", ("dp", "ctx"))
    tokens = P("dp", "ctx", None)
    in_specs = (
        (tokens, P("dp", None), rows, columns, columns, columns, rows, rows, turned, rows)
        + (columns, columns, turned, tokens)
    )
    out_specs = (
        (tokens, tokens, rows, columns, columns, columns, rows, rows, turned, rows)
        + (columns, columns, turned)
    )
    return jax.shard_map(shards, mesh=mesh, in_specs=in_specs, out_specs=out_specs, check_vma=False)
```

```python
import functools

import jax
import jax.numpy as jnp
from jax import lax
from jax.experimental import pallas as pl
from jax.experimental.pallas import tpu as pltpu
from jax.sharding import PartitionSpec as P

HEAD_DIM = 128
GROUP = 2 * HEAD_DIM
BLOCK = 128
EPSILON = 1e-06
ROPE_BASE = 1000000.0
MASKED = -1e30
VMEM_LIMIT = 56 * 1024 * 1024
F32 = jnp.float32
BF16 = jnp.bfloat16
FLOPS_PER_US = 1e10

CORE_SWAP = [(0, 1), (1, 0), (2, 3), (3, 2)]
X_SWAP = [(0, 2), (2, 0), (1, 3), (3, 1)]
TP_SWAP = [(0, 1), (1, 0)]


def nn(left, right):
    return lax.dot_general(left, right, (((1,), (0,)), ((), ())), preferred_element_type=F32)


def nt(left, right):
    return lax.dot_general(left, right, (((1,), (1,)), ((), ())), preferred_element_type=F32)


def tn(left, right):
    return lax.dot_general(left, right, (((0,), (0,)), ((), ())), preferred_element_type=F32)


def unit_norm(values):
    inverse = lax.rsqrt(jnp.mean(values * values, axis=-1, keepdims=True) + EPSILON)
    return values * inverse, inverse


def swap_halves(values):
    return pltpu.roll(values, HEAD_DIM // 2, 1)


def call(kernel, grid, ins, outs, scratch=(), scalars=(), alias=None, after=(), name=None, cost=1.0):
    any_space = pl.BlockSpec(memory_space=pl.ANY)
    specs = [any_space if b is None else pl.BlockSpec(b, m) for _, b, m in ins]
    n_in, n_after, n_scalar = len(ins), len(after), len(scalars)

    def body(*refs):
        keep = refs[: n_scalar + n_in] + refs[n_scalar + n_in + n_after :]
        kernel(*keep)

    return pl.pallas_call(
        body,
        grid_spec=pltpu.PrefetchScalarGridSpec(
            num_scalar_prefetch=n_scalar,
            grid=grid,
            in_specs=specs + [any_space] * n_after,
            out_specs=[pl.BlockSpec(b, m) for _, _, b, m in outs],
            scratch_shapes=list(scratch),
        ),
        out_shape=[jax.ShapeDtypeStruct(s, d) for s, d, _, _ in outs],
        input_output_aliases={n_scalar + i: o for o, i in (alias or {}).items()},
        compiler_params=pltpu.CompilerParams(
            dimension_semantics=("arbitrary",) * len(grid), vmem_limit_bytes=VMEM_LIMIT
        ),
        cost_estimate=pl.CostEstimate(
            flops=int(cost * FLOPS_PER_US), bytes_accessed=0, transcendentals=0
        ),
        name=name,
    )(*scalars, *[a for a, _, _ in ins], *after)


def pack_first_kernel(q_ref, k_ref, v_ref, o_ref, g_ref, u_ref, d_ref, small_ref, out_ref):
    columns, third = q_ref.shape[1], g_ref.shape[1]
    out_ref[:, 0:columns] = q_ref[...]
    for at in range(columns // GROUP):
        cut = slice(at * HEAD_DIM, (at + 1) * HEAD_DIM)
        start = columns + at * GROUP
        out_ref[:, start : start + HEAD_DIM] = k_ref[:, cut]
        out_ref[:, start + HEAD_DIM : start + GROUP] = v_ref[:, cut]
    out_ref[:, 2 * columns : 3 * columns] = o_ref[...].T
    start = 3 * columns
    out_ref[:, start : start + third] = g_ref[...]
    out_ref[:, start + third : start + 2 * third] = u_ref[...]
    out_ref[:, start + 2 * third : start + 3 * third] = d_ref[...].T
    out_ref[:, start + 3 * third :] = small_ref[...]


def pack_first(q, k, v, o, g, u, d, small, third):
    shard, columns = q.shape
    whole = lambda array: (array, array.shape, lambda j: (0, 0))
    total = 3 * columns + 3 * third + BLOCK
    return call(
        pack_first_kernel,
        (1,),
        [whole(q), whole(k), whole(v), whole(o)]
        + [(g, (shard, third), lambda j: (0, 0)), (u, (shard, third), lambda j: (0, 0))]
        + [(d, (third, shard), lambda j: (0, 0)), whole(small)],
        [((shard, total), BF16, (shard, total), lambda j: (0, 0))],
        name="pack_first",
        cost=3,
    )[0]


def pack_second_kernel(g_ref, u_ref, d_ref, out_ref):
    step = pl.program_id(0)
    part = step // 2

    @pl.when(part == 0)
    def _():
        out_ref[...] = g_ref[...]

    @pl.when(part == 1)
    def _():
        out_ref[...] = u_ref[...]

    @pl.when(part == 2)
    def _():
        out_ref[...] = d_ref[...].T


def pack_second(g, u, d, third, after=()):
    shard = g.shape[0]
    return call(
        pack_second_kernel,
        (6,),
        [(g, (shard, third), lambda j: (0, 1 + j % 2)), (u, (shard, third), lambda j: (0, 1 + j % 2))]
        + [(d, (third, shard), lambda j: (1 + j % 2, 0))],
        [((shard, 6 * third), BF16, (shard, third), lambda j: (0, j))],
        after=after,
        name="pack_second",
        cost=5,
    )[0]


def norm_kernel(x_ref, gain_ref, out_ref):
    out_ref[...] = (unit_norm(x_ref[...].astype(F32))[0] * gain_ref[...]).astype(BF16)


def norm_rows(x, gain, after=()):
    tokens, width = x.shape
    tile = min(256, tokens)
    block = (tile, width)
    return call(
        norm_kernel,
        (tokens // tile,),
        [(x, block, lambda j: (j, 0)), (gain, (1, width), lambda j: (0, 0))],
        [((tokens, width), BF16, block, lambda j: (j, 0))],
        after=after,
        name="norm_rows",
        cost=5,
    )[0]


def project_kernel(x_ref, w_ref, cos_ref, sin_ref, gain_ref, out_ref, raw_ref, *, turned, rows):
    for at in range(0, x_ref.shape[0], rows):
        part = pl.ds(at, rows)
        raw = nn(x_ref[part, :], w_ref[...])
        raw_ref[part, :] = raw
        cosine, sine = cos_ref[part, :], sin_ref[part, :]
        for head in range(2):
            values = raw[:, head * HEAD_DIM : (head + 1) * HEAD_DIM]
            if head < turned:
                scaled = unit_norm(values)[0] * gain_ref[...]
                values = scaled * cosine + swap_halves(scaled) * sine
            out_ref[part, head * HEAD_DIM : (head + 1) * HEAD_DIM] = values.astype(BF16)


def project(x, weights, cosine, sine, gain, groups, first, turned, row, rows, after=()):
    width = x.shape[1]
    some = lambda j: (row // rows, 0)
    column = lambda j: (0, j)
    columns = groups * GROUP
    return call(
        functools.partial(project_kernel, turned=turned, rows=min(256, rows)),
        (groups,),
        [
            (x, (rows, width), some),
            (weights, (width, GROUP), lambda j: (0, first + j)),
            (cosine, (rows, HEAD_DIM), some),
            (sine, (rows, HEAD_DIM), some),
            (gain, (1, HEAD_DIM), lambda j: (0, 0)),
        ],
        [
            ((rows, columns), BF16, (rows, GROUP), column),
            ((rows, columns), F32, (rows, GROUP), column),
        ],
        after=after,
        name="project",
        cost=10,
    )


def span_places(orders_ref, seq, piece, span, shape, dim):
    index = lax.broadcasted_iota(jnp.int32, shape, dim)
    first, second = orders_ref[seq, 2 * piece], orders_ref[seq, 2 * piece + 1]
    return jnp.where(index < span, first * span + index, second * span + index - span)


def stacked_heads(block):
    return jnp.concatenate([block[:, 0:HEAD_DIM], block[:, HEAD_DIM:GROUP]], axis=0)


def masked_exponents(orders_ref, seq, query, pieces, span):
    rows, keys = query.shape[0], pieces[0].shape[0]
    scale = HEAD_DIM**-0.5
    places = span_places(orders_ref, seq, 0, span, (rows // 2, 1), 0)
    places = jnp.concatenate([places, places], axis=0)
    scores = []
    for at, piece in enumerate(pieces):
        key_places = span_places(orders_ref, seq, at, span, (1, keys), 1)
        product = nt(query, piece[:, 0:HEAD_DIM]) * scale
        scores.append(jnp.where(key_places <= places, product, MASKED))
    peak = functools.reduce(jnp.maximum, [jnp.max(s, axis=1, keepdims=True) for s in scores])
    exponents = [jnp.exp(s - peak) for s in scores]
    total = functools.reduce(jnp.add, [jnp.sum(e, axis=1, keepdims=True) for e in exponents])
    return exponents, 1.0 / total


def attend_kernel(orders_ref, q_ref, own_ref, core_ref, x_ref, diag_ref, out_ref, prob_ref, *, first, span):
    seq = pl.program_id(0) + first
    local = q_ref.shape[0]
    for group in range(q_ref.shape[1] // GROUP):
        columns = slice(group * GROUP, (group + 1) * GROUP)
        rows = slice(group * 2 * local, (group + 1) * 2 * local)
        query = stacked_heads(q_ref[:, columns])
        pieces = [ref[:, columns] for ref in (own_ref, core_ref, x_ref, diag_ref)]
        exponents, inverse = masked_exponents(orders_ref, seq, query, pieces, span)
        total = None
        for at, (exponent, piece) in enumerate(zip(exponents, pieces)):
            prob = (exponent * inverse).astype(BF16)
            prob_ref[0, rows, at * local : (at + 1) * local] = prob
            product = nn(prob, piece[:, HEAD_DIM:GROUP])
            total = product if total is None else total + product
        result = total.astype(BF16)
        for head in range(2):
            start = group * GROUP + head * HEAD_DIM
            out_ref[:, start : start + HEAD_DIM] = result[head * local : (head + 1) * local]


def attend(orders, q, kv, others, first, count, local, after=()):
    columns = q.shape[1]
    block = (local, columns)
    at_whole = lambda s, o: (s + first, 0)
    at_half = lambda s, o: (s, 0)
    ins = [(q, block, at_whole), (kv, block, at_half)] + [(k, block, at_half) for k in others]
    prob = (1, columns // GROUP * 2 * local, 4 * local)
    return call(
        functools.partial(attend_kernel, first=first, span=local // 2),
        (count,),
        ins,
        [
            ((count * local, columns), BF16, block, at_half),
            ((count,) + prob[1:], BF16, prob, lambda s, o: (s, 0, 0)),
        ],
        scalars=(orders,),
        after=after,
        name="attend",
        cost=11,
    )


def turn_back(grad, raw, cosine, sine, gain):
    turned = grad * cosine - swap_halves(grad) * sine
    unit, inverse = unit_norm(raw)
    grad_normed = turned * gain
    mean = jnp.mean(grad_normed * unit, axis=-1, keepdims=True)
    terms = jnp.sum((turned * unit).reshape(-1, 8, HEAD_DIM), axis=0)
    return (inverse * (grad_normed - unit * mean)).astype(BF16), terms


def clear_at_start(ref, dims):
    start = functools.reduce(jnp.logical_and, [pl.program_id(d) == 0 for d in range(dims)])

    @pl.when(start)
    def _():
        ref[...] = jnp.zeros_like(ref)


def attend_back_kernel(
    q_ref, own_ref, core_ref, x_ref, diag_ref, prob_ref, grad_ref, raw_ref, cos_ref, sin_ref, gain_ref, *rest
):
    q_back_ref, own_out, x_out, core_out, gain_out = rest[-5:]
    clear_at_start(gain_out, 1)
    scale = HEAD_DIM**-0.5
    local = q_ref.shape[0]
    outs = (own_out, core_out.at[0], x_out, core_out.at[1])
    for group in range(q_ref.shape[1] // GROUP):
        start = group * GROUP
        both = slice(start, start + GROUP)
        rows = slice(group * 2 * local, (group + 1) * 2 * local)
        query = stacked_heads(q_ref[:, both])
        grad = stacked_heads(grad_ref[:, both])
        pieces = [ref[:, both] for ref in (own_ref, core_ref, x_ref, diag_ref)]
        lows = [prob_ref[0, rows, at * local : (at + 1) * local] for at in range(4)]
        products = [low.astype(F32) * nt(grad, p[:, HEAD_DIM:GROUP]) for low, p in zip(lows, pieces)]
        delta = functools.reduce(jnp.add, [jnp.sum(p, axis=1, keepdims=True) for p in products])
        grad_scores = [(p - low.astype(F32) * delta).astype(BF16) for p, low in zip(products, lows)]
        grad_query = functools.reduce(
            jnp.add, [nn(s, p[:, 0:HEAD_DIM]) for s, p in zip(grad_scores, pieces)]
        )
        for out, scores, low in zip(outs, grad_scores, lows):
            out[:, start : start + HEAD_DIM] = (tn(scores, query) * scale).astype(BF16)
            out[:, start + HEAD_DIM : start + GROUP] = tn(low, grad).astype(BF16)
        for head in range(2):
            columns = slice(start + head * HEAD_DIM, start + (head + 1) * HEAD_DIM)
            result, terms = turn_back(
                grad_query[head * local : (head + 1) * local] * scale,
                raw_ref[:, columns],
                cos_ref[...],
                sin_ref[...],
                gain_ref[...],
            )
            q_back_ref[:, columns] = result
            gain_out[...] += terms


def attend_back(q, kv, others, prob, grad, raw, cosine, sine, gain, first, count, local, into, after=()):
    columns = q.shape[1]
    block = (local, columns)
    at_whole = lambda s: (s + first, 0)
    at_half = lambda s: (s, 0)
    fixed = lambda s: (0, 0)
    ins = [(q, block, at_whole), (kv, block, at_half)] + [(k, block, at_half) for k in others]
    ins += [(prob, (1,) + prob.shape[1:], lambda s: (s, 0, 0))]
    ins += [(grad, block, at_half), (raw, block, at_whole)]
    ins += [(cosine, (local, HEAD_DIM), at_whole), (sine, (local, HEAD_DIM), at_whole)]
    ins += [(gain, (1, HEAD_DIM), fixed)]
    if into is not None:
        ins.append((into, None, None))
    piece = ((count * local, columns), BF16, block, at_half)
    return call(
        attend_back_kernel,
        (count,),
        ins,
        [(q.shape, BF16, block, at_whole)]
        + [piece] * 2
        + [((2, count * local, columns), BF16, (2, local, columns), lambda s: (0, s, 0))]
        + [((8, HEAD_DIM), F32, (8, HEAD_DIM), fixed)],
        alias=None if into is None else {0: len(ins) - 1},
        after=after,
        name="attend_back",
        cost=25,
    )


def key_back_kernel(mine_ref, core_ref, x_ref, raw_ref, cos_ref, sin_ref, gain_ref, *rest):
    out_ref, gain_out = rest[-2:]
    clear_at_start(gain_out, 1)
    for group in range(mine_ref.shape[1] // GROUP):
        start = group * GROUP
        both = slice(start, start + GROUP)
        parts = [ref[:, both].astype(F32) for ref in (mine_ref, core_ref.at[0], x_ref)]
        grad = functools.reduce(jnp.add, parts)
        result, terms = turn_back(
            grad[:, 0:HEAD_DIM],
            raw_ref[:, start : start + HEAD_DIM],
            cos_ref[...],
            sin_ref[...],
            gain_ref[...],
        )
        out_ref[:, start : start + HEAD_DIM] = result
        out_ref[:, start + HEAD_DIM : start + GROUP] = grad[:, HEAD_DIM:GROUP].astype(BF16)
        gain_out[...] += terms


def key_back(mine, core, x, raw, cosine, sine, gain, first, count, local, tokens, into, after=()):
    columns = mine.shape[1]
    block = (local, columns)
    at_whole = lambda s: (s + first, 0)
    at_half = lambda s: (s, 0)
    fixed = lambda s: (0, 0)
    ins = [(mine, block, at_half), (core, (1,) + block, lambda s: (0, s, 0)), (x, block, at_half)]
    ins += [(raw, block, at_half)]
    ins += [(cosine, (local, HEAD_DIM), at_whole), (sine, (local, HEAD_DIM), at_whole)]
    ins += [(gain, (1, HEAD_DIM), fixed)]
    if into is not None:
        ins.append((into, None, None))
    return call(
        key_back_kernel,
        (count,),
        ins,
        [
            ((tokens, columns), BF16, block, at_whole),
            ((8, HEAD_DIM), F32, (8, HEAD_DIM), fixed),
        ],
        alias=None if into is None else {0: len(ins) - 1},
        after=after,
        name="key_back",
        cost=5,
    )


def feed_kernel(x_ref, c_ref, g_ref, u_ref, d_ref, *outs, rows, steps):
    step, pieces = pl.program_id(0), len(outs) // 3

    def fill(hidden_ref, gate_ref, up_ref):
        for at in range(0, x_ref.shape[0], rows):
            part = pl.ds(at, rows)
            gate = nn(x_ref[part, :], g_ref[...])
            upward = nn(x_ref[part, :], u_ref[...])
            grad = nn(c_ref[part, :], d_ref[...])
            sigmoid = jax.nn.sigmoid(gate)
            silu = gate * sigmoid
            hidden_ref[part, :] = (silu * upward).astype(BF16)
            slope = sigmoid + silu * (1.0 - sigmoid)
            gate_ref[part, :] = (grad * upward * slope).astype(BF16)
            up_ref[part, :] = (grad * silu).astype(BF16)

    for piece in range(pieces):
        run = functools.partial(fill, *outs[piece::pieces])
        if pieces == 1:
            run()
        else:
            pl.when(step // steps == piece)(run)


def feed(x, c, weights, starts, tile, piece, pieces, after=()):
    tokens, width = x.shape
    steps = piece // tile
    whole = lambda j: (0, 0)
    ins = [(x, (tokens, width), whole), (c, (tokens, width), whole)]
    for start in starts:
        ins.append((weights, (width, tile), lambda j, start=start: (0, start // tile + j)))
    outs = [
        ((tokens, piece), BF16, (tokens, tile), lambda j, at=at: (0, jnp.clip(j - at * steps, 0, steps - 1)))
        for _ in range(3)
        for at in range(pieces)
    ]
    found = call(
        functools.partial(feed_kernel, rows=min(256, tokens), steps=steps),
        (steps * pieces,),
        ins,
        outs,
        after=after,
        name="feed",
        cost=2 + piece * pieces * 0.0165,
    )
    return [found[kind * pieces : (kind + 1) * pieces] for kind in range(3)]


def nt_kernel(*refs, count):
    out_ref = refs[-1]
    total = None
    for left_ref, w_ref in zip(refs[:count], refs[count : 2 * count]):
        product = nt(left_ref[...], w_ref[...])
        total = product if total is None else total + product
    out_ref[...] = total.astype(out_ref.dtype)


def nt_product(terms, row, rows, after=()):
    width = terms[0][1].shape[0]
    tile = min(512, width)
    ins = [(left, (rows, left.shape[1]), lambda j: (row // rows, 0)) for left, _, _ in terms]
    ins += [
        (weights, (tile, left.shape[1]), lambda j, at=at // left.shape[1]: (j, at))
        for left, weights, at in terms
    ]
    return call(
        functools.partial(nt_kernel, count=len(terms)),
        (width // tile,),
        ins,
        [((rows, width), BF16, (rows, tile), lambda j: (0, j))],
        after=after,
        name="nt_product",
        cost=1.5 + rows * sum(left.shape[1] for left, _, _ in terms) * 6.0e-6,
    )[0]


def nn_kernel(x_ref, w_ref, out_ref):
    out_ref[...] = nn(x_ref[...], w_ref[...]).astype(out_ref.dtype)


def nn_product(left, weights, first_column, columns, row, rows, after=()):
    width = weights.shape[0]
    tile = min(512, columns)
    return call(
        nn_kernel,
        (columns // tile,),
        [
            (left, (rows, width), lambda j: (row // rows, 0)),
            (weights, (width, tile), lambda j: (0, first_column // tile + j)),
        ],
        [((rows, columns), BF16, (rows, tile), lambda j: (0, j))],
        after=after,
        name="nn_product",
        cost=6,
    )[0]


def output_join_kernel(
    at_ref, x_ref, mine_ref, other_ref, w_mine_ref, w_same_ref, w_swap_ref, gain_ref, *rest, steps
):
    middle_ref, normed_ref, rows_ref = rest[-3:]
    step = pl.program_id(0)
    tile = x_ref.shape[1]
    is_first, core = at_ref[0] == 0, at_ref[1]
    direct = (step * 2 // steps) == core
    mine, other, w_mine = mine_ref[...], other_ref[...], w_mine_ref[...]
    w_other = jnp.where(direct, w_same_ref[...], w_swap_ref[...])
    total = nt(jnp.where(is_first, mine, other), jnp.where(is_first, w_mine, w_other))
    total += nt(jnp.where(is_first, other, mine), jnp.where(is_first, w_other, w_mine))
    columns = pl.ds(pl.multiple_of(step * tile, tile), tile)
    rows_ref[:, columns] = x_ref[...].astype(F32) + total

    @pl.when(step == steps - 1)
    def _():
        middle = rows_ref[...]
        middle_ref[...] = middle
        normed_ref[...] = (unit_norm(middle)[0] * gain_ref[...]).astype(BF16)


def output_join(at, x, mine, other, weights, block, same, swapped, gain, row, into, after=()):
    tokens, width = x.shape
    rows, columns = mine.shape
    tile = min(512, width // 2)
    steps = width // tile
    fixed = lambda j, a: (0, 0)
    fetched = lambda j, a: (j % (steps // 2), 0)
    ins = [
        (x, (rows, tile), lambda j, a: (row // rows, j)),
        (mine, (rows, columns), fixed),
        (other, (rows, columns), fixed),
        (weights, (tile, columns), lambda j, a: (j, block)),
        (same, (tile, columns), fetched),
        (swapped, (tile, columns), fetched),
        (gain, (1, width), fixed),
    ]
    alias = None
    if into is not None:
        alias = {o: len(ins) + o for o in range(2)}
        ins += [(array, None, None) for array in into]
    out = lambda kind: ((tokens, width), kind, (rows, width), lambda j, a: (row // rows, 0))
    return call(
        functools.partial(output_join_kernel, steps=steps),
        (steps,),
        ins,
        [out(F32), out(BF16)],
        scratch=[pltpu.VMEM((rows, width), F32)],
        scalars=(at,),
        alias=alias,
        after=after,
        name="output_join",
        cost=15,
    )


def turn_kernel(order_ref, *refs):
    ins, outs = refs[:4], refs[4:]
    step = pl.program_id(0)

    def fill(out_ref):
        for at, ref in enumerate(ins):
            out_ref[at * BLOCK : (at + 1) * BLOCK, :] = ref[...].T

    pl.when(step < 2)(lambda: fill(outs[0]))
    pl.when(step >= 2)(lambda: fill(outs[1]))


def turned_blocks(order, left, after=()):
    tokens, width = left.shape
    ins = [(left, (tokens, BLOCK), lambda j, o, at=at: (0, o[4 * j + at])) for at in range(4)]
    out = lambda spot: ((width // 2, tokens), BF16, (4 * BLOCK, tokens), spot)
    return call(
        turn_kernel,
        (width // BLOCK // 4,),
        ins,
        [out(lambda j, o: (jnp.minimum(j, 1), 0)), out(lambda j, o: (jnp.maximum(j - 2, 0), 0))],
        scalars=(order,),
        after=after,
        name="turned_blocks",
        cost=6,
    )


def grad_kernel(*refs, plan, outs):
    step, begin, used = pl.program_id(0), 0, 0
    out_refs = refs[-outs:]

    def fill(left_refs, right_refs):
        for at, out in enumerate(out_refs):
            size, total = out.shape[0], None
            rows = pl.ds(at * size, size)
            for left_ref, pieces in zip(left_refs, right_refs):
                start = 0
                for piece in pieces:
                    tokens = piece.shape[0]
                    product = nn(left_ref[rows, start : start + tokens], piece[...])
                    total = product if total is None else total + product
                    start += tokens
            out[...] = total.astype(BF16)

    for pieces, count in plan:
        part = refs[used : used + 2 + 2 * pieces]
        run = functools.partial(fill, part[:2], (part[2 : 2 + pieces], part[2 + pieces :]))
        if len(plan) == 1:
            run()
        else:
            pl.when((step >= begin) & (step < begin + count))(run)
        begin, used = begin + count, used + 2 + 2 * pieces


def grad_product(parts, tile, cuts, after=()):
    width, tokens = parts[0][0][0].shape
    ins, begin, plan = [], 0, []
    for lefts, rights in parts:
        count = rights[0][0].shape[1] // tile
        ins += [(left, left.shape, lambda j: (0, 0)) for left in lefts]
        spot = lambda j, begin=begin, count=count: (0, jnp.clip(j - begin, 0, count - 1))
        ins += [(piece, (piece.shape[0], tile), spot) for pieces in rights for piece in pieces]
        plan.append((len(rights[0]), count))
        begin += count
    return call(
        functools.partial(grad_kernel, plan=plan, outs=len(cuts)),
        (begin,),
        ins,
        [((cut, begin * tile), BF16, (cut, tile), lambda j: (0, j)) for cut in cuts],
        after=after,
        name="grad_product",
        cost=3.5 + begin * tile * 0.0047,
    )


def join_kernel(x_ref, own_ref, other_ref, gain_ref, *rest):
    middle_ref, normed_ref = rest[-2:]
    middle = x_ref[...].astype(F32) + (own_ref[...].astype(F32) + other_ref[...].astype(F32))
    middle_ref[...] = middle
    normed_ref[...] = (unit_norm(middle)[0] * gain_ref[...]).astype(BF16)


def join(x, own, other, gain, row, into, after=()):
    tokens, width = x.shape
    rows = own.shape[0]
    tile = min(256, rows)
    block = (tile, width)
    at_whole = lambda j: (row // tile + j, 0)
    at_half = lambda j: (j, 0)
    ins = [(x, block, at_whole), (own, block, at_half), (other, block, at_half)]
    ins += [(gain, (1, width), lambda j: (0, 0))]
    alias = None
    if into is not None:
        alias = {o: len(ins) + o for o in range(2)}
        ins += [(array, None, None) for array in into]
    return call(
        join_kernel,
        (rows // tile,),
        ins,
        [((tokens, width), F32, block, at_whole), ((tokens, width), BF16, block, at_whole)],
        alias=alias,
        after=after,
        name="join",
        cost=7.5,
    )


def norm_back_kernel(v_ref, base_ref, own_ref, other_ref, gain_ref, *rest, outs):
    out_refs, terms_ref = rest[-outs - 1 : -1], rest[-1]
    clear_at_start(terms_ref, 1)
    own = own_ref[...].astype(F32)
    unit, inverse = unit_norm(v_ref[...].astype(F32))
    grad_normed = (own + other_ref[...].astype(F32)) * gain_ref[...]
    mean = jnp.mean(grad_normed * unit, axis=-1, keepdims=True)
    result = base_ref[...].astype(F32) + inverse * (grad_normed - unit * mean)
    for ref in out_refs:
        ref[...] = result.astype(ref.dtype)
    terms_ref[...] += jnp.sum((own * unit).reshape(-1, 8, own.shape[1]), axis=0)


def norm_back(values, base, own, other, gain, row, types, into, after=(), cost=7.5):
    tokens, width = values.shape
    rows = own.shape[0]
    tile = min(256, rows)
    block = (tile, width)
    at_whole = lambda j: (row // tile + j, 0)
    at_half = lambda j: (j, 0)
    fixed = lambda j: (0, 0)
    ins = [(values, block, at_whole), (base, block, at_whole)]
    ins += [(own, block, at_half), (other, block, at_half), (gain, (1, width), fixed)]
    alias = None
    if into is not None:
        alias = {o: len(ins) + o for o in range(len(types))}
        ins += [(array, None, None) for array in into]
    return call(
        functools.partial(norm_back_kernel, outs=len(types)),
        (rows // tile,),
        ins,
        [((tokens, width), kind, block, at_whole) for kind in types]
        + [((8, width), F32, (8, width), fixed)],
        alias=alias,
        after=after,
        name="norm_back",
        cost=cost,
    )


def sum_kernel(*refs):
    own, other = refs[1][...].astype(F32), refs[2][...].astype(F32)
    refs[-1][...] = (refs[0][...] + (own + other)).astype(BF16)


def sum_rows(values, parts, row, into, after=()):
    tokens, width = values.shape
    rows = parts[0].shape[0]
    tile = min(256, rows)
    block = (tile, width)
    at_whole = lambda j: (row // tile + j, 0)
    ins = [(values, block, at_whole)] + [(part, block, lambda j: (j, 0)) for part in parts]
    if into is not None:
        ins.append((into, None, None))
    return call(
        sum_kernel,
        (rows // tile,),
        ins,
        [((tokens, width), BF16, block, at_whole)],
        alias=None if into is None else {0: len(ins) - 1},
        after=after,
        name="sum_rows",
        cost=6,
    )[0]


def terms_kernel(v_ref, own_ref, terms_ref):
    clear_at_start(terms_ref, 1)
    unit = unit_norm(v_ref[...].astype(F32))[0]
    terms_ref[...] += jnp.sum((own_ref[...].astype(F32) * unit).reshape(-1, 8, unit.shape[1]), axis=0)


def gain_terms(values, own, row, after=()):
    width = values.shape[1]
    rows = own.shape[0]
    tile = min(256, rows)
    return call(
        terms_kernel,
        (rows // tile,),
        [
            (values, (tile, width), lambda j: (row // tile + j, 0)),
            (own, (tile, width), lambda j: (j, 0)),
        ],
        [((8, width), F32, (8, width), lambda j: (0, 0))],
        after=after,
        name="gain_terms",
        cost=4,
    )[0]


def add_kernel(*refs, widths):
    start = 0
    for at, width in enumerate(widths):
        left, right = refs[2 * at][...].astype(F32), refs[2 * at + 1][...].astype(F32)
        refs[-1][:, start : start + width] = (left + right.reshape(left.shape)).astype(BF16)
        start += width


def add_rows(parts, after=()):
    rows = parts[0][0].shape[0]
    widths = [left.shape[1] for left, _ in parts]
    tile, total = rows // 2, sum(widths)
    ins = []
    for left, right in parts:
        ins.append((left, (tile, left.shape[1]), lambda j: (j, 0)))
        if right.ndim == 3:
            ins.append((right, (1, tile, right.shape[2]), lambda j: (1, j, 0)))
        else:
            ins.append((right, (tile, right.shape[1]), lambda j: (j, 0)))
    return call(
        functools.partial(add_kernel, widths=widths),
        (2,),
        ins,
        [((rows, total), BF16, (tile, total), lambda j: (j, 0))],
        after=after,
        name="add_rows",
        cost=3,
    )[0]


def split_heads(both, which):
    cuts = range(which, both.shape[1] // HEAD_DIM, 2)
    return jnp.concatenate([both[:, at * HEAD_DIM : (at + 1) * HEAD_DIM] for at in cuts], axis=1)


def behind(value, *others):
    return lax.optimization_barrier((value,) + others)[0]


def shards(
    inputs,
    span_order,
    first_gain,
    query_proj,
    key_matrix,
    value_matrix,
    query_norm,
    key_norm,
    output_proj,
    second_gain,
    gate_proj,
    up_proj,
    down_proj,
    cotangent,
):
    seqs, local, width = inputs.shape
    tokens = seqs * local
    span = local // 2
    shard = query_proj.shape[0]
    head_shard = query_norm.shape[0]
    columns = query_proj.shape[1]
    groups = columns // GROUP
    units = gate_proj.shape[1]
    third = units // 3
    dp_size, tp_size = lax.axis_size("dp"), lax.axis_size("tp")
    ctx, tp_at = lax.axis_index("ctx"), lax.axis_index("tp")
    x_at, core_at = ctx // 2, ctx % 2
    half_rows = tokens // 2
    half_seqs = seqs // 2
    pair = tp_size == 2

    def swap(axis, pairs, value, name):
        with jax.named_scope(name):
            return lax.ppermute(value, axis, pairs)

    tp_swap = lambda value, name: swap("tp", TP_SWAP, value, name + "_over_tp")
    core_swap = lambda value, name: swap("ctx", CORE_SWAP, value, name + "_over_core")
    x_swap = lambda value, name: swap("ctx", X_SWAP, value, name + "_over_x")

    def tp_start(part, name):
        if pair:
            return part, tp_swap(part, name)
        return lax.psum(part, "tp"), jnp.zeros_like(part)

    small = [first_gain, second_gain, jnp.pad(query_norm, (0, shard - head_shard))]
    small += [jnp.pad(key_norm, (0, shard - head_shard))]
    small = jnp.pad(jnp.stack(small), ((0, shard - len(small)), (0, BLOCK - shard)))
    shard_one = pack_first(
        query_proj, key_matrix, value_matrix, output_proj, gate_proj, up_proj, down_proj, small, third
    )
    weights = lax.all_gather(shard_one, ("dp", "ctx"), axis=0, tiled=True)

    pairs = span_order.reshape(seqs, 4, 2)
    relative = jnp.stack([ctx, ctx ^ 1, ctx ^ 2, ctx ^ 3])
    orders = jnp.take(pairs, relative, axis=1).reshape(seqs, 8)
    places = (
        orders[:, 0:2, None] * span + jnp.arange(span, dtype=jnp.int32)[None, None, :]
    ).reshape(tokens)
    half_dim = HEAD_DIM // 2
    frequency = ROPE_BASE ** (-(jnp.arange(half_dim, dtype=F32) * (2.0 / HEAD_DIM)))
    angles = places.astype(F32)[:, None] * frequency[None, :]
    cosine, sine = jnp.cos(angles), jnp.sin(angles)
    cosine = jnp.concatenate([cosine, cosine], axis=1)
    sine = jnp.concatenate([-sine, sine], axis=1)
    dps = jnp.arange(dp_size, dtype=jnp.int32)
    other_first = jnp.stack([1 - x_at, x_at])
    cores = jnp.stack([1 - core_at, core_at])
    order = cores[:, None, None] + 2 * other_first[None, :, None] + 4 * dps[None, None, :]
    order = order.reshape(-1).astype(jnp.int32)
    spot = jnp.stack([tp_at, core_at]).astype(jnp.int32)
    input_rows = inputs.reshape(tokens, width)
    cot_rows = cotangent.reshape(tokens, width)
    shard_two = pack_second(gate_proj, up_proj, down_proj, third, after=(shard_one,))

    def turned(left, name, after=()):
        to_core, own = turned_blocks(order, left, after=after)
        return own, core_swap(to_core, name)

    cot_turned = turned(cot_rows, "cotangent", after=(shard_two,))
    weights, cosine, sine, orders, order, spot, cot_turned, shard_two = lax.optimization_barrier(
        (weights, cosine, sine, orders, order, spot, cot_turned, shard_two)
    )

    small = weights[:, 3 * columns + 3 * third :].reshape(-1, shard, BLOCK)[:, 0:4, 0:shard]
    small = jnp.transpose(small, (1, 0, 2)).astype(F32)
    gain_first, gain_second = small[0].reshape(1, width), small[1].reshape(1, width)
    gain_query = small[2, :, 0:head_shard].reshape(1, HEAD_DIM)
    gain_key = small[3, :, 0:head_shard].reshape(1, HEAD_DIM)

    feed_one = norm_rows(input_rows, gain_first)
    kv, raw_kv, latest = [], [], ()
    for h in range(2):
        part = project(
            feed_one, weights, cosine, sine, gain_key, groups, groups, 1, h * half_rows, half_rows, after=latest
        )
        kv.append(part[0])
        raw_kv.append(part[1])
        latest = (part[0],)
        if pair and h == 0:
            half_width = width // 2
            sent = lax.dynamic_slice(
                behind(weights, part[0]), (core_at * half_width, 2 * columns), (half_width, columns)
            )
            output_same = tp_swap(sent, "output_proj")
            latest = (sent,)
    across = [x_swap(kv[0], "kv0")]
    beside = [core_swap(kv[0], "kv0")]
    one_turned = turned(feed_one, "normed_one", after=(kv[1],))
    across.append(x_swap(behind(kv[1], across[0], one_turned[0]), "kv1"))
    beside.append(core_swap(kv[1], "kv1"))
    others = [(beside[0], across[0], core_swap(across[0], "kv0_across"))]
    q, raw_q = project(
        feed_one, weights, cosine, sine, gain_query, groups, 0, 2, 0, tokens,
        after=(one_turned[0], beside[0], across[0], beside[1]),
    )
    found = [attend(orders, q, kv[0], others[0], 0, half_seqs, local)]
    attended = [found[0][0]]
    arrived = behind(across[1], attended[0])
    shard_two = behind(shard_two, arrived)
    others.append((beside[1], arrived, core_swap(arrived, "kv1_across")))
    weights_two = lax.all_gather(shard_two, ("dp", "ctx"), axis=0, tiled=True)

    settled = (attended[0],)
    if pair:
        output_swapped = core_swap(behind(output_same, arrived), "output_proj")
        settled += (output_swapped,)
    found.append(attend(orders, q, kv[1], others[1], half_seqs, half_seqs, local, after=settled))
    attended, probs = [list(parts) for parts in zip(*found)]
    joined = None
    attended_pair = attended, [core_swap(part, "attended") for part in attended]
    if pair:
        other_heads = [tp_swap(part, f"attended{h}") for h, part in enumerate(attended)]
        for h in range(2):
            joined = output_join(
                spot, input_rows, attended[h], other_heads[h], weights, 2,
                output_same, output_swapped, gain_second, h * half_rows, joined,
            )
    else:
        for h in range(2):
            part = nt_product([(attended[h], weights, 2 * columns)], 0, half_rows)
            started = tp_start(part, f"attended{h}")
            joined = join(input_rows, *started, gain_second, h * half_rows, joined)
    middle, feed_two = joined

    cut = width // 4
    tile = min(512, third)

    class Gradient:
        def __init__(self, name, parts, after=()):
            self.name = name
            to_x, self.keep = grad_product(parts, tile, (cut, cut), after=after)
            self.from_x = x_swap(to_x, name)

    def over_dp(name, grads, after=()):
        summed = add_rows([(grad.keep, grad.from_x) for grad in grads], after=after)
        with jax.named_scope(name + "_over_dp"):
            return summed, lax.psum_scatter(summed, "dp", scatter_dimension=0, tiled=True)

    def with_core(values, name):
        return [([value], [core_swap(value, name)]) for value in values]

    names = ("hidden", "gate_back", "up_back")
    starts = [3 * columns + at * third for at in range(3)]
    settled = (*attended_pair[1], one_turned[1])
    two_turned = turned(feed_two, "normed_two", after=settled)
    acts = feed(feed_two, cot_rows, weights, starts, tile, third, 1, after=(two_turned[0],))
    firsts = [([a[0]], [core_swap(a[0], n + "_one")]) for a, n in zip(acts, names)]
    parts = [(cot_turned, firsts[0]), (two_turned, firsts[1]), (two_turned, firsts[2])]
    first_third = Gradient("first_third", parts)
    starts = [at * 2 * third for at in range(3)]
    acts = feed(
        feed_two, cot_rows, weights_two, starts, tile, 2 * third, 1, after=(first_third.keep,)
    )
    seconds = [([a[0]], [core_swap(a[0], n + "_two")]) for a, n in zip(acts, names)]

    def feed_terms(at, kind):
        place = 3 * columns + kind * third
        return [(firsts[at][0][0], weights, place), (seconds[at][0][0], weights_two, 2 * kind * third)]

    back_terms = feed_terms(1, 0) + feed_terms(2, 1)
    back, out_started = [], []
    part = nt_product(back_terms, 0, half_rows)
    back.append(tp_start(part, "back0"))
    down_two = Gradient("down_two", [(cot_turned, seconds[0])], after=(part,))
    landed = (seconds[1][1][0], seconds[2][1][0])
    part = nt_product(back_terms, half_rows, half_rows, after=(down_two.keep, *landed))
    back.append(tp_start(part, "back1"))
    done, first_out = over_dp("first_third", [first_third], after=(part,))
    gate_two = Gradient("gate_two", [(two_turned, seconds[1])], after=(done,))

    def out_half(h, after):
        part = nt_product(feed_terms(0, 2), h * half_rows, half_rows, after=after)
        out_started.append(tp_start(part, f"out{h}"))
        return part

    grads, q_back, k_back, pieces, one = None, None, None, [], []
    sums = {"second": 0.0, "query": 0.0, "key": 0.0, "first": 0.0}

    def middle_half(h, after):
        *found, second = norm_back(
            middle, cot_rows, *back[h], gain_second, h * half_rows, (F32, BF16), grads, after=after
        )
        sums["second"] = sums["second"] + jnp.sum(second, axis=0)
        return found, nn_product(found[1], weights, 2 * columns, columns, h * half_rows, half_rows)

    def attention_half(h, grad_attended, after):
        found, to_own, to_x, to_core, query = attend_back(
            q, kv[h], others[h], probs[h], grad_attended, raw_q, cosine, sine, gain_query,
            h * half_seqs, half_seqs, local, q_back, after=after,
        )
        sums["query"] = sums["query"] + jnp.sum(query, axis=0)
        return found, to_own, to_x, core_swap(to_core, f"kv_grad{h}")

    def send_keys(h, held, after):
        to_own, to_x, from_core = held
        sent = add_rows([(to_x, from_core)], after=after)
        pieces.append((to_own, from_core, x_swap(sent, f"kv_grad{h}")))
        return sent

    def key_half(h, after):
        found, key = key_back(
            *pieces[h], raw_kv[h], cosine, sine, gain_key, h * half_seqs, half_seqs, local,
            tokens, k_back, after=after,
        )
        sums["key"] = sums["key"] + jnp.sum(key, axis=0)
        return found

    def one_half(h, after):
        terms = [(q_back, weights, 0), (k_back, weights, columns)]
        part = nt_product(terms, h * half_rows, half_rows, after=after)
        one.append(tp_start(part, f"one{h}"))
        return part

    grads, grad_attended = middle_half(0, (gate_two.keep,))
    part = out_half(0, (grad_attended,))
    q_back, *held = attention_half(0, grad_attended, (part,))
    grads, grad_attended = middle_half(1, (held[0],))
    grad_middle, middle_low = grads
    low_turned = turned(middle_low, "grad_middle", after=(grad_attended, gate_two.from_x))
    sent = send_keys(0, held, (low_turned[0],))
    done, more_out = over_dp("down_gate_two", [down_two, gate_two], after=(sent, first_out))
    output_grad = Gradient("output", [(low_turned, attended_pair)], after=(done,))
    part = out_half(1, (output_grad.keep,))
    landed = (part, out_started[0][1])
    up_two = Gradient("up_two", [(two_turned, seconds[2])], after=landed)
    k_back = key_half(0, (up_two.keep,))
    part = one_half(0, (output_grad.from_x,))
    q_back, *held = attention_half(1, grad_attended, (part,))
    q_pair = [q_back], [core_swap(q_back, "query_back")]
    outputs = sum_rows(middle, out_started[0], 0, None, after=(held[0],))
    sent = send_keys(1, held, (outputs,))
    query_grad = Gradient("query", [(one_turned, q_pair)], after=(sent,))
    outputs = sum_rows(middle, out_started[1], half_rows, outputs, after=(query_grad.keep,))
    done, output_out = over_dp("output", [output_grad], after=(outputs, more_out))
    done, up_out = over_dp("up_two", [up_two], after=(done,))
    terms = gain_terms(input_rows, one[0][0], 0, after=(done,))
    k_back = key_half(1, (terms,))
    part = one_half(1, ())
    k_pair = [k_back], [core_swap(k_back, "key_back")]
    key_grad = Gradient("key", [(one_turned, k_pair)], after=(part,))

    def input_half(h, into, after, cost):
        return norm_back(
            input_rows, grad_middle, *one[h], gain_first, h * half_rows, (BF16,), into, after=after, cost=cost
        )[0:1]

    result = input_half(0, None, (key_grad.keep, query_grad.from_x), 7.5)
    done, heads_out = over_dp("query_key", [query_grad, key_grad], after=(result[0],))
    part = gain_terms(input_rows, one[1][0], half_rows, after=(done,))
    sums["first"] = jnp.sum(terms + part, axis=0)

    if not pair:
        sums["first"], sums["second"] = sums["first"] / tp_size, sums["second"] / tp_size
    places = dp_size * 4
    totals = [sums[name].reshape(places, -1) for name in ("first", "second", "query", "key")]
    totals = jnp.concatenate(totals, axis=1)
    totals = jnp.broadcast_to(totals[:, None, :], (places, tp_size, totals.shape[1]))
    totals = totals.reshape(places * tp_size, -1)
    totals = lax.all_to_all(totals, ("dp", "ctx", "tp"), 0, 0, tiled=True)

    result = input_half(1, result, (part,), 300)
    totals = jnp.sum(behind(totals, result[0]), axis=0)
    grad_kv = heads_out[:, columns:].astype(F32)
    down_out, gate_out, up_first = [first_out[:, at * third : (at + 1) * third] for at in range(3)]
    beside = lambda left, right: jnp.concatenate([left, right], axis=1).astype(F32)
    return (
        outputs.reshape(inputs.shape),
        result[0].reshape(inputs.shape),
        totals[0:shard],
        heads_out[:, 0:columns].astype(F32),
        split_heads(grad_kv, 0),
        split_heads(grad_kv, 1),
        totals[2 * shard : 2 * shard + head_shard],
        totals[2 * shard + head_shard :],
        output_out.astype(F32).T,
        totals[shard : 2 * shard],
        beside(gate_out, more_out[:, 2 * third :]),
        beside(up_first, up_out),
        beside(down_out, more_out[:, 0 : 2 * third]).T,
    )


def solution(mesh):
    rows = P(("dp", "ctx"))
    columns = P(("dp", "ctx"), "tp")
    turned = P("tp", ("dp", "ctx"))
    tokens = P("dp", "ctx", None)
    in_specs = (
        (tokens, P("dp", None), rows, columns, columns, columns, rows, rows, turned, rows)
        + (columns, columns, turned, tokens)
    )
    out_specs = (
        (tokens, tokens, rows, columns, columns, columns, rows, rows, turned, rows)
        + (columns, columns, turned)
    )
    return jax.shard_map(shards, mesh=mesh, in_specs=in_specs, out_specs=out_specs, check_vma=False)
```

```python
import functools

import jax
import jax.numpy as jnp
from jax import lax
from jax.experimental import pallas as pl
from jax.experimental.pallas import tpu as pltpu
from jax.sharding import PartitionSpec as P

HEAD_DIM = 128
GROUP = 2 * HEAD_DIM
BLOCK = 128
EPSILON = 1e-06
ROPE_BASE = 1000000.0
MASKED = -1e30
VMEM_LIMIT = 56 * 1024 * 1024
F32 = jnp.float32
BF16 = jnp.bfloat16
FLOPS_PER_US = 1e10

CORE_SWAP = [(0, 1), (1, 0), (2, 3), (3, 2)]
X_SWAP = [(0, 2), (2, 0), (1, 3), (3, 1)]
TP_SWAP = [(0, 1), (1, 0)]


def nn(left, right):
    return lax.dot_general(left, right, (((1,), (0,)), ((), ())), preferred_element_type=F32)


def nt(left, right):
    return lax.dot_general(left, right, (((1,), (1,)), ((), ())), preferred_element_type=F32)


def tn(left, right):
    return lax.dot_general(left, right, (((0,), (0,)), ((), ())), preferred_element_type=F32)


def unit_norm(values):
    inverse = lax.rsqrt(jnp.mean(values * values, axis=-1, keepdims=True) + EPSILON)
    return values * inverse, inverse


def swap_halves(values):
    return pltpu.roll(values, HEAD_DIM // 2, 1)


def call(kernel, grid, ins, outs, scratch=(), scalars=(), alias=None, after=(), name=None, cost=1.0):
    any_space = pl.BlockSpec(memory_space=pl.ANY)
    specs = [any_space if b is None else pl.BlockSpec(b, m) for _, b, m in ins]
    n_in, n_after, n_scalar = len(ins), len(after), len(scalars)

    def body(*refs):
        keep = refs[: n_scalar + n_in] + refs[n_scalar + n_in + n_after :]
        kernel(*keep)

    return pl.pallas_call(
        body,
        grid_spec=pltpu.PrefetchScalarGridSpec(
            num_scalar_prefetch=n_scalar,
            grid=grid,
            in_specs=specs + [any_space] * n_after,
            out_specs=[pl.BlockSpec(b, m) for _, _, b, m in outs],
            scratch_shapes=list(scratch),
        ),
        out_shape=[jax.ShapeDtypeStruct(s, d) for s, d, _, _ in outs],
        input_output_aliases={n_scalar + i: o for o, i in (alias or {}).items()},
        compiler_params=pltpu.CompilerParams(
            dimension_semantics=("arbitrary",) * len(grid), vmem_limit_bytes=VMEM_LIMIT
        ),
        cost_estimate=pl.CostEstimate(
            flops=int(cost * FLOPS_PER_US), bytes_accessed=0, transcendentals=0
        ),
        name=name,
    )(*scalars, *[a for a, _, _ in ins], *after)


def pack_first_kernel(q_ref, k_ref, v_ref, o_ref, g_ref, u_ref, d_ref, small_ref, out_ref):
    columns, third = q_ref.shape[1], g_ref.shape[1]
    out_ref[:, 0:columns] = q_ref[...]
    for at in range(columns // GROUP):
        cut = slice(at * HEAD_DIM, (at + 1) * HEAD_DIM)
        start = columns + at * GROUP
        out_ref[:, start : start + HEAD_DIM] = k_ref[:, cut]
        out_ref[:, start + HEAD_DIM : start + GROUP] = v_ref[:, cut]
    out_ref[:, 2 * columns : 3 * columns] = o_ref[...].T
    start = 3 * columns
    out_ref[:, start : start + third] = g_ref[...]
    out_ref[:, start + third : start + 2 * third] = u_ref[...]
    out_ref[:, start + 2 * third : start + 3 * third] = d_ref[...].T
    out_ref[:, start + 3 * third :] = small_ref[...]


def pack_first(q, k, v, o, g, u, d, small, third):
    shard, columns = q.shape
    whole = lambda array: (array, array.shape, lambda j: (0, 0))
    total = 3 * columns + 3 * third + BLOCK
    return call(
        pack_first_kernel,
        (1,),
        [whole(q), whole(k), whole(v), whole(o)]
        + [(g, (shard, third), lambda j: (0, 0)), (u, (shard, third), lambda j: (0, 0))]
        + [(d, (third, shard), lambda j: (0, 0)), whole(small)],
        [((shard, total), BF16, (shard, total), lambda j: (0, 0))],
        name="pack_first",
        cost=3,
    )[0]


def pack_second_kernel(g_ref, u_ref, d_ref, out_ref):
    step = pl.program_id(0)
    part = step // 2

    @pl.when(part == 0)
    def _():
        out_ref[...] = g_ref[...]

    @pl.when(part == 1)
    def _():
        out_ref[...] = u_ref[...]

    @pl.when(part == 2)
    def _():
        out_ref[...] = d_ref[...].T


def pack_second(g, u, d, third, after=()):
    shard = g.shape[0]
    return call(
        pack_second_kernel,
        (6,),
        [(g, (shard, third), lambda j: (0, 1 + j % 2)), (u, (shard, third), lambda j: (0, 1 + j % 2))]
        + [(d, (third, shard), lambda j: (1 + j % 2, 0))],
        [((shard, 6 * third), BF16, (shard, third), lambda j: (0, j))],
        after=after,
        name="pack_second",
        cost=5,
    )[0]


def norm_kernel(x_ref, gain_ref, out_ref):
    out_ref[...] = (unit_norm(x_ref[...].astype(F32))[0] * gain_ref[...]).astype(BF16)


def norm_rows(x, gain, after=()):
    tokens, width = x.shape
    tile = min(256, tokens)
    block = (tile, width)
    return call(
        norm_kernel,
        (tokens // tile,),
        [(x, block, lambda j: (j, 0)), (gain, (1, width), lambda j: (0, 0))],
        [((tokens, width), BF16, block, lambda j: (j, 0))],
        after=after,
        name="norm_rows",
        cost=5,
    )[0]


def project_kernel(x_ref, w_ref, cos_ref, sin_ref, gain_ref, out_ref, raw_ref, *, turned, rows):
    for at in range(0, x_ref.shape[0], rows):
        part = pl.ds(at, rows)
        raw = nn(x_ref[part, :], w_ref[...])
        raw_ref[part, :] = raw
        cosine, sine = cos_ref[part, :], sin_ref[part, :]
        for head in range(2):
            values = raw[:, head * HEAD_DIM : (head + 1) * HEAD_DIM]
            if head < turned:
                scaled = unit_norm(values)[0] * gain_ref[...]
                values = scaled * cosine + swap_halves(scaled) * sine
            out_ref[part, head * HEAD_DIM : (head + 1) * HEAD_DIM] = values.astype(BF16)


def project(x, weights, cosine, sine, gain, groups, first, turned, row, rows, after=()):
    width = x.shape[1]
    some = lambda j: (row // rows, 0)
    column = lambda j: (0, j)
    columns = groups * GROUP
    return call(
        functools.partial(project_kernel, turned=turned, rows=min(256, rows)),
        (groups,),
        [
            (x, (rows, width), some),
            (weights, (width, GROUP), lambda j: (0, first + j)),
            (cosine, (rows, HEAD_DIM), some),
            (sine, (rows, HEAD_DIM), some),
            (gain, (1, HEAD_DIM), lambda j: (0, 0)),
        ],
        [
            ((rows, columns), BF16, (rows, GROUP), column),
            ((rows, columns), F32, (rows, GROUP), column),
        ],
        after=after,
        name="project",
        cost=10,
    )


def span_places(orders_ref, seq, piece, span, shape, dim):
    index = lax.broadcasted_iota(jnp.int32, shape, dim)
    first, second = orders_ref[seq, 2 * piece], orders_ref[seq, 2 * piece + 1]
    return jnp.where(index < span, first * span + index, second * span + index - span)


def stacked_heads(block):
    return jnp.concatenate([block[:, 0:HEAD_DIM], block[:, HEAD_DIM:GROUP]], axis=0)


def masked_exponents(orders_ref, seq, query, pieces, span):
    rows, keys = query.shape[0], pieces[0].shape[0]
    scale = HEAD_DIM**-0.5
    places = span_places(orders_ref, seq, 0, span, (rows // 2, 1), 0)
    places = jnp.concatenate([places, places], axis=0)
    scores = []
    for at, piece in enumerate(pieces):
        key_places = span_places(orders_ref, seq, at, span, (1, keys), 1)
        product = nt(query, piece[:, 0:HEAD_DIM]) * scale
        scores.append(jnp.where(key_places <= places, product, MASKED))
    peak = functools.reduce(jnp.maximum, [jnp.max(s, axis=1, keepdims=True) for s in scores])
    exponents = [jnp.exp(s - peak) for s in scores]
    total = functools.reduce(jnp.add, [jnp.sum(e, axis=1, keepdims=True) for e in exponents])
    return exponents, 1.0 / total


def attend_kernel(orders_ref, q_ref, own_ref, core_ref, x_ref, diag_ref, out_ref, prob_ref, *, first, span):
    seq = pl.program_id(0) + first
    local = q_ref.shape[0]
    for group in range(q_ref.shape[1] // GROUP):
        columns = slice(group * GROUP, (group + 1) * GROUP)
        rows = slice(group * 2 * local, (group + 1) * 2 * local)
        query = stacked_heads(q_ref[:, columns])
        pieces = [ref[:, columns] for ref in (own_ref, core_ref, x_ref, diag_ref)]
        exponents, inverse = masked_exponents(orders_ref, seq, query, pieces, span)
        total = None
        for at, (exponent, piece) in enumerate(zip(exponents, pieces)):
            prob = (exponent * inverse).astype(BF16)
            prob_ref[0, rows, at * local : (at + 1) * local] = prob
            product = nn(prob, piece[:, HEAD_DIM:GROUP])
            total = product if total is None else total + product
        result = total.astype(BF16)
        for head in range(2):
            start = group * GROUP + head * HEAD_DIM
            out_ref[:, start : start + HEAD_DIM] = result[head * local : (head + 1) * local]


def attend(orders, q, kv, others, first, count, local, after=()):
    columns = q.shape[1]
    block = (local, columns)
    at_whole = lambda s, o: (s + first, 0)
    at_half = lambda s, o: (s, 0)
    ins = [(q, block, at_whole), (kv, block, at_half)] + [(k, block, at_half) for k in others]
    prob = (1, columns // GROUP * 2 * local, 4 * local)
    return call(
        functools.partial(attend_kernel, first=first, span=local // 2),
        (count,),
        ins,
        [
            ((count * local, columns), BF16, block, at_half),
            ((count,) + prob[1:], BF16, prob, lambda s, o: (s, 0, 0)),
        ],
        scalars=(orders,),
        after=after,
        name="attend",
        cost=11,
    )


def turn_back(grad, raw, cosine, sine, gain):
    turned = grad * cosine - swap_halves(grad) * sine
    unit, inverse = unit_norm(raw)
    grad_normed = turned * gain
    mean = jnp.mean(grad_normed * unit, axis=-1, keepdims=True)
    terms = jnp.sum((turned * unit).reshape(-1, 8, HEAD_DIM), axis=0)
    return (inverse * (grad_normed - unit * mean)).astype(BF16), terms


def clear_at_start(ref, dims):
    start = functools.reduce(jnp.logical_and, [pl.program_id(d) == 0 for d in range(dims)])

    @pl.when(start)
    def _():
        ref[...] = jnp.zeros_like(ref)


def attend_back_kernel(
    q_ref, own_ref, core_ref, x_ref, diag_ref, prob_ref, grad_ref, raw_ref, cos_ref, sin_ref, gain_ref, *rest
):
    q_back_ref, own_out, x_out, core_out, gain_out = rest[-5:]
    clear_at_start(gain_out, 1)
    scale = HEAD_DIM**-0.5
    local = q_ref.shape[0]
    outs = (own_out, core_out.at[0], x_out, core_out.at[1])
    for group in range(q_ref.shape[1] // GROUP):
        start = group * GROUP
        both = slice(start, start + GROUP)
        rows = slice(group * 2 * local, (group + 1) * 2 * local)
        query = stacked_heads(q_ref[:, both])
        grad = stacked_heads(grad_ref[:, both])
        pieces = [ref[:, both] for ref in (own_ref, core_ref, x_ref, diag_ref)]
        lows = [prob_ref[0, rows, at * local : (at + 1) * local] for at in range(4)]
        products = [low.astype(F32) * nt(grad, p[:, HEAD_DIM:GROUP]) for low, p in zip(lows, pieces)]
        delta = functools.reduce(jnp.add, [jnp.sum(p, axis=1, keepdims=True) for p in products])
        grad_scores = [(p - low.astype(F32) * delta).astype(BF16) for p, low in zip(products, lows)]
        grad_query = functools.reduce(
            jnp.add, [nn(s, p[:, 0:HEAD_DIM]) for s, p in zip(grad_scores, pieces)]
        )
        for out, scores, low in zip(outs, grad_scores, lows):
            out[:, start : start + HEAD_DIM] = (tn(scores, query) * scale).astype(BF16)
            out[:, start + HEAD_DIM : start + GROUP] = tn(low, grad).astype(BF16)
        for head in range(2):
            columns = slice(start + head * HEAD_DIM, start + (head + 1) * HEAD_DIM)
            result, terms = turn_back(
                grad_query[head * local : (head + 1) * local] * scale,
                raw_ref[:, columns],
                cos_ref[...],
                sin_ref[...],
                gain_ref[...],
            )
            q_back_ref[:, columns] = result
            gain_out[...] += terms


def attend_back(q, kv, others, prob, grad, raw, cosine, sine, gain, first, count, local, into, after=()):
    columns = q.shape[1]
    block = (local, columns)
    at_whole = lambda s: (s + first, 0)
    at_half = lambda s: (s, 0)
    fixed = lambda s: (0, 0)
    ins = [(q, block, at_whole), (kv, block, at_half)] + [(k, block, at_half) for k in others]
    ins += [(prob, (1,) + prob.shape[1:], lambda s: (s, 0, 0))]
    ins += [(grad, block, at_half), (raw, block, at_whole)]
    ins += [(cosine, (local, HEAD_DIM), at_whole), (sine, (local, HEAD_DIM), at_whole)]
    ins += [(gain, (1, HEAD_DIM), fixed)]
    if into is not None:
        ins.append((into, None, None))
    piece = ((count * local, columns), BF16, block, at_half)
    return call(
        attend_back_kernel,
        (count,),
        ins,
        [(q.shape, BF16, block, at_whole)]
        + [piece] * 2
        + [((2, count * local, columns), BF16, (2, local, columns), lambda s: (0, s, 0))]
        + [((8, HEAD_DIM), F32, (8, HEAD_DIM), fixed)],
        alias=None if into is None else {0: len(ins) - 1},
        after=after,
        name="attend_back",
        cost=25,
    )


def key_back_kernel(mine_ref, core_ref, x_ref, raw_ref, cos_ref, sin_ref, gain_ref, *rest):
    out_ref, gain_out = rest[-2:]
    clear_at_start(gain_out, 1)
    for group in range(mine_ref.shape[1] // GROUP):
        start = group * GROUP
        both = slice(start, start + GROUP)
        parts = [ref[:, both].astype(F32) for ref in (mine_ref, core_ref.at[0], x_ref)]
        grad = functools.reduce(jnp.add, parts)
        result, terms = turn_back(
            grad[:, 0:HEAD_DIM],
            raw_ref[:, start : start + HEAD_DIM],
            cos_ref[...],
            sin_ref[...],
            gain_ref[...],
        )
        out_ref[:, start : start + HEAD_DIM] = result
        out_ref[:, start + HEAD_DIM : start + GROUP] = grad[:, HEAD_DIM:GROUP].astype(BF16)
        gain_out[...] += terms


def key_back(mine, core, x, raw, cosine, sine, gain, first, count, local, tokens, into, after=()):
    columns = mine.shape[1]
    block = (local, columns)
    at_whole = lambda s: (s + first, 0)
    at_half = lambda s: (s, 0)
    fixed = lambda s: (0, 0)
    ins = [(mine, block, at_half), (core, (1,) + block, lambda s: (0, s, 0)), (x, block, at_half)]
    ins += [(raw, block, at_half)]
    ins += [(cosine, (local, HEAD_DIM), at_whole), (sine, (local, HEAD_DIM), at_whole)]
    ins += [(gain, (1, HEAD_DIM), fixed)]
    if into is not None:
        ins.append((into, None, None))
    return call(
        key_back_kernel,
        (count,),
        ins,
        [
            ((tokens, columns), BF16, block, at_whole),
            ((8, HEAD_DIM), F32, (8, HEAD_DIM), fixed),
        ],
        alias=None if into is None else {0: len(ins) - 1},
        after=after,
        name="key_back",
        cost=5,
    )


def feed_kernel(x_ref, c_ref, g_ref, u_ref, d_ref, *outs, rows, steps):
    step, pieces = pl.program_id(0), len(outs) // 3

    def fill(hidden_ref, gate_ref, up_ref):
        for at in range(0, x_ref.shape[0], rows):
            part = pl.ds(at, rows)
            gate = nn(x_ref[part, :], g_ref[...])
            upward = nn(x_ref[part, :], u_ref[...])
            grad = nn(c_ref[part, :], d_ref[...])
            sigmoid = jax.nn.sigmoid(gate)
            silu = gate * sigmoid
            hidden_ref[part, :] = (silu * upward).astype(BF16)
            slope = sigmoid + silu * (1.0 - sigmoid)
            gate_ref[part, :] = (grad * upward * slope).astype(BF16)
            up_ref[part, :] = (grad * silu).astype(BF16)

    for piece in range(pieces):
        run = functools.partial(fill, *outs[piece::pieces])
        if pieces == 1:
            run()
        else:
            pl.when(step // steps == piece)(run)


def feed(x, c, weights, starts, tile, piece, pieces, after=()):
    tokens, width = x.shape
    steps = piece // tile
    whole = lambda j: (0, 0)
    ins = [(x, (tokens, width), whole), (c, (tokens, width), whole)]
    for start in starts:
        ins.append((weights, (width, tile), lambda j, start=start: (0, start // tile + j)))
    outs = [
        ((tokens, piece), BF16, (tokens, tile), lambda j, at=at: (0, jnp.clip(j - at * steps, 0, steps - 1)))
        for _ in range(3)
        for at in range(pieces)
    ]
    found = call(
        functools.partial(feed_kernel, rows=min(256, tokens), steps=steps),
        (steps * pieces,),
        ins,
        outs,
        after=after,
        name="feed",
        cost=2 + piece * pieces * 0.0165,
    )
    return [found[kind * pieces : (kind + 1) * pieces] for kind in range(3)]


def nt_kernel(*refs, count):
    out_ref = refs[-1]
    total = None
    for left_ref, w_ref in zip(refs[:count], refs[count : 2 * count]):
        product = nt(left_ref[...], w_ref[...])
        total = product if total is None else total + product
    out_ref[...] = total.astype(out_ref.dtype)


def nt_product(terms, row, rows, after=()):
    width = terms[0][1].shape[0]
    tile = min(512, width)
    ins = [(left, (rows, left.shape[1]), lambda j: (row // rows, 0)) for left, _, _ in terms]
    ins += [
        (weights, (tile, left.shape[1]), lambda j, at=at // left.shape[1]: (j, at))
        for left, weights, at in terms
    ]
    return call(
        functools.partial(nt_kernel, count=len(terms)),
        (width // tile,),
        ins,
        [((rows, width), BF16, (rows, tile), lambda j: (0, j))],
        after=after,
        name="nt_product",
        cost=1.5 + rows * sum(left.shape[1] for left, _, _ in terms) * 6.0e-6,
    )[0]


def nn_kernel(x_ref, w_ref, out_ref):
    out_ref[...] = nn(x_ref[...], w_ref[...]).astype(out_ref.dtype)


def nn_product(left, weights, first_column, columns, row, rows, after=()):
    width = weights.shape[0]
    tile = min(512, columns)
    return call(
        nn_kernel,
        (columns // tile,),
        [
            (left, (rows, width), lambda j: (row // rows, 0)),
            (weights, (width, tile), lambda j: (0, first_column // tile + j)),
        ],
        [((rows, columns), BF16, (rows, tile), lambda j: (0, j))],
        after=after,
        name="nn_product",
        cost=6,
    )[0]


def output_join_kernel(
    at_ref, x_ref, mine_ref, other_ref, w_mine_ref, w_same_ref, w_swap_ref, gain_ref, *rest, steps
):
    middle_ref, normed_ref, rows_ref = rest[-3:]
    step = pl.program_id(0)
    tile = x_ref.shape[1]
    is_first, core = at_ref[0] == 0, at_ref[1]
    direct = (step * 2 // steps) == core
    mine, other, w_mine = mine_ref[...], other_ref[...], w_mine_ref[...]
    w_other = jnp.where(direct, w_same_ref[...], w_swap_ref[...])
    total = nt(jnp.where(is_first, mine, other), jnp.where(is_first, w_mine, w_other))
    total += nt(jnp.where(is_first, other, mine), jnp.where(is_first, w_other, w_mine))
    columns = pl.ds(pl.multiple_of(step * tile, tile), tile)
    rows_ref[:, columns] = x_ref[...].astype(F32) + total

    @pl.when(step == steps - 1)
    def _():
        middle = rows_ref[...]
        middle_ref[...] = middle
        normed_ref[...] = (unit_norm(middle)[0] * gain_ref[...]).astype(BF16)


def output_join(at, x, mine, other, weights, block, same, swapped, gain, row, into, after=()):
    tokens, width = x.shape
    rows, columns = mine.shape
    tile = min(512, width // 2)
    steps = width // tile
    fixed = lambda j, a: (0, 0)
    fetched = lambda j, a: (j % (steps // 2), 0)
    ins = [
        (x, (rows, tile), lambda j, a: (row // rows, j)),
        (mine, (rows, columns), fixed),
        (other, (rows, columns), fixed),
        (weights, (tile, columns), lambda j, a: (j, block)),
        (same, (tile, columns), fetched),
        (swapped, (tile, columns), fetched),
        (gain, (1, width), fixed),
    ]
    alias = None
    if into is not None:
        alias = {o: len(ins) + o for o in range(2)}
        ins += [(array, None, None) for array in into]
    out = lambda kind: ((tokens, width), kind, (rows, width), lambda j, a: (row // rows, 0))
    return call(
        functools.partial(output_join_kernel, steps=steps),
        (steps,),
        ins,
        [out(F32), out(BF16)],
        scratch=[pltpu.VMEM((rows, width), F32)],
        scalars=(at,),
        alias=alias,
        after=after,
        name="output_join",
        cost=15,
    )


def turn_kernel(order_ref, *refs):
    ins, outs = refs[:4], refs[4:]
    step = pl.program_id(0)

    def fill(out_ref):
        for at, ref in enumerate(ins):
            out_ref[at * BLOCK : (at + 1) * BLOCK, :] = ref[...].T

    pl.when(step < 2)(lambda: fill(outs[0]))
    pl.when(step >= 2)(lambda: fill(outs[1]))


def turned_blocks(order, left, after=()):
    tokens, width = left.shape
    ins = [(left, (tokens, BLOCK), lambda j, o, at=at: (0, o[4 * j + at])) for at in range(4)]
    out = lambda spot: ((width // 2, tokens), BF16, (4 * BLOCK, tokens), spot)
    return call(
        turn_kernel,
        (width // BLOCK // 4,),
        ins,
        [out(lambda j, o: (jnp.minimum(j, 1), 0)), out(lambda j, o: (jnp.maximum(j - 2, 0), 0))],
        scalars=(order,),
        after=after,
        name="turned_blocks",
        cost=6,
    )


def grad_kernel(*refs, plan, outs):
    step, begin, used = pl.program_id(0), 0, 0
    out_refs = refs[-outs:]

    def fill(left_refs, right_refs):
        for at, out in enumerate(out_refs):
            size, total = out.shape[0], None
            rows = pl.ds(at * size, size)
            for left_ref, pieces in zip(left_refs, right_refs):
                start = 0
                for piece in pieces:
                    tokens = piece.shape[0]
                    product = nn(left_ref[rows, start : start + tokens], piece[...])
                    total = product if total is None else total + product
                    start += tokens
            out[...] = total.astype(BF16)

    for pieces, count in plan:
        part = refs[used : used + 2 + 2 * pieces]
        run = functools.partial(fill, part[:2], (part[2 : 2 + pieces], part[2 + pieces :]))
        if len(plan) == 1:
            run()
        else:
            pl.when((step >= begin) & (step < begin + count))(run)
        begin, used = begin + count, used + 2 + 2 * pieces


def grad_product(parts, tile, cuts, after=()):
    width, tokens = parts[0][0][0].shape
    ins, begin, plan = [], 0, []
    for lefts, rights in parts:
        count = rights[0][0].shape[1] // tile
        ins += [(left, left.shape, lambda j: (0, 0)) for left in lefts]
        spot = lambda j, begin=begin, count=count: (0, jnp.clip(j - begin, 0, count - 1))
        ins += [(piece, (piece.shape[0], tile), spot) for pieces in rights for piece in pieces]
        plan.append((len(rights[0]), count))
        begin += count
    return call(
        functools.partial(grad_kernel, plan=plan, outs=len(cuts)),
        (begin,),
        ins,
        [((cut, begin * tile), BF16, (cut, tile), lambda j: (0, j)) for cut in cuts],
        after=after,
        name="grad_product",
        cost=3.5 + begin * tile * 0.0047,
    )


def join_kernel(x_ref, own_ref, other_ref, gain_ref, *rest):
    middle_ref, normed_ref = rest[-2:]
    middle = x_ref[...].astype(F32) + (own_ref[...].astype(F32) + other_ref[...].astype(F32))
    middle_ref[...] = middle
    normed_ref[...] = (unit_norm(middle)[0] * gain_ref[...]).astype(BF16)


def join(x, own, other, gain, row, into, after=()):
    tokens, width = x.shape
    rows = own.shape[0]
    tile = min(256, rows)
    block = (tile, width)
    at_whole = lambda j: (row // tile + j, 0)
    at_half = lambda j: (j, 0)
    ins = [(x, block, at_whole), (own, block, at_half), (other, block, at_half)]
    ins += [(gain, (1, width), lambda j: (0, 0))]
    alias = None
    if into is not None:
        alias = {o: len(ins) + o for o in range(2)}
        ins += [(array, None, None) for array in into]
    return call(
        join_kernel,
        (rows // tile,),
        ins,
        [((tokens, width), F32, block, at_whole), ((tokens, width), BF16, block, at_whole)],
        alias=alias,
        after=after,
        name="join",
        cost=7.5,
    )


def norm_back_kernel(v_ref, base_ref, own_ref, other_ref, gain_ref, *rest, outs):
    out_refs, terms_ref = rest[-outs - 1 : -1], rest[-1]
    clear_at_start(terms_ref, 1)
    own = own_ref[...].astype(F32)
    unit, inverse = unit_norm(v_ref[...].astype(F32))
    grad_normed = (own + other_ref[...].astype(F32)) * gain_ref[...]
    mean = jnp.mean(grad_normed * unit, axis=-1, keepdims=True)
    result = base_ref[...].astype(F32) + inverse * (grad_normed - unit * mean)
    for ref in out_refs:
        ref[...] = result.astype(ref.dtype)
    terms_ref[...] += jnp.sum((own * unit).reshape(-1, 8, own.shape[1]), axis=0)


def norm_back(values, base, own, other, gain, row, types, into, after=(), cost=7.5):
    tokens, width = values.shape
    rows = own.shape[0]
    tile = min(256, rows)
    block = (tile, width)
    at_whole = lambda j: (row // tile + j, 0)
    at_half = lambda j: (j, 0)
    fixed = lambda j: (0, 0)
    ins = [(values, block, at_whole), (base, block, at_whole)]
    ins += [(own, block, at_half), (other, block, at_half), (gain, (1, width), fixed)]
    alias = None
    if into is not None:
        alias = {o: len(ins) + o for o in range(len(types))}
        ins += [(array, None, None) for array in into]
    return call(
        functools.partial(norm_back_kernel, outs=len(types)),
        (rows // tile,),
        ins,
        [((tokens, width), kind, block, at_whole) for kind in types]
        + [((8, width), F32, (8, width), fixed)],
        alias=alias,
        after=after,
        name="norm_back",
        cost=cost,
    )


def sum_kernel(*refs):
    own, other = refs[1][...].astype(F32), refs[2][...].astype(F32)
    refs[-1][...] = (refs[0][...] + (own + other)).astype(BF16)


def sum_rows(values, parts, row, into, after=()):
    tokens, width = values.shape
    rows = parts[0].shape[0]
    tile = min(256, rows)
    block = (tile, width)
    at_whole = lambda j: (row // tile + j, 0)
    ins = [(values, block, at_whole)] + [(part, block, lambda j: (j, 0)) for part in parts]
    if into is not None:
        ins.append((into, None, None))
    return call(
        sum_kernel,
        (rows // tile,),
        ins,
        [((tokens, width), BF16, block, at_whole)],
        alias=None if into is None else {0: len(ins) - 1},
        after=after,
        name="sum_rows",
        cost=6,
    )[0]


def terms_kernel(v_ref, own_ref, terms_ref):
    clear_at_start(terms_ref, 1)
    unit = unit_norm(v_ref[...].astype(F32))[0]
    terms_ref[...] += jnp.sum((own_ref[...].astype(F32) * unit).reshape(-1, 8, unit.shape[1]), axis=0)


def gain_terms(values, own, row, after=()):
    width = values.shape[1]
    rows = own.shape[0]
    tile = min(256, rows)
    return call(
        terms_kernel,
        (rows // tile,),
        [
            (values, (tile, width), lambda j: (row // tile + j, 0)),
            (own, (tile, width), lambda j: (j, 0)),
        ],
        [((8, width), F32, (8, width), lambda j: (0, 0))],
        after=after,
        name="gain_terms",
        cost=4,
    )[0]


def add_kernel(*refs, widths):
    start = 0
    for at, width in enumerate(widths):
        left, right = refs[2 * at][...].astype(F32), refs[2 * at + 1][...].astype(F32)
        refs[-1][:, start : start + width] = (left + right.reshape(left.shape)).astype(BF16)
        start += width


def add_rows(parts, after=()):
    rows = parts[0][0].shape[0]
    widths = [left.shape[1] for left, _ in parts]
    tile, total = rows // 2, sum(widths)
    ins = []
    for left, right in parts:
        ins.append((left, (tile, left.shape[1]), lambda j: (j, 0)))
        if right.ndim == 3:
            ins.append((right, (1, tile, right.shape[2]), lambda j: (1, j, 0)))
        else:
            ins.append((right, (tile, right.shape[1]), lambda j: (j, 0)))
    return call(
        functools.partial(add_kernel, widths=widths),
        (2,),
        ins,
        [((rows, total), BF16, (tile, total), lambda j: (j, 0))],
        after=after,
        name="add_rows",
        cost=3,
    )[0]


def split_heads(both, which):
    cuts = range(which, both.shape[1] // HEAD_DIM, 2)
    return jnp.concatenate([both[:, at * HEAD_DIM : (at + 1) * HEAD_DIM] for at in cuts], axis=1)


def behind(value, *others):
    return lax.optimization_barrier((value,) + others)[0]


def shards(
    inputs,
    span_order,
    first_gain,
    query_proj,
    key_matrix,
    value_matrix,
    query_norm,
    key_norm,
    output_proj,
    second_gain,
    gate_proj,
    up_proj,
    down_proj,
    cotangent,
):
    seqs, local, width = inputs.shape
    tokens = seqs * local
    span = local // 2
    shard = query_proj.shape[0]
    head_shard = query_norm.shape[0]
    columns = query_proj.shape[1]
    groups = columns // GROUP
    units = gate_proj.shape[1]
    third = units // 3
    dp_size, tp_size = lax.axis_size("dp"), lax.axis_size("tp")
    ctx, tp_at = lax.axis_index("ctx"), lax.axis_index("tp")
    x_at, core_at = ctx // 2, ctx % 2
    half_rows = tokens // 2
    half_seqs = seqs // 2
    pair = tp_size == 2

    def swap(axis, pairs, value, name):
        with jax.named_scope(name):
            return lax.ppermute(value, axis, pairs)

    tp_swap = lambda value, name: swap("tp", TP_SWAP, value, name + "_over_tp")
    core_swap = lambda value, name: swap("ctx", CORE_SWAP, value, name + "_over_core")
    x_swap = lambda value, name: swap("ctx", X_SWAP, value, name + "_over_x")

    def tp_start(part, name):
        if pair:
            return part, tp_swap(part, name)
        return lax.psum(part, "tp"), jnp.zeros_like(part)

    small = [first_gain, second_gain, jnp.pad(query_norm, (0, shard - head_shard))]
    small += [jnp.pad(key_norm, (0, shard - head_shard))]
    small = jnp.pad(jnp.stack(small), ((0, shard - len(small)), (0, BLOCK - shard)))
    shard_one = pack_first(
        query_proj, key_matrix, value_matrix, output_proj, gate_proj, up_proj, down_proj, small, third
    )
    weights = lax.all_gather(shard_one, ("dp", "ctx"), axis=0, tiled=True)

    pairs = span_order.reshape(seqs, 4, 2)
    relative = jnp.stack([ctx, ctx ^ 1, ctx ^ 2, ctx ^ 3])
    orders = jnp.take(pairs, relative, axis=1).reshape(seqs, 8)
    places = (
        orders[:, 0:2, None] * span + jnp.arange(span, dtype=jnp.int32)[None, None, :]
    ).reshape(tokens)
    half_dim = HEAD_DIM // 2
    frequency = ROPE_BASE ** (-(jnp.arange(half_dim, dtype=F32) * (2.0 / HEAD_DIM)))
    angles = places.astype(F32)[:, None] * frequency[None, :]
    cosine, sine = jnp.cos(angles), jnp.sin(angles)
    cosine = jnp.concatenate([cosine, cosine], axis=1)
    sine = jnp.concatenate([-sine, sine], axis=1)
    dps = jnp.arange(dp_size, dtype=jnp.int32)
    other_first = jnp.stack([1 - x_at, x_at])
    cores = jnp.stack([1 - core_at, core_at])
    order = cores[:, None, None] + 2 * other_first[None, :, None] + 4 * dps[None, None, :]
    order = order.reshape(-1).astype(jnp.int32)
    spot = jnp.stack([tp_at, core_at]).astype(jnp.int32)
    input_rows = inputs.reshape(tokens, width)
    cot_rows = cotangent.reshape(tokens, width)
    shard_two = pack_second(gate_proj, up_proj, down_proj, third, after=(shard_one,))

    def turned(left, name, after=()):
        to_core, own = turned_blocks(order, left, after=after)
        return own, core_swap(to_core, name)

    cot_turned = turned(cot_rows, "cotangent", after=(shard_two,))
    weights, cosine, sine, orders, order, spot, cot_turned, shard_two = lax.optimization_barrier(
        (weights, cosine, sine, orders, order, spot, cot_turned, shard_two)
    )

    small = weights[:, 3 * columns + 3 * third :].reshape(-1, shard, BLOCK)[:, 0:4, 0:shard]
    small = jnp.transpose(small, (1, 0, 2)).astype(F32)
    gain_first, gain_second = small[0].reshape(1, width), small[1].reshape(1, width)
    gain_query = small[2, :, 0:head_shard].reshape(1, HEAD_DIM)
    gain_key = small[3, :, 0:head_shard].reshape(1, HEAD_DIM)

    feed_one = norm_rows(input_rows, gain_first)
    kv, raw_kv, latest = [], [], ()
    for h in range(2):
        part = project(
            feed_one, weights, cosine, sine, gain_key, groups, groups, 1, h * half_rows, half_rows, after=latest
        )
        kv.append(part[0])
        raw_kv.append(part[1])
        latest = (part[0],)
        if pair and h == 0:
            half_width = width // 2
            sent = lax.dynamic_slice(
                behind(weights, part[0]), (core_at * half_width, 2 * columns), (half_width, columns)
            )
            output_same = tp_swap(sent, "output_proj")
            latest = (sent,)
    across = [x_swap(kv[0], "kv0")]
    beside = [core_swap(kv[0], "kv0")]
    one_turned = turned(feed_one, "normed_one", after=(kv[1],))
    across.append(x_swap(behind(kv[1], across[0], one_turned[0]), "kv1"))
    beside.append(core_swap(kv[1], "kv1"))
    others = [(beside[0], across[0], core_swap(across[0], "kv0_across"))]
    q, raw_q = project(
        feed_one, weights, cosine, sine, gain_query, groups, 0, 2, 0, tokens,
        after=(one_turned[0], beside[0], across[0], beside[1]),
    )
    found = [attend(orders, q, kv[0], others[0], 0, half_seqs, local)]
    attended = [found[0][0]]
    arrived = behind(across[1], attended[0])
    shard_two = behind(shard_two, arrived)
    others.append((beside[1], arrived, core_swap(arrived, "kv1_across")))
    weights_two = lax.all_gather(shard_two, ("dp", "ctx"), axis=0, tiled=True)

    settled = (attended[0],)
    if pair:
        output_swapped = core_swap(behind(output_same, arrived), "output_proj")
        settled += (output_swapped,)
    found.append(attend(orders, q, kv[1], others[1], half_seqs, half_seqs, local, after=settled))
    attended, probs = [list(parts) for parts in zip(*found)]
    joined = None
    attended_pair = attended, [core_swap(part, "attended") for part in attended]
    if pair:
        other_heads = [tp_swap(part, f"attended{h}") for h, part in enumerate(attended)]
        for h in range(2):
            joined = output_join(
                spot, input_rows, attended[h], other_heads[h], weights, 2,
                output_same, output_swapped, gain_second, h * half_rows, joined,
            )
    else:
        for h in range(2):
            part = nt_product([(attended[h], weights, 2 * columns)], 0, half_rows)
            started = tp_start(part, f"attended{h}")
            joined = join(input_rows, *started, gain_second, h * half_rows, joined)
    middle, feed_two = joined

    cut = width // 4
    tile = min(512, third)

    class Gradient:
        def __init__(self, name, parts, after=()):
            self.name = name
            to_x, self.keep = grad_product(parts, tile, (cut, cut), after=after)
            self.from_x = x_swap(to_x, name)

    def over_dp(name, grads, after=()):
        summed = add_rows([(grad.keep, grad.from_x) for grad in grads], after=after)
        with jax.named_scope(name + "_over_dp"):
            return summed, lax.psum_scatter(summed, "dp", scatter_dimension=0, tiled=True)

    def with_core(values, name):
        return [([value], [core_swap(value, name)]) for value in values]

    names = ("hidden", "gate_back", "up_back")
    starts = [3 * columns + at * third for at in range(3)]
    settled = (*attended_pair[1], one_turned[1])
    two_turned = turned(feed_two, "normed_two", after=settled)
    acts = feed(feed_two, cot_rows, weights, starts, min(256, third), third, 1, after=(two_turned[0],))
    firsts = [([a[0]], [core_swap(a[0], n + "_one")]) for a, n in zip(acts, names)]
    parts = [(cot_turned, firsts[0]), (two_turned, firsts[1]), (two_turned, firsts[2])]
    first_third = Gradient("first_third", parts)
    starts = [at * 2 * third for at in range(3)]
    acts = feed(
        feed_two, cot_rows, weights_two, starts, min(256, third), 2 * third, 1, after=(first_third.keep,)
    )
    seconds = [([a[0]], [core_swap(a[0], n + "_two")]) for a, n in zip(acts, names)]

    def feed_terms(at, kind):
        place = 3 * columns + kind * third
        return [(firsts[at][0][0], weights, place), (seconds[at][0][0], weights_two, 2 * kind * third)]

    back_terms = feed_terms(1, 0) + feed_terms(2, 1)
    back, out_started = [], []
    part = nt_product(back_terms, 0, half_rows)
    back.append(tp_start(part, "back0"))
    down_two = Gradient("down_two", [(cot_turned, seconds[0])], after=(part,))
    landed = (seconds[1][1][0], seconds[2][1][0])
    part = nt_product(back_terms, half_rows, half_rows, after=(down_two.keep, *landed))
    back.append(tp_start(part, "back1"))
    done, first_out = over_dp("first_third", [first_third], after=(part,))
    gate_two = Gradient("gate_two", [(two_turned, seconds[1])], after=(done,))

    def out_half(h, after):
        part = nt_product(feed_terms(0, 2), h * half_rows, half_rows, after=after)
        out_started.append(tp_start(part, f"out{h}"))
        return part

    grads, q_back, k_back, pieces, one = None, None, None, [], []
    sums = {"second": 0.0, "query": 0.0, "key": 0.0, "first": 0.0}

    def middle_half(h, after):
        *found, second = norm_back(
            middle, cot_rows, *back[h], gain_second, h * half_rows, (F32, BF16), grads, after=after
        )
        sums["second"] = sums["second"] + jnp.sum(second, axis=0)
        return found, nn_product(found[1], weights, 2 * columns, columns, h * half_rows, half_rows)

    def attention_half(h, grad_attended, after):
        found, to_own, to_x, to_core, query = attend_back(
            q, kv[h], others[h], probs[h], grad_attended, raw_q, cosine, sine, gain_query,
            h * half_seqs, half_seqs, local, q_back, after=after,
        )
        sums["query"] = sums["query"] + jnp.sum(query, axis=0)
        return found, to_own, to_x, core_swap(to_core, f"kv_grad{h}")

    def send_keys(h, held, after):
        to_own, to_x, from_core = held
        sent = add_rows([(to_x, from_core)], after=after)
        pieces.append((to_own, from_core, x_swap(sent, f"kv_grad{h}")))
        return sent

    def key_half(h, after):
        found, key = key_back(
            *pieces[h], raw_kv[h], cosine, sine, gain_key, h * half_seqs, half_seqs, local,
            tokens, k_back, after=after,
        )
        sums["key"] = sums["key"] + jnp.sum(key, axis=0)
        return found

    def one_half(h, after):
        terms = [(q_back, weights, 0), (k_back, weights, columns)]
        part = nt_product(terms, h * half_rows, half_rows, after=after)
        one.append(tp_start(part, f"one{h}"))
        return part

    grads, grad_attended = middle_half(0, (gate_two.keep,))
    part = out_half(0, (grad_attended,))
    q_back, *held = attention_half(0, grad_attended, (part,))
    grads, grad_attended = middle_half(1, (held[0],))
    grad_middle, middle_low = grads
    low_turned = turned(middle_low, "grad_middle", after=(grad_attended, gate_two.from_x))
    sent = send_keys(0, held, (low_turned[0],))
    done, more_out = over_dp("down_gate_two", [down_two, gate_two], after=(sent, first_out))
    output_grad = Gradient("output", [(low_turned, attended_pair)], after=(done,))
    part = out_half(1, (output_grad.keep,))
    landed = (part, out_started[0][1])
    up_two = Gradient("up_two", [(two_turned, seconds[2])], after=landed)
    k_back = key_half(0, (up_two.keep,))
    part = one_half(0, (output_grad.from_x,))
    q_back, *held = attention_half(1, grad_attended, (part,))
    q_pair = [q_back], [core_swap(q_back, "query_back")]
    outputs = sum_rows(middle, out_started[0], 0, None, after=(held[0],))
    sent = send_keys(1, held, (outputs,))
    query_grad = Gradient("query", [(one_turned, q_pair)], after=(sent,))
    done, output_out = over_dp("output", [output_grad], after=(query_grad.keep, more_out))
    done, up_out = over_dp("up_two", [up_two], after=(done,))
    outputs = sum_rows(middle, out_started[1], half_rows, outputs, after=(done,))
    terms = gain_terms(input_rows, one[0][0], 0, after=(outputs,))
    k_back = key_half(1, (terms,))
    part = one_half(1, ())
    k_pair = [k_back], [core_swap(k_back, "key_back")]
    key_grad = Gradient("key", [(one_turned, k_pair)], after=(part,))

    def input_half(h, into, after, cost):
        return norm_back(
            input_rows, grad_middle, *one[h], gain_first, h * half_rows, (BF16,), into, after=after, cost=cost
        )[0:1]

    result = input_half(0, None, (key_grad.keep, query_grad.from_x), 7.5)
    done, heads_out = over_dp("query_key", [query_grad, key_grad], after=(result[0],))
    part = gain_terms(input_rows, one[1][0], half_rows, after=(done,))
    sums["first"] = jnp.sum(terms + part, axis=0)

    if not pair:
        sums["first"], sums["second"] = sums["first"] / tp_size, sums["second"] / tp_size
    places = dp_size * 4
    totals = [sums[name].reshape(places, -1) for name in ("first", "second", "query", "key")]
    totals = jnp.concatenate(totals, axis=1)
    totals = jnp.broadcast_to(totals[:, None, :], (places, tp_size, totals.shape[1]))
    totals = totals.reshape(places * tp_size, -1)
    totals = lax.all_to_all(totals, ("dp", "ctx", "tp"), 0, 0, tiled=True)

    result = input_half(1, result, (part,), 300)
    totals = jnp.sum(behind(totals, result[0]), axis=0)
    grad_kv = heads_out[:, columns:].astype(F32)
    down_out, gate_out, up_first = [first_out[:, at * third : (at + 1) * third] for at in range(3)]
    beside = lambda left, right: jnp.concatenate([left, right], axis=1).astype(F32)
    return (
        outputs.reshape(inputs.shape),
        result[0].reshape(inputs.shape),
        totals[0:shard],
        heads_out[:, 0:columns].astype(F32),
        split_heads(grad_kv, 0),
        split_heads(grad_kv, 1),
        totals[2 * shard : 2 * shard + head_shard],
        totals[2 * shard + head_shard :],
        output_out.astype(F32).T,
        totals[shard : 2 * shard],
        beside(gate_out, more_out[:, 2 * third :]),
        beside(up_first, up_out),
        beside(down_out, more_out[:, 0 : 2 * third]).T,
    )


def solution(mesh):
    rows = P(("dp", "ctx"))
    columns = P(("dp", "ctx"), "tp")
    turned = P("tp", ("dp", "ctx"))
    tokens = P("dp", "ctx", None)
    in_specs = (
        (tokens, P("dp", None), rows, columns, columns, columns, rows, rows, turned, rows)
        + (columns, columns, turned, tokens)
    )
    out_specs = (
        (tokens, tokens, rows, columns, columns, columns, rows, rows, turned, rows)
        + (columns, columns, turned)
    )
    return jax.shard_map(shards, mesh=mesh, in_specs=in_specs, out_specs=out_specs, check_vma=False)
```

```python
import functools

import jax
import jax.numpy as jnp
from jax import lax
from jax.experimental import pallas as pl
from jax.experimental.pallas import tpu as pltpu
from jax.sharding import PartitionSpec as P

HEAD_DIM = 128
GROUP = 2 * HEAD_DIM
BLOCK = 128
EPSILON = 1e-06
ROPE_BASE = 1000000.0
MASKED = -1e30
VMEM_LIMIT = 56 * 1024 * 1024
F32 = jnp.float32
BF16 = jnp.bfloat16
FLOPS_PER_US = 1e10

CORE_SWAP = [(0, 1), (1, 0), (2, 3), (3, 2)]
X_SWAP = [(0, 2), (2, 0), (1, 3), (3, 1)]
TP_SWAP = [(0, 1), (1, 0)]


def nn(left, right):
    return lax.dot_general(left, right, (((1,), (0,)), ((), ())), preferred_element_type=F32)


def nt(left, right):
    return lax.dot_general(left, right, (((1,), (1,)), ((), ())), preferred_element_type=F32)


def tn(left, right):
    return lax.dot_general(left, right, (((0,), (0,)), ((), ())), preferred_element_type=F32)


def unit_norm(values):
    inverse = lax.rsqrt(jnp.mean(values * values, axis=-1, keepdims=True) + EPSILON)
    return values * inverse, inverse


def swap_halves(values):
    return pltpu.roll(values, HEAD_DIM // 2, 1)


def call(kernel, grid, ins, outs, scratch=(), scalars=(), alias=None, after=(), name=None, cost=1.0):
    any_space = pl.BlockSpec(memory_space=pl.ANY)
    specs = [any_space if b is None else pl.BlockSpec(b, m) for _, b, m in ins]
    n_in, n_after, n_scalar = len(ins), len(after), len(scalars)

    def body(*refs):
        keep = refs[: n_scalar + n_in] + refs[n_scalar + n_in + n_after :]
        kernel(*keep)

    return pl.pallas_call(
        body,
        grid_spec=pltpu.PrefetchScalarGridSpec(
            num_scalar_prefetch=n_scalar,
            grid=grid,
            in_specs=specs + [any_space] * n_after,
            out_specs=[pl.BlockSpec(b, m) for _, _, b, m in outs],
            scratch_shapes=list(scratch),
        ),
        out_shape=[jax.ShapeDtypeStruct(s, d) for s, d, _, _ in outs],
        input_output_aliases={n_scalar + i: o for o, i in (alias or {}).items()},
        compiler_params=pltpu.CompilerParams(
            dimension_semantics=("arbitrary",) * len(grid), vmem_limit_bytes=VMEM_LIMIT
        ),
        cost_estimate=pl.CostEstimate(
            flops=int(cost * FLOPS_PER_US), bytes_accessed=0, transcendentals=0
        ),
        name=name,
    )(*scalars, *[a for a, _, _ in ins], *after)


def pack_first_kernel(q_ref, k_ref, v_ref, o_ref, g_ref, u_ref, d_ref, small_ref, out_ref):
    columns, third = q_ref.shape[1], g_ref.shape[1]
    out_ref[:, 0:columns] = q_ref[...]
    for at in range(columns // GROUP):
        cut = slice(at * HEAD_DIM, (at + 1) * HEAD_DIM)
        start = columns + at * GROUP
        out_ref[:, start : start + HEAD_DIM] = k_ref[:, cut]
        out_ref[:, start + HEAD_DIM : start + GROUP] = v_ref[:, cut]
    out_ref[:, 2 * columns : 3 * columns] = o_ref[...].T
    start = 3 * columns
    out_ref[:, start : start + third] = g_ref[...]
    out_ref[:, start + third : start + 2 * third] = u_ref[...]
    out_ref[:, start + 2 * third : start + 3 * third] = d_ref[...].T
    out_ref[:, start + 3 * third :] = small_ref[...]


def pack_first(q, k, v, o, g, u, d, small, third):
    shard, columns = q.shape
    whole = lambda array: (array, array.shape, lambda j: (0, 0))
    total = 3 * columns + 3 * third + BLOCK
    return call(
        pack_first_kernel,
        (1,),
        [whole(q), whole(k), whole(v), whole(o)]
        + [(g, (shard, third), lambda j: (0, 0)), (u, (shard, third), lambda j: (0, 0))]
        + [(d, (third, shard), lambda j: (0, 0)), whole(small)],
        [((shard, total), BF16, (shard, total), lambda j: (0, 0))],
        name="pack_first",
        cost=3,
    )[0]


def pack_second_kernel(g_ref, u_ref, d_ref, out_ref):
    step = pl.program_id(0)
    part = step // 2

    @pl.when(part == 0)
    def _():
        out_ref[...] = g_ref[...]

    @pl.when(part == 1)
    def _():
        out_ref[...] = u_ref[...]

    @pl.when(part == 2)
    def _():
        out_ref[...] = d_ref[...].T


def pack_second(g, u, d, third, after=()):
    shard = g.shape[0]
    return call(
        pack_second_kernel,
        (6,),
        [(g, (shard, third), lambda j: (0, 1 + j % 2)), (u, (shard, third), lambda j: (0, 1 + j % 2))]
        + [(d, (third, shard), lambda j: (1 + j % 2, 0))],
        [((shard, 6 * third), BF16, (shard, third), lambda j: (0, j))],
        after=after,
        name="pack_second",
        cost=5,
    )[0]


def norm_kernel(x_ref, gain_ref, *rest):
    rest[-1][...] = (unit_norm(x_ref[...].astype(F32))[0] * gain_ref[...]).astype(BF16)


def norm_rows(x, gain, row, rows, into, after=()):
    tokens, width = x.shape
    tile = min(256, rows)
    block = (tile, width)
    spot = lambda j: (row // tile + j, 0)
    ins = [(x, block, spot), (gain, (1, width), lambda j: (0, 0))]
    if into is not None:
        ins.append((into, None, None))
    return call(
        norm_kernel,
        (rows // tile,),
        ins,
        [((tokens, width), BF16, block, spot)],
        alias=None if into is None else {0: len(ins) - 1},
        after=after,
        name="norm_rows",
        cost=3,
    )[0]


def project_kernel(x_ref, w_ref, cos_ref, sin_ref, gain_ref, out_ref, raw_ref, *, turned, rows):
    for at in range(0, x_ref.shape[0], rows):
        part = pl.ds(at, rows)
        raw = nn(x_ref[part, :], w_ref[...])
        raw_ref[part, :] = raw
        cosine, sine = cos_ref[part, :], sin_ref[part, :]
        for head in range(2):
            values = raw[:, head * HEAD_DIM : (head + 1) * HEAD_DIM]
            if head < turned:
                scaled = unit_norm(values)[0] * gain_ref[...]
                values = scaled * cosine + swap_halves(scaled) * sine
            out_ref[part, head * HEAD_DIM : (head + 1) * HEAD_DIM] = values.astype(BF16)


def project(x, weights, cosine, sine, gain, groups, first, turned, row, rows, after=()):
    width = x.shape[1]
    some = lambda j: (row // rows, 0)
    column = lambda j: (0, j)
    columns = groups * GROUP
    return call(
        functools.partial(project_kernel, turned=turned, rows=min(256, rows)),
        (groups,),
        [
            (x, (rows, width), some),
            (weights, (width, GROUP), lambda j: (0, first + j)),
            (cosine, (rows, HEAD_DIM), some),
            (sine, (rows, HEAD_DIM), some),
            (gain, (1, HEAD_DIM), lambda j: (0, 0)),
        ],
        [
            ((rows, columns), BF16, (rows, GROUP), column),
            ((rows, columns), F32, (rows, GROUP), column),
        ],
        after=after,
        name="project",
        cost=10,
    )


def span_places(orders_ref, seq, piece, span, shape, dim):
    index = lax.broadcasted_iota(jnp.int32, shape, dim)
    first, second = orders_ref[seq, 2 * piece], orders_ref[seq, 2 * piece + 1]
    return jnp.where(index < span, first * span + index, second * span + index - span)


def stacked_heads(block):
    return jnp.concatenate([block[:, 0:HEAD_DIM], block[:, HEAD_DIM:GROUP]], axis=0)


def masked_exponents(orders_ref, seq, query, pieces, span):
    rows, keys = query.shape[0], pieces[0].shape[0]
    scale = HEAD_DIM**-0.5
    places = span_places(orders_ref, seq, 0, span, (rows // 2, 1), 0)
    places = jnp.concatenate([places, places], axis=0)
    scores = []
    for at, piece in enumerate(pieces):
        key_places = span_places(orders_ref, seq, at, span, (1, keys), 1)
        product = nt(query, piece[:, 0:HEAD_DIM]) * scale
        scores.append(jnp.where(key_places <= places, product, MASKED))
    peak = functools.reduce(jnp.maximum, [jnp.max(s, axis=1, keepdims=True) for s in scores])
    exponents = [jnp.exp(s - peak) for s in scores]
    total = functools.reduce(jnp.add, [jnp.sum(e, axis=1, keepdims=True) for e in exponents])
    return exponents, 1.0 / total


def attend_kernel(orders_ref, q_ref, own_ref, core_ref, x_ref, diag_ref, out_ref, prob_ref, *, first, span):
    seq = pl.program_id(0) + first
    local = q_ref.shape[0]
    for group in range(q_ref.shape[1] // GROUP):
        columns = slice(group * GROUP, (group + 1) * GROUP)
        rows = slice(group * 2 * local, (group + 1) * 2 * local)
        query = stacked_heads(q_ref[:, columns])
        pieces = [ref[:, columns] for ref in (own_ref, core_ref, x_ref, diag_ref)]
        exponents, inverse = masked_exponents(orders_ref, seq, query, pieces, span)
        total = None
        for at, (exponent, piece) in enumerate(zip(exponents, pieces)):
            prob = (exponent * inverse).astype(BF16)
            prob_ref[0, rows, at * local : (at + 1) * local] = prob
            product = nn(prob, piece[:, HEAD_DIM:GROUP])
            total = product if total is None else total + product
        result = total.astype(BF16)
        for head in range(2):
            start = group * GROUP + head * HEAD_DIM
            out_ref[:, start : start + HEAD_DIM] = result[head * local : (head + 1) * local]


def attend(orders, q, kv, others, first, count, local, after=()):
    columns = q.shape[1]
    block = (local, columns)
    at_whole = lambda s, o: (s + first, 0)
    at_half = lambda s, o: (s, 0)
    ins = [(q, block, at_whole), (kv, block, at_half)] + [(k, block, at_half) for k in others]
    prob = (1, columns // GROUP * 2 * local, 4 * local)
    return call(
        functools.partial(attend_kernel, first=first, span=local // 2),
        (count,),
        ins,
        [
            ((count * local, columns), BF16, block, at_half),
            ((count,) + prob[1:], BF16, prob, lambda s, o: (s, 0, 0)),
        ],
        scalars=(orders,),
        after=after,
        name="attend",
        cost=11,
    )


def turn_back(grad, raw, cosine, sine, gain):
    turned = grad * cosine - swap_halves(grad) * sine
    unit, inverse = unit_norm(raw)
    grad_normed = turned * gain
    mean = jnp.mean(grad_normed * unit, axis=-1, keepdims=True)
    terms = jnp.sum((turned * unit).reshape(-1, 8, HEAD_DIM), axis=0)
    return (inverse * (grad_normed - unit * mean)).astype(BF16), terms


def clear_at_start(ref, dims):
    start = functools.reduce(jnp.logical_and, [pl.program_id(d) == 0 for d in range(dims)])

    @pl.when(start)
    def _():
        ref[...] = jnp.zeros_like(ref)


def attend_back_kernel(
    q_ref, own_ref, core_ref, x_ref, diag_ref, prob_ref, grad_ref, raw_ref, cos_ref, sin_ref, gain_ref, *rest
):
    q_back_ref, own_out, x_out, core_out, gain_out = rest[-5:]
    clear_at_start(gain_out, 1)
    scale = HEAD_DIM**-0.5
    local = q_ref.shape[0]
    outs = (own_out, core_out.at[0], x_out, core_out.at[1])
    for group in range(q_ref.shape[1] // GROUP):
        start = group * GROUP
        both = slice(start, start + GROUP)
        rows = slice(group * 2 * local, (group + 1) * 2 * local)
        query = stacked_heads(q_ref[:, both])
        grad = stacked_heads(grad_ref[:, both])
        pieces = [ref[:, both] for ref in (own_ref, core_ref, x_ref, diag_ref)]
        lows = [prob_ref[0, rows, at * local : (at + 1) * local] for at in range(4)]
        products = [low.astype(F32) * nt(grad, p[:, HEAD_DIM:GROUP]) for low, p in zip(lows, pieces)]
        delta = functools.reduce(jnp.add, [jnp.sum(p, axis=1, keepdims=True) for p in products])
        grad_scores = [(p - low.astype(F32) * delta).astype(BF16) for p, low in zip(products, lows)]
        grad_query = functools.reduce(
            jnp.add, [nn(s, p[:, 0:HEAD_DIM]) for s, p in zip(grad_scores, pieces)]
        )
        for out, scores, low in zip(outs, grad_scores, lows):
            out[:, start : start + HEAD_DIM] = (tn(scores, query) * scale).astype(BF16)
            out[:, start + HEAD_DIM : start + GROUP] = tn(low, grad).astype(BF16)
        for head in range(2):
            columns = slice(start + head * HEAD_DIM, start + (head + 1) * HEAD_DIM)
            result, terms = turn_back(
                grad_query[head * local : (head + 1) * local] * scale,
                raw_ref[:, columns],
                cos_ref[...],
                sin_ref[...],
                gain_ref[...],
            )
            q_back_ref[:, columns] = result
            gain_out[...] += terms


def attend_back(q, kv, others, prob, grad, raw, cosine, sine, gain, first, count, local, into, after=()):
    columns = q.shape[1]
    block = (local, columns)
    at_whole = lambda s: (s + first, 0)
    at_half = lambda s: (s, 0)
    fixed = lambda s: (0, 0)
    ins = [(q, block, at_whole), (kv, block, at_half)] + [(k, block, at_half) for k in others]
    ins += [(prob, (1,) + prob.shape[1:], lambda s: (s, 0, 0))]
    ins += [(grad, block, at_half), (raw, block, at_whole)]
    ins += [(cosine, (local, HEAD_DIM), at_whole), (sine, (local, HEAD_DIM), at_whole)]
    ins += [(gain, (1, HEAD_DIM), fixed)]
    if into is not None:
        ins.append((into, None, None))
    piece = ((count * local, columns), BF16, block, at_half)
    return call(
        attend_back_kernel,
        (count,),
        ins,
        [(q.shape, BF16, block, at_whole)]
        + [piece] * 2
        + [((2, count * local, columns), BF16, (2, local, columns), lambda s: (0, s, 0))]
        + [((8, HEAD_DIM), F32, (8, HEAD_DIM), fixed)],
        alias=None if into is None else {0: len(ins) - 1},
        after=after,
        name="attend_back",
        cost=25,
    )


def key_back_kernel(mine_ref, core_ref, x_ref, raw_ref, cos_ref, sin_ref, gain_ref, *rest):
    out_ref, gain_out = rest[-2:]
    clear_at_start(gain_out, 1)
    for group in range(mine_ref.shape[1] // GROUP):
        start = group * GROUP
        both = slice(start, start + GROUP)
        parts = [ref[:, both].astype(F32) for ref in (mine_ref, core_ref.at[0], x_ref)]
        grad = functools.reduce(jnp.add, parts)
        result, terms = turn_back(
            grad[:, 0:HEAD_DIM],
            raw_ref[:, start : start + HEAD_DIM],
            cos_ref[...],
            sin_ref[...],
            gain_ref[...],
        )
        out_ref[:, start : start + HEAD_DIM] = result
        out_ref[:, start + HEAD_DIM : start + GROUP] = grad[:, HEAD_DIM:GROUP].astype(BF16)
        gain_out[...] += terms


def key_back(mine, core, x, raw, cosine, sine, gain, first, count, local, tokens, into, after=()):
    columns = mine.shape[1]
    block = (local, columns)
    at_whole = lambda s: (s + first, 0)
    at_half = lambda s: (s, 0)
    fixed = lambda s: (0, 0)
    ins = [(mine, block, at_half), (core, (1,) + block, lambda s: (0, s, 0)), (x, block, at_half)]
    ins += [(raw, block, at_half)]
    ins += [(cosine, (local, HEAD_DIM), at_whole), (sine, (local, HEAD_DIM), at_whole)]
    ins += [(gain, (1, HEAD_DIM), fixed)]
    if into is not None:
        ins.append((into, None, None))
    return call(
        key_back_kernel,
        (count,),
        ins,
        [
            ((tokens, columns), BF16, block, at_whole),
            ((8, HEAD_DIM), F32, (8, HEAD_DIM), fixed),
        ],
        alias=None if into is None else {0: len(ins) - 1},
        after=after,
        name="key_back",
        cost=5,
    )


def feed_kernel(x_ref, c_ref, g_ref, u_ref, d_ref, *outs, rows, steps):
    step, pieces = pl.program_id(0), len(outs) // 3

    def fill(hidden_ref, gate_ref, up_ref):
        for at in range(0, x_ref.shape[0], rows):
            part = pl.ds(at, rows)
            gate = nn(x_ref[part, :], g_ref[...])
            upward = nn(x_ref[part, :], u_ref[...])
            grad = nn(c_ref[part, :], d_ref[...])
            sigmoid = jax.nn.sigmoid(gate)
            silu = gate * sigmoid
            hidden_ref[part, :] = (silu * upward).astype(BF16)
            slope = sigmoid + silu * (1.0 - sigmoid)
            gate_ref[part, :] = (grad * upward * slope).astype(BF16)
            up_ref[part, :] = (grad * silu).astype(BF16)

    for piece in range(pieces):
        run = functools.partial(fill, *outs[piece::pieces])
        if pieces == 1:
            run()
        else:
            pl.when(step // steps == piece)(run)


def feed(x, c, weights, starts, tile, piece, pieces, after=()):
    tokens, width = x.shape
    steps = piece // tile
    whole = lambda j: (0, 0)
    ins = [(x, (tokens, width), whole), (c, (tokens, width), whole)]
    for start in starts:
        ins.append((weights, (width, tile), lambda j, start=start: (0, start // tile + j)))
    outs = [
        ((tokens, piece), BF16, (tokens, tile), lambda j, at=at: (0, jnp.clip(j - at * steps, 0, steps - 1)))
        for _ in range(3)
        for at in range(pieces)
    ]
    found = call(
        functools.partial(feed_kernel, rows=min(256, tokens), steps=steps),
        (steps * pieces,),
        ins,
        outs,
        after=after,
        name="feed",
        cost=2 + piece * pieces * 0.0165,
    )
    return [found[kind * pieces : (kind + 1) * pieces] for kind in range(3)]


def nt_kernel(*refs, count):
    out_ref = refs[-1]
    total = None
    for left_ref, w_ref in zip(refs[:count], refs[count : 2 * count]):
        product = nt(left_ref[...], w_ref[...])
        total = product if total is None else total + product
    out_ref[...] = total.astype(out_ref.dtype)


def nt_product(terms, row, rows, after=()):
    width = terms[0][1].shape[0]
    tile = min(512, width)
    ins = [(left, (rows, left.shape[1]), lambda j: (row // rows, 0)) for left, _, _ in terms]
    ins += [
        (weights, (tile, left.shape[1]), lambda j, at=at // left.shape[1]: (j, at))
        for left, weights, at in terms
    ]
    return call(
        functools.partial(nt_kernel, count=len(terms)),
        (width // tile,),
        ins,
        [((rows, width), BF16, (rows, tile), lambda j: (0, j))],
        after=after,
        name="nt_product",
        cost=1.5 + rows * sum(left.shape[1] for left, _, _ in terms) * 6.0e-6,
    )[0]


def nn_kernel(x_ref, w_ref, out_ref):
    out_ref[...] = nn(x_ref[...], w_ref[...]).astype(out_ref.dtype)


def nn_product(left, weights, first_column, columns, row, rows, after=()):
    width = weights.shape[0]
    tile = min(512, columns)
    return call(
        nn_kernel,
        (columns // tile,),
        [
            (left, (rows, width), lambda j: (row // rows, 0)),
            (weights, (width, tile), lambda j: (0, first_column // tile + j)),
        ],
        [((rows, columns), BF16, (rows, tile), lambda j: (0, j))],
        after=after,
        name="nn_product",
        cost=6,
    )[0]


def output_join_kernel(
    at_ref, x_ref, mine_ref, other_ref, w_mine_ref, w_same_ref, w_swap_ref, gain_ref, *rest, steps
):
    middle_ref, normed_ref, rows_ref = rest[-3:]
    step = pl.program_id(0)
    tile = x_ref.shape[1]
    is_first, core = at_ref[0] == 0, at_ref[1]
    direct = (step * 2 // steps) == core
    mine, other, w_mine = mine_ref[...], other_ref[...], w_mine_ref[...]
    w_other = jnp.where(direct, w_same_ref[...], w_swap_ref[...])
    total = nt(jnp.where(is_first, mine, other), jnp.where(is_first, w_mine, w_other))
    total += nt(jnp.where(is_first, other, mine), jnp.where(is_first, w_other, w_mine))
    columns = pl.ds(pl.multiple_of(step * tile, tile), tile)
    rows_ref[:, columns] = x_ref[...].astype(F32) + total

    @pl.when(step == steps - 1)
    def _():
        middle = rows_ref[...]
        middle_ref[...] = middle
        normed_ref[...] = (unit_norm(middle)[0] * gain_ref[...]).astype(BF16)


def output_join(at, x, mine, other, weights, block, same, swapped, gain, row, into, after=()):
    tokens, width = x.shape
    rows, columns = mine.shape
    tile = min(512, width // 2)
    steps = width // tile
    fixed = lambda j, a: (0, 0)
    fetched = lambda j, a: (j % (steps // 2), 0)
    ins = [
        (x, (rows, tile), lambda j, a: (row // rows, j)),
        (mine, (rows, columns), fixed),
        (other, (rows, columns), fixed),
        (weights, (tile, columns), lambda j, a: (j, block)),
        (same, (tile, columns), fetched),
        (swapped, (tile, columns), fetched),
        (gain, (1, width), fixed),
    ]
    alias = None
    if into is not None:
        alias = {o: len(ins) + o for o in range(2)}
        ins += [(array, None, None) for array in into]
    out = lambda kind: ((tokens, width), kind, (rows, width), lambda j, a: (row // rows, 0))
    return call(
        functools.partial(output_join_kernel, steps=steps),
        (steps,),
        ins,
        [out(F32), out(BF16)],
        scratch=[pltpu.VMEM((rows, width), F32)],
        scalars=(at,),
        alias=alias,
        after=after,
        name="output_join",
        cost=15,
    )


def turn_kernel(order_ref, *refs):
    ins, outs = refs[:4], refs[4:]
    step = pl.program_id(0)

    def fill(out_ref):
        for at, ref in enumerate(ins):
            out_ref[at * BLOCK : (at + 1) * BLOCK, :] = ref[...].T

    pl.when(step < 2)(lambda: fill(outs[0]))
    pl.when(step >= 2)(lambda: fill(outs[1]))


def turned_blocks(order, left, after=()):
    tokens, width = left.shape
    ins = [(left, (tokens, BLOCK), lambda j, o, at=at: (0, o[4 * j + at])) for at in range(4)]
    out = lambda spot: ((width // 2, tokens), BF16, (4 * BLOCK, tokens), spot)
    return call(
        turn_kernel,
        (width // BLOCK // 4,),
        ins,
        [out(lambda j, o: (jnp.minimum(j, 1), 0)), out(lambda j, o: (jnp.maximum(j - 2, 0), 0))],
        scalars=(order,),
        after=after,
        name="turned_blocks",
        cost=6,
    )


def grad_kernel(*refs, plan, outs):
    step, begin, used = pl.program_id(0), 0, 0
    out_refs = refs[-outs:]

    def fill(left_refs, right_refs):
        for at, out in enumerate(out_refs):
            size, total = out.shape[0], None
            rows = pl.ds(at * size, size)
            for left_ref, pieces in zip(left_refs, right_refs):
                start = 0
                for piece in pieces:
                    tokens = piece.shape[0]
                    product = nn(left_ref[rows, start : start + tokens], piece[...])
                    total = product if total is None else total + product
                    start += tokens
            out[...] = total.astype(BF16)

    for pieces, count in plan:
        part = refs[used : used + 2 + 2 * pieces]
        run = functools.partial(fill, part[:2], (part[2 : 2 + pieces], part[2 + pieces :]))
        if len(plan) == 1:
            run()
        else:
            pl.when((step >= begin) & (step < begin + count))(run)
        begin, used = begin + count, used + 2 + 2 * pieces


def grad_product(parts, tile, cuts, after=()):
    width, tokens = parts[0][0][0].shape
    ins, begin, plan = [], 0, []
    for lefts, rights in parts:
        count = rights[0][0].shape[1] // tile
        ins += [(left, left.shape, lambda j: (0, 0)) for left in lefts]
        spot = lambda j, begin=begin, count=count: (0, jnp.clip(j - begin, 0, count - 1))
        ins += [(piece, (piece.shape[0], tile), spot) for pieces in rights for piece in pieces]
        plan.append((len(rights[0]), count))
        begin += count
    return call(
        functools.partial(grad_kernel, plan=plan, outs=len(cuts)),
        (begin,),
        ins,
        [((cut, begin * tile), BF16, (cut, tile), lambda j: (0, j)) for cut in cuts],
        after=after,
        name="grad_product",
        cost=3.5 + begin * tile * 0.0047,
    )


def join_kernel(x_ref, own_ref, other_ref, gain_ref, *rest):
    middle_ref, normed_ref = rest[-2:]
    middle = x_ref[...].astype(F32) + (own_ref[...].astype(F32) + other_ref[...].astype(F32))
    middle_ref[...] = middle
    normed_ref[...] = (unit_norm(middle)[0] * gain_ref[...]).astype(BF16)


def join(x, own, other, gain, row, into, after=()):
    tokens, width = x.shape
    rows = own.shape[0]
    tile = min(256, rows)
    block = (tile, width)
    at_whole = lambda j: (row // tile + j, 0)
    at_half = lambda j: (j, 0)
    ins = [(x, block, at_whole), (own, block, at_half), (other, block, at_half)]
    ins += [(gain, (1, width), lambda j: (0, 0))]
    alias = None
    if into is not None:
        alias = {o: len(ins) + o for o in range(2)}
        ins += [(array, None, None) for array in into]
    return call(
        join_kernel,
        (rows // tile,),
        ins,
        [((tokens, width), F32, block, at_whole), ((tokens, width), BF16, block, at_whole)],
        alias=alias,
        after=after,
        name="join",
        cost=7.5,
    )


def norm_back_kernel(v_ref, base_ref, own_ref, other_ref, gain_ref, *rest, outs):
    out_refs, terms_ref = rest[-outs - 1 : -1], rest[-1]
    clear_at_start(terms_ref, 1)
    own = own_ref[...].astype(F32)
    unit, inverse = unit_norm(v_ref[...].astype(F32))
    grad_normed = (own + other_ref[...].astype(F32)) * gain_ref[...]
    mean = jnp.mean(grad_normed * unit, axis=-1, keepdims=True)
    result = base_ref[...].astype(F32) + inverse * (grad_normed - unit * mean)
    for ref in out_refs:
        ref[...] = result.astype(ref.dtype)
    terms_ref[...] += jnp.sum((own * unit).reshape(-1, 8, own.shape[1]), axis=0)


def norm_back(values, base, own, other, gain, row, types, into, after=(), cost=7.5):
    tokens, width = values.shape
    rows = own.shape[0]
    tile = min(256, rows)
    block = (tile, width)
    at_whole = lambda j: (row // tile + j, 0)
    at_half = lambda j: (j, 0)
    fixed = lambda j: (0, 0)
    ins = [(values, block, at_whole), (base, block, at_whole)]
    ins += [(own, block, at_half), (other, block, at_half), (gain, (1, width), fixed)]
    alias = None
    if into is not None:
        alias = {o: len(ins) + o for o in range(len(types))}
        ins += [(array, None, None) for array in into]
    return call(
        functools.partial(norm_back_kernel, outs=len(types)),
        (rows // tile,),
        ins,
        [((tokens, width), kind, block, at_whole) for kind in types]
        + [((8, width), F32, (8, width), fixed)],
        alias=alias,
        after=after,
        name="norm_back",
        cost=cost,
    )


def sum_kernel(*refs):
    own, other = refs[1][...].astype(F32), refs[2][...].astype(F32)
    refs[-1][...] = (refs[0][...] + (own + other)).astype(BF16)


def sum_rows(values, parts, row, into, after=()):
    tokens, width = values.shape
    rows = parts[0].shape[0]
    tile = min(256, rows)
    block = (tile, width)
    at_whole = lambda j: (row // tile + j, 0)
    ins = [(values, block, at_whole)] + [(part, block, lambda j: (j, 0)) for part in parts]
    if into is not None:
        ins.append((into, None, None))
    return call(
        sum_kernel,
        (rows // tile,),
        ins,
        [((tokens, width), BF16, block, at_whole)],
        alias=None if into is None else {0: len(ins) - 1},
        after=after,
        name="sum_rows",
        cost=6,
    )[0]


def terms_kernel(v_ref, own_ref, terms_ref):
    clear_at_start(terms_ref, 1)
    unit = unit_norm(v_ref[...].astype(F32))[0]
    terms_ref[...] += jnp.sum((own_ref[...].astype(F32) * unit).reshape(-1, 8, unit.shape[1]), axis=0)


def gain_terms(values, own, row, after=()):
    width = values.shape[1]
    rows = own.shape[0]
    tile = min(256, rows)
    return call(
        terms_kernel,
        (rows // tile,),
        [
            (values, (tile, width), lambda j: (row // tile + j, 0)),
            (own, (tile, width), lambda j: (j, 0)),
        ],
        [((8, width), F32, (8, width), lambda j: (0, 0))],
        after=after,
        name="gain_terms",
        cost=4,
    )[0]


def add_kernel(*refs, widths):
    start = 0
    for at, width in enumerate(widths):
        left, right = refs[2 * at][...].astype(F32), refs[2 * at + 1][...].astype(F32)
        refs[-1][:, start : start + width] = (left + right.reshape(left.shape)).astype(BF16)
        start += width


def add_rows(parts, after=()):
    rows = parts[0][0].shape[0]
    widths = [left.shape[1] for left, _ in parts]
    tile, total = rows // 2, sum(widths)
    ins = []
    for left, right in parts:
        ins.append((left, (tile, left.shape[1]), lambda j: (j, 0)))
        if right.ndim == 3:
            ins.append((right, (1, tile, right.shape[2]), lambda j: (1, j, 0)))
        else:
            ins.append((right, (tile, right.shape[1]), lambda j: (j, 0)))
    return call(
        functools.partial(add_kernel, widths=widths),
        (2,),
        ins,
        [((rows, total), BF16, (tile, total), lambda j: (j, 0))],
        after=after,
        name="add_rows",
        cost=3,
    )[0]


def split_heads(both, which):
    cuts = range(which, both.shape[1] // HEAD_DIM, 2)
    return jnp.concatenate([both[:, at * HEAD_DIM : (at + 1) * HEAD_DIM] for at in cuts], axis=1)


def behind(value, *others):
    return lax.optimization_barrier((value,) + others)[0]


def shards(
    inputs,
    span_order,
    first_gain,
    query_proj,
    key_matrix,
    value_matrix,
    query_norm,
    key_norm,
    output_proj,
    second_gain,
    gate_proj,
    up_proj,
    down_proj,
    cotangent,
):
    seqs, local, width = inputs.shape
    tokens = seqs * local
    span = local // 2
    shard = query_proj.shape[0]
    head_shard = query_norm.shape[0]
    columns = query_proj.shape[1]
    groups = columns // GROUP
    units = gate_proj.shape[1]
    third = units // 3
    dp_size, tp_size = lax.axis_size("dp"), lax.axis_size("tp")
    ctx, tp_at = lax.axis_index("ctx"), lax.axis_index("tp")
    x_at, core_at = ctx // 2, ctx % 2
    half_rows = tokens // 2
    half_seqs = seqs // 2
    pair = tp_size == 2

    def swap(axis, pairs, value, name):
        with jax.named_scope(name):
            return lax.ppermute(value, axis, pairs)

    tp_swap = lambda value, name: swap("tp", TP_SWAP, value, name + "_over_tp")
    core_swap = lambda value, name: swap("ctx", CORE_SWAP, value, name + "_over_core")
    x_swap = lambda value, name: swap("ctx", X_SWAP, value, name + "_over_x")

    def tp_start(part, name):
        if pair:
            return part, tp_swap(part, name)
        return lax.psum(part, "tp"), jnp.zeros_like(part)

    small = [first_gain, second_gain, jnp.pad(query_norm, (0, shard - head_shard))]
    small += [jnp.pad(key_norm, (0, shard - head_shard))]
    small = jnp.pad(jnp.stack(small), ((0, shard - len(small)), (0, BLOCK - shard)))
    shard_one = pack_first(
        query_proj, key_matrix, value_matrix, output_proj, gate_proj, up_proj, down_proj, small, third
    )
    weights = lax.all_gather(shard_one, ("dp", "ctx"), axis=0, tiled=True)

    pairs = span_order.reshape(seqs, 4, 2)
    relative = jnp.stack([ctx, ctx ^ 1, ctx ^ 2, ctx ^ 3])
    orders = jnp.take(pairs, relative, axis=1).reshape(seqs, 8)
    places = (
        orders[:, 0:2, None] * span + jnp.arange(span, dtype=jnp.int32)[None, None, :]
    ).reshape(tokens)
    half_dim = HEAD_DIM // 2
    frequency = ROPE_BASE ** (-(jnp.arange(half_dim, dtype=F32) * (2.0 / HEAD_DIM)))
    angles = places.astype(F32)[:, None] * frequency[None, :]
    cosine, sine = jnp.cos(angles), jnp.sin(angles)
    cosine = jnp.concatenate([cosine, cosine], axis=1)
    sine = jnp.concatenate([-sine, sine], axis=1)
    dps = jnp.arange(dp_size, dtype=jnp.int32)
    other_first = jnp.stack([1 - x_at, x_at])
    cores = jnp.stack([1 - core_at, core_at])
    order = cores[:, None, None] + 2 * other_first[None, :, None] + 4 * dps[None, None, :]
    order = order.reshape(-1).astype(jnp.int32)
    spot = jnp.stack([tp_at, core_at]).astype(jnp.int32)
    input_rows = inputs.reshape(tokens, width)
    cot_rows = cotangent.reshape(tokens, width)
    shard_two = pack_second(gate_proj, up_proj, down_proj, third, after=(shard_one,))

    def turned(left, name, after=()):
        to_core, own = turned_blocks(order, left, after=after)
        return own, core_swap(to_core, name)

    cot_turned = turned(cot_rows, "cotangent", after=(shard_two,))
    weights, cosine, sine, orders, order, spot, cot_turned, shard_two = lax.optimization_barrier(
        (weights, cosine, sine, orders, order, spot, cot_turned, shard_two)
    )

    small = weights[:, 3 * columns + 3 * third :].reshape(-1, shard, BLOCK)[:, 0:4, 0:shard]
    small = jnp.transpose(small, (1, 0, 2)).astype(F32)
    gain_first, gain_second = small[0].reshape(1, width), small[1].reshape(1, width)
    gain_query = small[2, :, 0:head_shard].reshape(1, HEAD_DIM)
    gain_key = small[3, :, 0:head_shard].reshape(1, HEAD_DIM)

    feed_one = None
    kv, raw_kv, latest = [], [], ()
    for h in range(2):
        feed_one = norm_rows(input_rows, gain_first, h * half_rows, half_rows, feed_one, after=latest)
        part = project(
            feed_one, weights, cosine, sine, gain_key, groups, groups, 1, h * half_rows, half_rows, after=latest
        )
        kv.append(part[0])
        raw_kv.append(part[1])
        latest = (part[0],)
        if pair and h == 0:
            half_width = width // 2
            sent = lax.dynamic_slice(
                behind(weights, part[0]), (core_at * half_width, 2 * columns), (half_width, columns)
            )
            output_same = tp_swap(sent, "output_proj")
            latest = (sent,)
    across = [x_swap(kv[0], "kv0")]
    beside = [core_swap(kv[0], "kv0")]
    one_turned = turned(feed_one, "normed_one", after=(kv[1],))
    across.append(x_swap(behind(kv[1], across[0], one_turned[0]), "kv1"))
    beside.append(core_swap(kv[1], "kv1"))
    others = [(beside[0], across[0], core_swap(across[0], "kv0_across"))]
    q, raw_q = project(
        feed_one, weights, cosine, sine, gain_query, groups, 0, 2, 0, tokens,
        after=(one_turned[0], beside[0], across[0], beside[1]),
    )
    found = [attend(orders, q, kv[0], others[0], 0, half_seqs, local)]
    attended = [found[0][0]]
    arrived = behind(across[1], attended[0])
    shard_two = behind(shard_two, arrived)
    others.append((beside[1], arrived, core_swap(arrived, "kv1_across")))
    weights_two = lax.all_gather(shard_two, ("dp", "ctx"), axis=0, tiled=True)

    settled = (attended[0],)
    if pair:
        output_swapped = core_swap(behind(output_same, others[1][2]), "output_proj")
        settled += (output_swapped,)
    found.append(attend(orders, q, kv[1], others[1], half_seqs, half_seqs, local, after=settled))
    attended, probs = [list(parts) for parts in zip(*found)]
    joined = None
    attended_pair = attended, [core_swap(part, "attended") for part in attended]
    if pair:
        other_heads = [tp_swap(part, f"attended{h}") for h, part in enumerate(attended)]
        for h in range(2):
            joined = output_join(
                spot, input_rows, attended[h], other_heads[h], weights, 2,
                output_same, output_swapped, gain_second, h * half_rows, joined,
            )
    else:
        for h in range(2):
            part = nt_product([(attended[h], weights, 2 * columns)], 0, half_rows)
            started = tp_start(part, f"attended{h}")
            joined = join(input_rows, *started, gain_second, h * half_rows, joined)
    middle, feed_two = joined

    cut = width // 4
    tile = min(512, third)

    class Gradient:
        def __init__(self, name, parts, after=()):
            self.name = name
            to_x, self.keep = grad_product(parts, tile, (cut, cut), after=after)
            self.from_x = x_swap(to_x, name)

    def over_dp(name, grads, after=()):
        summed = add_rows([(grad.keep, grad.from_x) for grad in grads], after=after)
        with jax.named_scope(name + "_over_dp"):
            return summed, lax.psum_scatter(summed, "dp", scatter_dimension=0, tiled=True)

    def with_core(values, name):
        return [([value], [core_swap(value, name)]) for value in values]

    names = ("hidden", "gate_back", "up_back")
    starts = [3 * columns + at * third for at in range(3)]
    settled = (*attended_pair[1], one_turned[1])
    two_turned = turned(feed_two, "normed_two", after=settled)
    acts = feed(feed_two, cot_rows, weights, starts, min(256, third), third, 1, after=(two_turned[0],))
    firsts = [([a[0]], [core_swap(a[0], n + "_one")]) for a, n in zip(acts, names)]
    parts = [(cot_turned, firsts[0]), (two_turned, firsts[1]), (two_turned, firsts[2])]
    first_third = Gradient("first_third", parts)
    starts = [at * 2 * third for at in range(3)]
    acts = feed(
        feed_two, cot_rows, weights_two, starts, min(256, third), 2 * third, 1, after=(first_third.keep,)
    )
    seconds = [([a[0]], [core_swap(a[0], n + "_two")]) for a, n in zip(acts, names)]

    def feed_terms(at, kind):
        place = 3 * columns + kind * third
        return [(firsts[at][0][0], weights, place), (seconds[at][0][0], weights_two, 2 * kind * third)]

    back_terms = feed_terms(1, 0) + feed_terms(2, 1)
    back, out_started = [], []
    part = nt_product(back_terms, 0, half_rows)
    back.append(tp_start(part, "back0"))
    down_two = Gradient("down_two", [(cot_turned, seconds[0])], after=(part,))
    landed = (seconds[1][1][0], seconds[2][1][0])
    part = nt_product(back_terms, half_rows, half_rows, after=(down_two.keep, *landed))
    back.append(tp_start(part, "back1"))
    done, first_out = over_dp("first_third", [first_third], after=(part,))
    gate_two = Gradient("gate_two", [(two_turned, seconds[1])], after=(done,))

    def out_half(h, after):
        part = nt_product(feed_terms(0, 2), h * half_rows, half_rows, after=after)
        out_started.append(tp_start(part, f"out{h}"))
        return part

    grads, q_back, k_back, pieces, one = None, None, None, [], []
    sums = {"second": 0.0, "query": 0.0, "key": 0.0, "first": 0.0}

    def middle_half(h, after):
        *found, second = norm_back(
            middle, cot_rows, *back[h], gain_second, h * half_rows, (F32, BF16), grads, after=after
        )
        sums["second"] = sums["second"] + jnp.sum(second, axis=0)
        return found, nn_product(found[1], weights, 2 * columns, columns, h * half_rows, half_rows)

    def attention_half(h, grad_attended, after):
        found, to_own, to_x, to_core, query = attend_back(
            q, kv[h], others[h], probs[h], grad_attended, raw_q, cosine, sine, gain_query,
            h * half_seqs, half_seqs, local, q_back, after=after,
        )
        sums["query"] = sums["query"] + jnp.sum(query, axis=0)
        return found, to_own, to_x, core_swap(to_core, f"kv_grad{h}")

    def send_keys(h, held, after):
        to_own, to_x, from_core = held
        sent = add_rows([(to_x, from_core)], after=after)
        pieces.append((to_own, from_core, x_swap(sent, f"kv_grad{h}")))
        return sent

    def key_half(h, after):
        found, key = key_back(
            *pieces[h], raw_kv[h], cosine, sine, gain_key, h * half_seqs, half_seqs, local,
            tokens, k_back, after=after,
        )
        sums["key"] = sums["key"] + jnp.sum(key, axis=0)
        return found

    def one_half(h, after):
        terms = [(q_back, weights, 0), (k_back, weights, columns)]
        part = nt_product(terms, h * half_rows, half_rows, after=after)
        one.append(tp_start(part, f"one{h}"))
        return part

    grads, grad_attended = middle_half(0, (gate_two.keep,))
    part = out_half(0, (grad_attended,))
    q_back, *held = attention_half(0, grad_attended, (part,))
    grads, grad_attended = middle_half(1, (held[0],))
    grad_middle, middle_low = grads
    low_turned = turned(middle_low, "grad_middle", after=(grad_attended, gate_two.from_x))
    sent = send_keys(0, held, (low_turned[0],))
    done, more_out = over_dp("down_gate_two", [down_two, gate_two], after=(sent, first_out))
    output_grad = Gradient("output", [(low_turned, attended_pair)], after=(done,))
    part = out_half(1, (output_grad.keep,))
    landed = (part, out_started[0][1])
    up_two = Gradient("up_two", [(two_turned, seconds[2])], after=landed)
    k_back = key_half(0, (up_two.keep,))
    part = one_half(0, (output_grad.from_x,))
    q_back, *held = attention_half(1, grad_attended, (part,))
    q_pair = [q_back], [core_swap(q_back, "query_back")]
    outputs = sum_rows(middle, out_started[0], 0, None, after=(held[0],))
    sent = send_keys(1, held, (outputs,))
    query_grad = Gradient("query", [(one_turned, q_pair)], after=(sent,))
    done, output_out = over_dp("output", [output_grad], after=(query_grad.keep, more_out))
    done, up_out = over_dp("up_two", [up_two], after=(done,))
    outputs = sum_rows(middle, out_started[1], half_rows, outputs, after=(done,))
    terms = gain_terms(input_rows, one[0][0], 0, after=(outputs,))
    k_back = key_half(1, (terms,))
    part = one_half(1, ())
    k_pair = [k_back], [core_swap(k_back, "key_back")]
    key_grad = Gradient("key", [(one_turned, k_pair)], after=(part,))

    def input_half(h, into, after, cost):
        return norm_back(
            input_rows, grad_middle, *one[h], gain_first, h * half_rows, (BF16,), into, after=after, cost=cost
        )[0:1]

    result = input_half(0, None, (key_grad.keep, query_grad.from_x), 7.5)
    done, heads_out = over_dp("query_key", [query_grad, key_grad], after=(result[0],))
    part = gain_terms(input_rows, one[1][0], half_rows, after=(done,))
    sums["first"] = jnp.sum(terms + part, axis=0)

    if not pair:
        sums["first"], sums["second"] = sums["first"] / tp_size, sums["second"] / tp_size
    places = dp_size * 4
    totals = [sums[name].reshape(places, -1) for name in ("first", "second", "query", "key")]
    totals = jnp.concatenate(totals, axis=1)
    totals = jnp.broadcast_to(totals[:, None, :], (places, tp_size, totals.shape[1]))
    totals = totals.reshape(places * tp_size, -1)
    totals = lax.all_to_all(totals, ("dp", "ctx", "tp"), 0, 0, tiled=True)

    result = input_half(1, result, (part,), 300)
    totals = jnp.sum(behind(totals, result[0]), axis=0)
    grad_kv = heads_out[:, columns:].astype(F32)
    down_out, gate_out, up_first = [first_out[:, at * third : (at + 1) * third] for at in range(3)]
    beside = lambda left, right: jnp.concatenate([left, right], axis=1).astype(F32)
    return (
        outputs.reshape(inputs.shape),
        result[0].reshape(inputs.shape),
        totals[0:shard],
        heads_out[:, 0:columns].astype(F32),
        split_heads(grad_kv, 0),
        split_heads(grad_kv, 1),
        totals[2 * shard : 2 * shard + head_shard],
        totals[2 * shard + head_shard :],
        output_out.astype(F32).T,
        totals[shard : 2 * shard],
        beside(gate_out, more_out[:, 2 * third :]),
        beside(up_first, up_out),
        beside(down_out, more_out[:, 0 : 2 * third]).T,
    )


def solution(mesh):
    rows = P(("dp", "ctx"))
    columns = P(("dp", "ctx"), "tp")
    turned = P("tp", ("dp", "ctx"))
    tokens = P("dp", "ctx", None)
    in_specs = (
        (tokens, P("dp", None), rows, columns, columns, columns, rows, rows, turned, rows)
        + (columns, columns, turned, tokens)
    )
    out_specs = (
        (tokens, tokens, rows, columns, columns, columns, rows, rows, turned, rows)
        + (columns, columns, turned)
    )
    return jax.shard_map(shards, mesh=mesh, in_specs=in_specs, out_specs=out_specs, check_vma=False)
```
